128 devices in a mesh: grp: 4 (over z), dev: 32 (over y, x, core).
Axes of the slice: x: 4, y: 4, z: 4, core: 2. Of those that a mesh axis runs over, the one named last changes fastest.
Arguments:
- prior_iterate_velocity: float32 [8192, 2, 4096], P(('grp', 'dev')), may hold values from -3 to 3
- forcing: float32 [8192, 2, 4096], P(('grp', 'dev')), may hold values from -18 to 18
- mass_with_drag: float32 [8192, 4096], P(('grp', 'dev')), may hold values from 0.5 to 3
- coriolis: float32 [8192, 4096], P(('grp', 'dev')), may hold values from -1 to 1
- bulk_viscosity: float32 [8192, 4096], P(('grp', 'dev')), may hold values from 0.05 to 1.5
- line_inverse: float32 [8192, 4096], P(('grp', 'dev')), may hold values from -0.35 to 1.2
- tile_source_slot: int32 [4096], P(('grp', 'dev')), may hold values from 0 to 8191, as said below
- ocean_tile: int32 [8192], P(('grp', 'dev')), may hold values from -1 to 4095, as said below
Outputs:
- new_velocity: float32 [8192, 2, 4096], P(('grp', 'dev'))
The draws below stay inside these ranges and needn't reach their ends.
Inputs may be any that keep to these rules, and one draw needn't show every extreme that they name: Tile t's data sit in slot tile_source_slot[t]; distinct tiles name distinct slots; the slot's ocean device, slot // 64, has the same index along grp as tile t's ice device t // 32; no ocean device holds more than 2 tiles of one ice device, and some pair holds exactly 2. ocean_tile[s] is the tile t with tile_source_slot[t] = s, or -1 where no tile names slot s.
All inputs are finite; a program needn't handle non-finite values.
Results may differ from the reference program's by a relative error of at most 0.0003.
Values sent between devices are 32-bit elements; how exact they have to be, the bound alone decides.
No kernel may reach another device: no remote copies, remote signals or barrier semaphores. Data moves between devices by JAX's collectives and lax.ppermute only.
A program may use at most 128 MiB of HBM per device.

```python
import math
import jax
import jax.numpy as jnp
from jax import lax

TILE_SIDE = 64
TR = 4
TC = 8
SWEEPS = 3
TPD = 32
OSLOT = 64
ICE_TILES = 4096
OCEAN_SLOTS = 8192
NY = 1024
NX = 16384
N_GRP = 4
N_DEV = 32


def tile_plan(key):
    group_keys = jax.random.split(key, N_GRP)

    def one_group(group_key):
        key_weight, key_noise, key_extra, key_perm = jax.random.split(group_key, 4)
        weight = jax.random.randint(key_weight, (N_DEV,), 0, 3)
        noise = jax.random.randint(key_noise, (N_DEV, N_DEV), 0, 1024)
        score = (weight[None, :] * 1024 + noise) * N_DEV + jnp.arange(N_DEV)[None, :]
        ranking = jnp.argsort(-score, axis=1)
        extra = jax.random.randint(key_extra, (N_DEV,), 0, N_DEV // 2)
        extra = extra.at[0].set(0)
        reach = N_DEV // 2 + extra
        pick = jnp.arange(TPD)[None, :] % reach[:, None]
        owner = jnp.take_along_axis(ranking, pick, axis=1).reshape(-1)
        onehot = (owner[:, None] == jnp.arange(N_DEV)[None, :]).astype(jnp.int32)
        rank = jnp.sum((jnp.cumsum(onehot, axis=0) - onehot) * onehot, axis=1)
        perms = jax.vmap(lambda one_key: jax.random.permutation(one_key, OSLOT))(jax.random.split(key_perm, N_DEV))
        return owner * OSLOT + perms[owner, rank]
    local_slots = jax.vmap(one_group)(group_keys)
    source_index = (local_slots + (jnp.arange(N_GRP) * N_DEV * OSLOT)[:, None]).reshape(-1).astype(jnp.int32)
    inverse_matrix = jnp.full((OCEAN_SLOTS,), -1, jnp.int32).at[source_index].set(jnp.arange(ICE_TILES, dtype=jnp.int32))
    return (source_index, inverse_matrix)


def draw_tile_source_slot(key, part):
    source_index, inverse_matrix = tile_plan(key)
    return source_index


def draw_ocean_tile(key, part):
    source_index, inverse_matrix = tile_plan(key)
    return inverse_matrix


def draw_forcing(key, part):
    source_index, inverse_matrix = tile_plan(key)
    key = jax.random.fold_in(key, 7)
    base_key_seed = jax.random.fold_in(key, 0)
    device = jnp.where(inverse_matrix >= 0, inverse_matrix // TPD, 0).astype(jnp.float32)
    amplitude = jnp.where(inverse_matrix >= 0, 1.0 + 2.0 * device / (N_GRP * N_DEV - 1), 1.0)[:, None, None]
    base_value = jax.random.truncated_normal(base_key_seed, -4.0, 4.0, (OCEAN_SLOTS, 2, TILE_SIDE * TILE_SIDE), jnp.float32)
    return base_value * amplitude


def draw_line_inverse(key, part):
    key = jax.random.fold_in(key, 9)
    offdiag_key, diagonal_key = jax.random.split(key, 2)
    cells = jnp.arange(TILE_SIDE * TILE_SIDE)
    row_place = cells // TILE_SIDE
    col_place = cells % TILE_SIDE
    gap = jnp.abs(row_place - col_place).astype(jnp.float32)
    decay = jnp.where(row_place == col_place, 0.0, 0.08 * jnp.power(0.85, gap))
    offdiagonal_part = jax.random.truncated_normal(offdiag_key, -5.0, 5.0, (OCEAN_SLOTS, TILE_SIDE * TILE_SIDE), jnp.float32)
    diagonal_part = jax.random.uniform(diagonal_key, (OCEAN_SLOTS, TILE_SIDE * TILE_SIDE), jnp.float32, 0.8, 1.2)
    return jnp.where((row_place == col_place)[None, :], diagonal_part, offdiagonal_part * decay[None, :])


def levels(own_key, dims, cuts, low, high):
    def one(dim, blocks):
        heights = jax.random.uniform(jax.random.fold_in(jax.random.fold_in(own_key, 6), dim), (blocks,), jnp.float32, low / len(cuts), high / len(cuts))
        return jnp.repeat(jnp.exp(heights), dims[dim] // blocks).reshape((-1,) + (1,) * (len(dims) - dim - 1))

    gain = one(*cuts[0])
    for cut in cuts[1:]:
        gain = gain * one(*cut)
    return gain


def normal_values(rng, shape, width, limit, cuts=(), held_as=jnp.bfloat16):
    gain = levels(rng, shape, cuts, -0.22, 0.18) if cuts else 1.0
    values = jax.random.normal(rng, shape, jnp.float32) * width * gain
    return jnp.minimum(jnp.maximum(values, -limit), limit).astype(held_as)


def setup_inputs(seed: int = 0) -> dict:
    splits = jax.random.split(jax.random.key(seed), 9)
    prior_iterate_velocity = normal_values(splits[0], (OCEAN_SLOTS, 2, TILE_SIDE * TILE_SIDE), 0.5, 3.0, ((0, 128),), jnp.float32)
    forcing = draw_forcing(jax.random.fold_in(splits[8], 71), 0)
    mass_with_drag = jnp.clip(jnp.exp(math.log(3.0) - 1.7917595 * jax.random.uniform(splits[2], (OCEAN_SLOTS, TILE_SIDE * TILE_SIDE), jnp.float32) ** levels(splits[2], (OCEAN_SLOTS, TILE_SIDE * TILE_SIDE), ((0, 128),), -0.2, 0.2)), 0.5, 3.0)
    coriolis = jnp.clip(jax.random.uniform(splits[3], (OCEAN_SLOTS, TILE_SIDE * TILE_SIDE), jnp.float32, -1.0, 1.0) * levels(splits[3], (OCEAN_SLOTS, TILE_SIDE * TILE_SIDE), ((0, 128),), -0.4, 0.0), -1.0, 1.0)
    bulk_viscosity = jnp.clip(jnp.exp(math.log(1.5) - 3.4011974 * jax.random.uniform(splits[4], (OCEAN_SLOTS, TILE_SIDE * TILE_SIDE), jnp.float32) ** levels(splits[4], (OCEAN_SLOTS, TILE_SIDE * TILE_SIDE), ((0, 128),), -0.2, 0.2)), 0.05, 1.5)
    line_inverse = draw_line_inverse(jax.random.fold_in(splits[8], 71), 0)
    tile_source_slot = draw_tile_source_slot(jax.random.fold_in(splits[8], 71), 0)
    ocean_tile = draw_ocean_tile(jax.random.fold_in(splits[8], 71), 0)
    return dict(prior_iterate_velocity=prior_iterate_velocity, forcing=forcing, mass_with_drag=mass_with_drag, coriolis=coriolis, bulk_viscosity=bulk_viscosity, line_inverse=line_inverse, tile_source_slot=tile_source_slot, ocean_tile=ocean_tile)


EPSILON = 1e-06

def face_values(padded):
    centre = padded[1:-1, 1:-1]
    west_face = 0.5 * (centre + padded[1:-1, :-2])
    east_face = 0.5 * (centre + padded[1:-1, 2:])
    south_face = 0.5 * (centre + padded[:-2, 1:-1])
    north_face = 0.5 * (centre + padded[2:, 1:-1])
    return (west_face, east_face, south_face, north_face)

def component_factors():
    along_x = jnp.array([1.25, 0.25], jnp.float32)[:, None, None]
    along_y = jnp.array([0.25, 1.25], jnp.float32)[:, None, None]
    return (along_x, along_y)

def jacobian(padded, damping, turning_rate, face_set, tile_cuts):
    centre = padded[:, 1:-1, 1:-1]
    west_cell = padded[:, 1:-1, :-2]
    east_cell = padded[:, 1:-1, 2:]
    south_cell = padded[:, :-2, 1:-1]
    north_cell = padded[:, 2:, 1:-1]
    if tile_cuts is not None:
        west_cell = west_cell * tile_cuts[0]
        east_cell = east_cell * tile_cuts[1]
        south_cell = south_cell * tile_cuts[2]
        north_cell = north_cell * tile_cuts[3]
    along_x, along_y = component_factors()
    west_face, east_face, south_face, north_face = face_set
    viscous = along_x * (west_face * (centre - west_cell) + east_face * (centre - east_cell))
    viscous = viscous + along_y * (south_face * (centre - south_cell) + north_face * (centre - north_cell))
    turning = jnp.stack([-turning_rate * centre[1], turning_rate * centre[0]])
    return damping * centre + turning + viscous

def diagonal_scale(damping, face_set):
    along_x, along_y = component_factors()
    west_face, east_face, south_face, north_face = face_set
    return lax.rsqrt(damping + along_x * (west_face + east_face) + along_y * (south_face + north_face))

def tile_masks(row_count, col_count):
    row_place = lax.broadcasted_iota(jnp.int32, (row_count, col_count), 0) % TILE_SIDE
    col_place = lax.broadcasted_iota(jnp.int32, (row_count, col_count), 1) % TILE_SIDE
    return ((col_place != 0).astype(jnp.float32), (col_place != TILE_SIDE - 1).astype(jnp.float32), (row_place != 0).astype(jnp.float32), (row_place != TILE_SIDE - 1).astype(jnp.float32))

def precondition(source_index, apply_lines, damping, turning_rate, face_set, tile_cuts):
    iterate = apply_lines(source_index)
    for sweep in range(SWEEPS - 1):
        padded = jnp.pad(iterate, ((0, 0), (1, 1), (1, 1)))
        iterate = iterate + apply_lines(source_index - jacobian(padded, damping, turning_rate, face_set, tile_cuts))
    return iterate

def least_squares(magnitude, upper_first, below_first, upper_cross, upper_second, below_second):
    radius_first = jnp.sqrt(upper_first * upper_first + below_first * below_first)
    cosine_first = upper_first / radius_first
    sine_first = below_first / radius_first
    lifted_top = cosine_first * upper_cross + sine_first * upper_second
    lifted_low = cosine_first * upper_second - sine_first * upper_cross
    radius_second = jnp.sqrt(lifted_low * lifted_low + below_second * below_second)
    weight_second = -(sine_first * magnitude) * (lifted_low / radius_second) / radius_second
    weight_first = (cosine_first * magnitude - lifted_top * weight_second) / radius_first
    return (weight_first, weight_second)

def gather_grid(tile_data):
    channels = tile_data.shape[1]
    blocks = tile_data.reshape(N_GRP, N_DEV, TR, TC, channels, TILE_SIDE, TILE_SIDE)
    return blocks.transpose(4, 0, 2, 5, 1, 3, 6).reshape(channels, N_GRP * TR * TILE_SIDE, N_DEV * TC * TILE_SIDE)

def divided_grid(grid_array):
    channels = grid_array.shape[0]
    blocks = grid_array.reshape(channels, N_GRP, TR, TILE_SIDE, N_DEV, TC, TILE_SIDE)
    return blocks.transpose(1, 4, 2, 5, 0, 3, 6).reshape(N_GRP * N_DEV * TR * TC, channels, TILE_SIDE * TILE_SIDE)

def reference(prior_iterate_velocity, forcing, mass_with_drag, coriolis, bulk_viscosity, line_inverse, tile_source_slot, ocean_tile):
    velocity = gather_grid(prior_iterate_velocity[tile_source_slot])
    forcing_grid = gather_grid(forcing[tile_source_slot])
    damping = gather_grid(mass_with_drag[tile_source_slot][:, None])[0]
    turning_rate = gather_grid(coriolis[tile_source_slot][:, None])[0]
    viscosity = gather_grid(bulk_viscosity[tile_source_slot][:, None])[0]
    line_mats = line_inverse[tile_source_slot].reshape(N_GRP, N_DEV, TR, TC, TILE_SIDE, TILE_SIDE)
    line_mats = line_mats.transpose(0, 2, 1, 3, 4, 5).reshape(N_GRP * TR, N_DEV * TC, TILE_SIDE, TILE_SIDE)
    face_set = face_values(jnp.pad(viscosity, 1))
    scale = diagonal_scale(damping, face_set)
    tile_cuts = tile_masks(NY, NX)

    def apply_lines(source_index):
        scaled = (scale * source_index).reshape(2, N_GRP * TR, TILE_SIDE, N_DEV * TC, TILE_SIDE)
        output = jnp.einsum('caybx,abwx->caybw', scaled, line_mats, precision=lax.Precision.HIGHEST)
        return output.reshape(2, NY, NX) * scale

    def operator(values):
        return jacobian(jnp.pad(values, ((0, 0), (1, 1), (1, 1))), damping, turning_rate, face_set, None)

    def inner_product(left, right):
        return jnp.sum(left * right)
    residual = forcing_grid - operator(velocity)
    magnitude = jnp.sqrt(inner_product(residual, residual) + EPSILON)
    basis_one = residual / magnitude
    step_one = precondition(basis_one, apply_lines, damping, turning_rate, face_set, tile_cuts)
    mapped = operator(step_one)
    upper_first = inner_product(mapped, basis_one)
    mapped = mapped - upper_first * basis_one
    below_first = jnp.sqrt(inner_product(mapped, mapped) + EPSILON)
    basis_two = mapped / below_first
    step_two = precondition(basis_two, apply_lines, damping, turning_rate, face_set, tile_cuts)
    mapped = operator(step_two)
    upper_cross = inner_product(mapped, basis_one)
    upper_second = inner_product(mapped, basis_two)
    mapped = mapped - upper_cross * basis_one - upper_second * basis_two
    below_second = jnp.sqrt(inner_product(mapped, mapped) + EPSILON)
    weight_first, weight_second = least_squares(magnitude, upper_first, below_first, upper_cross, upper_second, below_second)
    updated_velocity = velocity + weight_first * step_one + weight_second * step_two
    tile_values = divided_grid(updated_velocity)
    occupied = (ocean_tile >= 0).astype(jnp.float32)[:, None, None]
    return tile_values[jnp.maximum(ocean_tile, 0).astype(jnp.int32)] * occupied
```

```python
import jax
import jax.numpy as jnp
from jax import lax
from jax.experimental import pallas as pl
from jax.experimental.pallas import tpu as pltpu
from jax.sharding import PartitionSpec as P

F32 = jnp.float32
BF16 = jnp.bfloat16
SLOTS = 64
PAIRS = 32
TILES = 32
EPSILON = 1e-06
VMEM_LIMIT = 56 * 1024 * 1024


def params():
    return pltpu.CompilerParams(vmem_limit_bytes=VMEM_LIMIT)


def vmem():
    return pl.BlockSpec(memory_space=pltpu.VMEM)


def smem():
    return pl.BlockSpec(memory_space=pltpu.SMEM)


def struct(*shape, dtype=F32):
    return jax.ShapeDtypeStruct(shape, dtype)


def iota(shape, dim):
    return lax.broadcasted_iota(jnp.int32, shape, dim)


def roll(x, shift, axis):
    return pltpu.roll(x, shift, axis)


def pair_up(t0, t1):
    low = iota(t0.shape, 1) < 64
    return jnp.concatenate(
        [jnp.where(low, t0, roll(t1, 64, 1)), jnp.where(low, roll(t0, 64, 1), t1)], axis=0
    )


def split_up(q):
    even, odd = q[:32], q[32:]
    low = iota(even.shape, 1) < 64
    return (
        jnp.where(low, even, roll(odd, 64, 1)),
        jnp.where(low, roll(even, 64, 1), odd),
    )


def load_field(ref, table, j, empty):
    tiles = []
    for r in range(2):
        s = table[2 * j + r]
        t = jnp.maximum(s, 0)
        x = ref[t // 8, pl.ds(t % 8, 32, stride=8), :]
        tiles.append(jnp.where(s >= 0, x, empty))
    return pair_up(*tiles)


def load_vector(ref, table, j):
    parts = []
    for c in range(2):
        tiles = []
        for r in range(2):
            s = table[2 * j + r]
            x = ref[jnp.maximum(s, 0), pl.ds(c, 32, stride=2), :]
            tiles.append(jnp.where(s >= 0, x, 0.0))
        parts.append(pair_up(*tiles))
    return parts


def put_columns(acc_ref, x, j):
    mine = ((iota(x.shape, 1) % 64) // 2) == j
    acc_ref[...] = jnp.where(mine, roll(x, 2 * j + 1, 1), acc_ref[...])


def get_columns(acc, j):
    return roll(acc, 128 - (2 * j + 1), 1)


COLUMN_ROWS = (1, 64, 65, 0)


def columns_to_message(acc_ref, turned_ref, message_ref, first, stride):
    turned_ref[...] = acc_ref[...].T
    for row, source in enumerate(COLUMN_ROWS):
        message_ref[pl.ds(first + row, 32, stride=stride), :] = turned_ref[pl.ds(source, 32, stride=2), :]


def message_to_columns(message_ref, turned_ref, acc_ref, first, stride):
    for row, source in enumerate(COLUMN_ROWS):
        turned_ref[pl.ds(source, 32, stride=2), :] = message_ref[pl.ds(first + row, 32, stride=stride), :]
    acc_ref[...] = turned_ref[...].T


def put_rows(message_ref, x, base):
    for row, source in enumerate((0, 63, 64, 127)):
        message_ref[pl.ds(base + 4 + row, 1), :] = x[source : source + 1, :]


def south_of(x, halo=None):
    even, odd = x[:32], x[32:]
    below = roll(odd, 1, 0)
    if halo is not None:
        below = jnp.where(iota(below.shape, 0) == 0, halo, below)
    return jnp.concatenate([below, even], axis=0)


def north_of(x, halo=None):
    even, odd = x[:32], x[32:]
    above = roll(even, 31, 0)
    if halo is not None:
        above = jnp.where(iota(above.shape, 0) == 31, halo, above)
    return jnp.concatenate([odd, above], axis=0)


def tile_part(y, west, south, turn):
    parts = []
    for c in range(2):
        rows = slice(64 * c, 64 * c + 64)
        x, w, s = y[rows], west[rows], south[rows]
        even, odd = x[:32], x[32:]
        s_even, s_odd = s[:32], s[32:]
        across = w * roll(x, 1, 1) + roll(w * x, 127, 1)
        along = jnp.concatenate(
            [
                s_even * roll(odd, 1, 0) + s_odd * odd,
                s_odd * even + roll(s_even * even, 31, 0),
            ],
            axis=0,
        )
        other = y[64:] if c == 0 else y[:64]
        spin = turn * other
        parts.append(x - across - along - spin if c == 0 else x - across - along + spin)
    return jnp.concatenate(parts, axis=0)


def line_solve(t, weight):
    high = t.astype(BF16)
    low = (t - high.astype(F32)).astype(BF16)
    out = lax.dot_general(
        jnp.concatenate([high, low], axis=1),
        weight,
        (((1,), (0,)), ((), ())),
        preferred_element_type=F32,
    )
    return out[:, :128] + out[:, 128:]


def relax(q, weight, west, south, turn):
    y = line_solve(q, weight)
    for _ in range(2):
        y = y + line_solve(q - tile_part(y, west, south, turn), weight)
    return y


def first_edges(table, u_ref, z_ref, message_ref, acc_v, acc_z, turned):
    def body(j, carry):
        u, v = load_vector(u_ref, table, j)
        z = load_field(z_ref, table, j, 0.0)
        vector = jnp.concatenate([u, v], axis=0)
        visc = jnp.concatenate([z, z], axis=0)
        put_columns(acc_v, vector, j)
        put_columns(acc_z, visc, j)
        put_rows(message_ref, vector, 16 * j)
        put_rows(message_ref, visc, 16 * j + 8)
        return carry

    lax.fori_loop(0, PAIRS, body, 0)
    columns_to_message(acc_v, turned, message_ref, 0, 16)
    columns_to_message(acc_z, turned, message_ref, 8, 16)


def line_weights(table, p_ref, weight_ref, natural):
    low = iota((32, 128), 1) < 64

    def body(j, carry):
        tiles = []
        for r in range(2):
            s = table[2 * j + r]
            t = jnp.maximum(s, 0)
            x = p_ref[t // 8, pl.ds(t % 8, 32, stride=8), :]
            tiles.append(jnp.where(s >= 0, x, 0.0))
        t0, t1 = tiles
        natural[pl.ds(0, 32, stride=2), :] = jnp.where(low, t0, 0.0)
        natural[pl.ds(1, 32, stride=2), :] = jnp.where(low, roll(t0, 64, 1), 0.0)
        natural[pl.ds(64, 32, stride=2), :] = jnp.where(low, 0.0, roll(t1, 64, 1))
        natural[pl.ds(65, 32, stride=2), :] = jnp.where(low, 0.0, t1)
        turned = natural[...].T
        high = turned.astype(BF16)
        rest = (turned - high.astype(F32)).astype(BF16)
        both = jnp.concatenate([high, rest], axis=1)
        weight_ref[j, 0:128, :] = both
        weight_ref[j, 128:256, :] = both
        return carry

    lax.fori_loop(0, PAIRS, body, 0)


def side_masks():
    x = iota((64, 128), 1) % 64
    return x == 0, x == 63


KX = (1.25, 0.25)
KY = (0.25, 1.25)


def first_step(
    table, u_ref, b_ref, a_ref, f_ref, z_ref, halo_ref, weight_ref,
    west_ref, south_ref, turn_ref, diag_ref, r_ref, z0_ref, message_ref, rowcoef_ref, colcoef_ref,
    acc, hv, hz, turned,
):
    message_to_columns(halo_ref, turned, hv, 0, 16)
    message_to_columns(halo_ref, turned, hz, 8, 16)
    at_west, at_east = side_masks()

    def body(j, carry):
        u0 = load_vector(u_ref, table, j)
        b = load_vector(b_ref, table, j)
        a = load_field(a_ref, table, j, 1.0)
        f = load_field(f_ref, table, j, 0.0)
        z = load_field(z_ref, table, j, 0.0)
        side_v = get_columns(hv[...], j)
        side_z = get_columns(hz[0:64, :], j)
        rows = halo_ref[pl.ds(pl.multiple_of(16 * j, 16), 16), :]
        face_w = 0.5 * (z + jnp.where(at_west, side_z, roll(z, 1, 1)))
        face_e = 0.5 * (z + jnp.where(at_east, side_z, roll(z, 127, 1)))
        face_s = 0.5 * (z + south_of(z, rows[12:13]))
        face_n = 0.5 * (z + north_of(z, rows[13:14]))
        scale, diag = [], []
        for c in range(2):
            d = a + KX[c] * (face_w + face_e) + KY[c] * (face_s + face_n)
            diag.append(d)
            scale.append(lax.rsqrt(d))
        turn = f * scale[0] * scale[1]
        rhat, west, south, column, south_row, north_row = [], [], [], [], [], []
        for c in range(2):
            x, s = u0[c], scale[c]
            side = side_v[64 * c : 64 * c + 64]
            x_w = jnp.where(at_west, side, roll(x, 1, 1))
            x_e = jnp.where(at_east, side, roll(x, 127, 1))
            x_s = south_of(x, rows[4 + 2 * c : 5 + 2 * c])
            x_n = north_of(x, rows[5 + 2 * c : 6 + 2 * c])
            spin = -f * u0[1] if c == 0 else f * u0[0]
            applied = (
                diag[c] * x + spin
                - KX[c] * (face_w * x_w + face_e * x_e)
                - KY[c] * (face_s * x_s + face_n * x_n)
            )
            rhat.append(s * (b[c] - applied))
            k_w = KX[c] * s * face_w
            k_e = KX[c] * s * face_e
            k_s = KY[c] * s * face_s
            west.append(jnp.where(at_west, 0.0, k_w * roll(s, 1, 1)))
            south.append(k_s * south_of(s, jnp.zeros((1, 128), F32)))
            column.append(jnp.where(at_west, k_w, k_e))
            south_row.append(k_s[0:1])
            north_row.append(KY[c] * s[63:64] * face_n[63:64])
        rhat = jnp.concatenate(rhat, axis=0)
        west = jnp.concatenate(west, axis=0)
        south = jnp.concatenate(south, axis=0)
        put_columns(colcoef_ref, jnp.concatenate(column, axis=0), j)
        for c in range(2):
            rowcoef_ref[pl.ds(8 * j + 4 + 2 * c, 1), :] = south_row[c]
            rowcoef_ref[pl.ds(8 * j + 5 + 2 * c, 1), :] = north_row[c]
        west_ref[j] = west
        south_ref[j] = south
        turn_ref[j] = turn
        diag_ref[j] = jnp.concatenate(diag, axis=0)
        r_ref[j] = rhat
        y = relax(rhat, weight_ref[j], west, south, turn)
        z0 = jnp.concatenate(scale, axis=0) * y
        z0_ref[j] = z0
        put_columns(acc, z0, j)
        put_rows(message_ref, z0, 8 * j)
        return carry

    lax.fori_loop(0, PAIRS, body, 0)
    columns_to_message(acc, turned, message_ref, 0, 8)


def second_step(
    west_ref, south_ref, turn_ref, diag_ref, r_ref, z0_ref, rowcoef_ref, colcoef_ref, halo_ref, weight_ref,
    z1_ref, message_ref, sums_ref,
    acc_z, acc_p, acc_r, acc_d, hv, turned,
):
    message_to_columns(halo_ref, turned, hv, 0, 8)
    hv[...] = hv[...] * colcoef_ref[...]
    lane = iota((128, 128), 1) % 64
    at_side = (lane == 0) | (lane == 63)
    sums_ref[...] = jnp.zeros((6, 8, 128), F32)

    def body(j, carry):
        west, south, turn = west_ref[j], south_ref[j], turn_ref[j]
        diag = diag_ref[j]
        scale = lax.rsqrt(diag)
        root = diag * scale
        rhat = r_ref[j]
        y0 = root * z0_ref[j]
        what = tile_part(y0, west, south, turn)
        what = what - jnp.where(at_side, get_columns(hv[...], j), 0.0)
        base = pl.multiple_of(8 * j, 8)
        rows = halo_ref[pl.ds(base, 8), :] * rowcoef_ref[pl.ds(base, 8), :]
        fixed = []
        first, last = iota((8, 128), 0) == 0, iota((8, 128), 0) == 7
        for c in range(2):
            part = what[64 * c : 64 * c + 64]
            low = part[:8] - jnp.where(first, rows[4 + 2 * c : 5 + 2 * c], 0.0)
            high = part[56:] - jnp.where(last, rows[5 + 2 * c : 6 + 2 * c], 0.0)
            fixed += [low, part[8:56], high]
        what = jnp.concatenate(fixed, axis=0)
        dhat = what - rhat
        y1 = relax(dhat, weight_ref[j], west, south, turn)
        phat = tile_part(y1, west, south, turn) - dhat
        z1 = scale * y1
        z1_ref[j] = z1
        r, d, p = root * rhat, root * dhat, root * phat
        for index, (left, right) in enumerate(((r, r), (r, d), (d, d), (r, p), (d, p), (p, p))):
            product = left * right
            total = product[0:8]
            for k in range(1, 16):
                total = total + product[8 * k : 8 * k + 8]
            sums_ref[index] += total
        for k, (acc, x) in enumerate(((acc_z, z1), (acc_p, p), (acc_r, r), (acc_d, d))):
            put_columns(acc, x, j)
            put_rows(message_ref, x, 32 * j + 8 * k)
        return carry

    lax.fori_loop(0, PAIRS, body, 0)
    for k, acc in enumerate((acc_z, acc_p, acc_r, acc_d)):
        columns_to_message(acc, turned, message_ref, 8 * k, 32)


def to_normal(x, r):
    row = iota((8, 128), 0)
    return jnp.where(r == 1, jnp.where(row < 4, roll(x, 6, 0), roll(x, 64, 1)), x)


def halo_of(west, east, south, north):
    row = iota((8, 128), 0)
    side = jnp.where(row == 0, roll(west, 7, 0), roll(east, 1, 0))
    end = jnp.where(row % 2 == 0, roll(south, 7, 0), roll(north, 1, 0))
    return jnp.where(row < 2, side, jnp.where(row >= 4, end, 0.0))


def collect(count, arrival, received_ref, tiles_ref, west_ref, east_ref, south_ref, north_ref):
    outgoing = west_ref.shape[1] // 8
    for t in range(TILES):
        at = arrival[t]
        for k in range(count):
            x = received_ref[at // 2, 8 * k : 8 * k + 8, :]
            x = to_normal(x, at % 2)
            tiles_ref[t, 8 * k : 8 * k + 8, :] = x
            if k < outgoing:
                rows = slice(8 * k, 8 * k + 8)
                if t % 8 == 0:
                    west_ref[t // 8, rows, :] = x
                if t % 8 == 7:
                    east_ref[t // 8, rows, :] = x
                if t // 8 == 0:
                    south_ref[t % 8, rows, :] = x
                if t // 8 == 3:
                    north_ref[t % 8, rows, :] = x


def tile_halo(t, rows, tiles_ref, from_west, from_east, from_south, from_north):
    ty, tx = t // 8, t % 8
    return halo_of(
        tiles_ref[t - 1, rows, :] if tx > 0 else from_west[ty, rows, :],
        tiles_ref[t + 1, rows, :] if tx < 7 else from_east[ty, rows, :],
        tiles_ref[t - 8, rows, :] if ty > 0 else from_south[tx, rows, :],
        tiles_ref[t + 8, rows, :] if ty < 3 else from_north[tx, rows, :],
    )


def hand_back(arrival, t, k, halo, out_ref):
    at = arrival[t]
    r = at % 2
    row, lane = iota((8, 128), 0), iota((8, 128), 1)
    placed = jnp.where(r == 1, jnp.where(row < 4, roll(halo, 2, 0), roll(halo, 64, 1)), halo)
    mine = ((row < 4) & (row // 2 == r)) | ((row >= 4) & (lane // 64 == r))
    rows = slice(8 * k, 8 * k + 8)
    out_ref[at // 2, rows, :] += jnp.where(mine, placed, 0.0)


def first_return(arrival, tiles_ref, west, east, south, north, out_ref, face_ref):
    row, lane = iota((8, 128), 0), iota((8, 128), 1)
    along_x = jnp.where(lane < 64, KX[0], KX[1])
    along_y = jnp.where(row < 6, KY[0], KY[1])
    factor = 0.5 * jnp.where(row < 4, along_x, along_y)
    out_ref[...] = jnp.zeros(out_ref.shape, F32)
    for t in range(TILES):
        for k in range(2):
            rows = slice(8 * k, 8 * k + 8)
            halo = tile_halo(t, rows, tiles_ref, west, east, south, north)
            hand_back(arrival, t, k, halo, out_ref)
            if k == 1:
                face_ref[t] = factor * (tiles_ref[t, rows, :] + halo)


def second_return(arrival, tiles_ref, west, east, south, north, out_ref):
    out_ref[...] = jnp.zeros(out_ref.shape, F32)
    for t in range(TILES):
        halo = tile_halo(t, slice(0, 8), tiles_ref, west, east, south, north)
        hand_back(arrival, t, 0, halo, out_ref)


def edge_sums(tiles_ref, west, east, south, north, face_ref, sums_ref, out_ref):
    row, lane = iota((8, 128), 0), iota((8, 128), 1)
    valid = (row < 2) | ((row >= 4) & (lane < 64))
    total_r = jnp.zeros((8, 128), F32)
    total_d = jnp.zeros((8, 128), F32)
    total_p = jnp.zeros((8, 128), F32)
    for t in range(TILES):
        halo = tile_halo(t, slice(0, 8), tiles_ref, west, east, south, north)
        h = jnp.where(valid, -face_ref[t] * halo, 0.0)
        p, r, d = tiles_ref[t, 8:16, :], tiles_ref[t, 16:24, :], tiles_ref[t, 24:32, :]
        total_r = total_r + jnp.where(valid, h * r, 0.0)
        total_d = total_d + jnp.where(valid, h * d, 0.0)
        wide_w = jnp.broadcast_to(h[0:1], (8, 128))
        wide_e = jnp.broadcast_to(h[1:2], (8, 128))
        corner_w = jnp.where(
            row == 4, wide_w,
            jnp.where(row == 5, roll(wide_w, 65, 1), jnp.where(row == 6, roll(wide_w, 64, 1), roll(wide_w, 1, 1))),
        )
        corner_e = jnp.where(
            row == 4, roll(wide_e, 63, 1),
            jnp.where(row == 5, wide_e, jnp.where(row == 6, roll(wide_e, 127, 1), roll(wide_e, 64, 1))),
        )
        corner = jnp.where(lane == 0, corner_w, jnp.where(lane == 63, corner_e, 0.0))
        corner = jnp.where(row >= 4, corner, 0.0)
        total_p = total_p + jnp.where(valid, h * (2.0 * (p + corner) + h), 0.0)
    lane = iota((1, 128), 1)
    out = jnp.zeros((1, 128), F32)
    for index in range(6):
        total = sums_ref[index]
        if index == 3:
            total = total + total_r
        if index == 4:
            total = total + total_d
        if index == 5:
            total = total + total_p
        value = jnp.sum(jnp.sum(total, axis=0, keepdims=True), axis=1, keepdims=True)
        out = jnp.where(lane == index, value, out)
    out_ref[...] = jnp.broadcast_to(out, (128, 128))


def least_squares(magnitude, upper_first, below_first, upper_cross, upper_second, below_second):
    radius_first = jnp.sqrt(upper_first * upper_first + below_first * below_first)
    cosine_first = upper_first / radius_first
    sine_first = below_first / radius_first
    lifted_top = cosine_first * upper_cross + sine_first * upper_second
    lifted_low = cosine_first * upper_second - sine_first * upper_cross
    radius_second = jnp.sqrt(lifted_low * lifted_low + below_second * below_second)
    weight_second = -(sine_first * magnitude) * (lifted_low / radius_second) / radius_second
    weight_first = (cosine_first * magnitude - lifted_top * weight_second) / radius_first
    return (weight_first, weight_second)


def final_weights(gathered):
    total = jnp.sum(gathered, axis=0, keepdims=True)
    lane = iota((1, 128), 1)
    rr, rd, dd, re, de, ee = [
        jnp.sum(jnp.where(lane == index, total, 0.0), axis=1, keepdims=True) for index in range(6)
    ]
    square = rr + EPSILON
    magnitude = jnp.sqrt(square)
    h11 = (rr + rd) / square
    gap = -(rd - EPSILON) / square
    h21_square = jnp.maximum((dd + 2.0 * gap * rd + gap * gap * rr) / square, 0.0) + EPSILON
    h21 = jnp.sqrt(h21_square)
    unit = 1.0 / (magnitude * h21)
    h12 = (gap * rr + (1.0 + gap) * rd + re) * unit / magnitude
    h22 = (
        gap * (gap * rr + rd) + (1.0 + gap) * (gap * rd + dd) + (gap * re + de)
    ) * unit * unit
    c_r = gap * unit - h12 / magnitude - h22 * gap * unit
    c_d = (1.0 + gap - h22) * unit
    c_e = unit
    h32_square = (
        c_r * c_r * rr + c_d * c_d * dd + c_e * c_e * ee
        + 2.0 * (c_r * c_d * rd + c_r * c_e * re + c_d * c_e * de)
    )
    h32 = jnp.sqrt(jnp.maximum(h32_square, 0.0) + EPSILON)
    y1, y2 = least_squares(magnitude, h11, h21, h12, h22, h32)
    return y1 / magnitude + y2 * gap * unit, y2 * unit


def last_step(table, gathered_ref, u_ref, z0_ref, z1_ref, out_ref):
    weight0, weight1 = final_weights(gathered_ref[...])
    out_ref[...] = jnp.zeros(out_ref.shape, F32)

    def body(j, carry):
        change = weight0 * z0_ref[j] + weight1 * z1_ref[j]
        for c in range(2):
            for r, x in enumerate(split_up(change[64 * c : 64 * c + 64])):
                s = table[2 * j + r]

                @pl.when(s >= 0)
                def _():
                    rows = pl.ds(c, 32, stride=2)
                    out_ref[s, rows, :] = u_ref[s, rows, :] + x

        return carry

    lax.fori_loop(0, PAIRS, body, 0)


def call(kernel, outs, specs, scratch=()):
    return pl.pallas_call(
        kernel,
        out_shape=outs,
        in_specs=specs,
        out_specs=jax.tree.map(lambda _: vmem(), outs),
        scratch_shapes=list(scratch),
        compiler_params=params(),
    )


def square(rows=128):
    return pltpu.VMEM((rows, 128), F32)


def vector_view(x):
    return x.reshape(64, 2, 32, 128).transpose(0, 2, 1, 3).reshape(64, 64, 128)


def field_view(x):
    return x.reshape(8, 8, 32, 128).transpose(0, 2, 1, 3).reshape(8, 256, 128)


def exchange(x):
    return lax.all_to_all(x, "dev", split_axis=0, concat_axis=0, tiled=True)


def shifted(west, east, south, north):
    dev, grp = lax.axis_size("dev"), lax.axis_size("grp")
    up_dev = [(i, i + 1) for i in range(dev - 1)]
    up_grp = [(i, i + 1) for i in range(grp - 1)]
    return (
        lax.ppermute(east, "dev", up_dev),
        lax.ppermute(west, "dev", [(j, i) for i, j in up_dev]),
        lax.ppermute(north, "grp", up_grp),
        lax.ppermute(south, "grp", [(j, i) for i, j in up_grp]),
    )


def collected(received, arrival, count, outgoing):
    outs = (
        struct(TILES, 8 * count, 128),
        struct(4, 8 * outgoing, 128),
        struct(4, 8 * outgoing, 128),
        struct(8, 8 * outgoing, 128),
        struct(8, 8 * outgoing, 128),
    )

    def kernel(*refs):
        collect(count, *refs)

    tiles, west, east, south, north = call(kernel, outs, [smem(), vmem()])(arrival, received)
    return (tiles,) + shifted(west, east, south, north)


def shards(velocity, forcing, mass, coriolis, viscosity, lines, tile_source_slot, ocean_tile):
    slots = jnp.arange(SLOTS)
    occupied = ocean_tile >= 0
    target = ocean_tile // TILES % PAIRS
    earlier = (
        (target[None, :] == target[:, None])
        & (ocean_tile[None, :] < ocean_tile[:, None])
        & occupied[None, :]
    )
    position = jnp.where(
        occupied, target * 2 + jnp.sum(earlier.astype(jnp.int32), axis=1), -1
    )
    table = jnp.max(jnp.where(position[None, :] == slots[:, None], slots[None, :], -1), axis=1)
    owner = tile_source_slot // SLOTS % PAIRS
    order = jnp.arange(TILES)
    sooner = (owner[None, :] == owner[:, None]) & (order[None, :] < order[:, None])
    arrival = owner * 2 + jnp.sum(sooner.astype(jnp.int32), axis=1)

    u, b = vector_view(velocity), vector_view(forcing)
    a, f, z, p = [field_view(x) for x in (mass, coriolis, viscosity, lines)]

    message = call(
        first_edges, struct(PAIRS * 16, 128), [smem(), vmem(), vmem()], [square(), square(), square()]
    )(table, u, z)
    weight = call(
        line_weights, struct(PAIRS, 256, 256, dtype=BF16), [smem(), vmem()], [square()]
    )(table, p)
    landed = collected(exchange(message.reshape(PAIRS, 16, 128)), arrival, 2, 2)
    halo, face = call(
        first_return, (struct(PAIRS, 16, 128), struct(TILES, 8, 128)), [smem()] + [vmem()] * 5
    )(arrival, *landed)
    halo = exchange(halo).reshape(PAIRS * 16, 128)

    whole = struct(PAIRS, 128, 128)
    west, south, turn, diag, r, z0, message, rowcoef, colcoef = call(
        first_step,
        (
            whole, whole, struct(PAIRS, 64, 128), whole, whole, whole,
            struct(PAIRS * 8, 128), struct(PAIRS * 8, 128), struct(128, 128),
        ),
        [smem()] + [vmem()] * 7,
        [square(), square(), square(), square()],
    )(table, u, b, a, f, z, halo, weight)
    landed = collected(exchange(message.reshape(PAIRS, 8, 128)), arrival, 1, 1)
    halo = call(second_return, struct(PAIRS, 8, 128), [smem()] + [vmem()] * 5)(arrival, *landed)
    halo = exchange(halo).reshape(PAIRS * 8, 128)

    z1, message, sums = call(
        second_step,
        (whole, struct(PAIRS * 32, 128), struct(6, 8, 128)),
        [vmem()] * 10,
        [square() for _ in range(6)],
    )(west, south, turn, diag, r, z0, rowcoef, colcoef, halo, weight)
    landed = collected(exchange(message.reshape(PAIRS, 32, 128)), arrival, 4, 1)
    partial = call(edge_sums, struct(128, 128), [vmem()] * 7)(*landed, face, sums)
    gathered = lax.all_to_all(partial, ("grp", "dev"), split_axis=0, concat_axis=0, tiled=True)

    out = call(last_step, struct(SLOTS, 64, 128), [smem()] + [vmem()] * 4)(table, gathered, u, z0, z1)
    return out.reshape(64, 32, 2, 128).transpose(0, 2, 1, 3).reshape(64, 2, 4096)


def solution(mesh):
    return jax.shard_map(
        shards,
        mesh=mesh,
        in_specs=(
            P(("grp", "dev"), None, None),
            P(("grp", "dev"), None, None),
            P(("grp", "dev"), None),
            P(("grp", "dev"), None),
            P(("grp", "dev"), None),
            P(("grp", "dev"), None),
            P(("grp", "dev")),
            P(("grp", "dev")),
        ),
        out_specs=P(("grp", "dev"), None, None),
        check_vma=False,
    )
```

```python
import jax
import jax.numpy as jnp
from jax import lax
from jax.experimental import pallas as pl
from jax.experimental.pallas import tpu as pltpu
from jax.sharding import PartitionSpec as P

F32 = jnp.float32
BF16 = jnp.bfloat16
SLOTS = 64
PAIRS = 32
TILES = 32
CHUNK = 4
CHUNKS = PAIRS // CHUNK
TABLE = 72
CODES = 144
STATE = 704
EPSILON = 1e-06
VMEM_LIMIT = 56 * 1024 * 1024


def params():
    return pltpu.CompilerParams(vmem_limit_bytes=VMEM_LIMIT)


def vmem():
    return pl.BlockSpec(memory_space=pltpu.VMEM)


def smem():
    return pl.BlockSpec(memory_space=pltpu.SMEM)


def struct(*shape, dtype=F32):
    return jax.ShapeDtypeStruct(shape, dtype)


def iota(shape, dim):
    return lax.broadcasted_iota(jnp.int32, shape, dim)


def roll(x, shift, axis):
    return pltpu.roll(x, shift, axis)


def pair_up(t0, t1):
    low = iota(t0.shape, 1) < 64
    return jnp.concatenate(
        [jnp.where(low, t0, roll(t1, 64, 1)), jnp.where(low, roll(t0, 64, 1), t1)], axis=0
    )


def split_up(q):
    even, odd = q[:32], q[32:]
    low = iota(even.shape, 1) < 64
    return (
        jnp.where(low, even, roll(odd, 64, 1)),
        jnp.where(low, roll(even, 64, 1), odd),
    )


def load_field(ref, table, j, empty):
    tiles = []
    for r in range(2):
        s = table[2 * j + r]
        t = jnp.maximum(s, 0)
        x = ref[t // 8, pl.ds(t % 8, 32, stride=8), :]
        tiles.append(jnp.where(s >= 0, x, empty))
    return pair_up(*tiles)


def load_vector(ref, table, j):
    parts = []
    for c in range(2):
        tiles = []
        for r in range(2):
            s = table[2 * j + r]
            x = ref[jnp.maximum(s, 0), pl.ds(c, 32, stride=2), :]
            tiles.append(jnp.where(s >= 0, x, 0.0))
        parts.append(pair_up(*tiles))
    return parts


def put_columns(acc_ref, x, j):
    mine = ((iota(x.shape, 1) % 64) // 2) == j
    acc_ref[...] = jnp.where(mine, roll(x, 2 * j + 1, 1), acc_ref[...])


def get_columns(acc, j):
    return roll(acc, 128 - (2 * j + 1), 1)


COLUMN_ROWS = (1, 64, 65, 0)


def columns_to_message(acc_ref, turned_ref, message_ref, first, stride):
    turned_ref[...] = acc_ref[...].T
    for row, source in enumerate(COLUMN_ROWS):
        message_ref[pl.ds(first + row, 32, stride=stride), :] = turned_ref[pl.ds(source, 32, stride=2), :]


def message_to_columns(message_ref, turned_ref, acc_ref, first, stride):
    for row, source in enumerate(COLUMN_ROWS):
        turned_ref[pl.ds(source, 32, stride=2), :] = message_ref[pl.ds(first + row, 32, stride=stride), :]
    acc_ref[...] = turned_ref[...].T


def put_rows(message_ref, x, base):
    for row, source in enumerate((0, 63, 64, 127)):
        message_ref[pl.ds(base + 4 + row, 1), :] = x[source : source + 1, :]


def south_of(x, halo=None):
    even, odd = x[:32], x[32:]
    below = roll(odd, 1, 0)
    if halo is not None:
        below = jnp.where(iota(below.shape, 0) == 0, halo, below)
    return jnp.concatenate([below, even], axis=0)


def north_of(x, halo=None):
    even, odd = x[:32], x[32:]
    above = roll(even, 31, 0)
    if halo is not None:
        above = jnp.where(iota(above.shape, 0) == 31, halo, above)
    return jnp.concatenate([odd, above], axis=0)


def tile_part(y, west, south, turn):
    parts = []
    for c in range(2):
        rows = slice(64 * c, 64 * c + 64)
        x, w, s = y[rows], west[rows], south[rows]
        even, odd = x[:32], x[32:]
        s_even, s_odd = s[:32], s[32:]
        across = w * roll(x, 1, 1) + roll(w * x, 127, 1)
        along = jnp.concatenate(
            [
                s_even * roll(odd, 1, 0) + s_odd * odd,
                s_odd * even + roll(s_even * even, 31, 0),
            ],
            axis=0,
        )
        other = y[64:] if c == 0 else y[:64]
        spin = turn * other
        parts.append(x - across - along - spin if c == 0 else x - across - along + spin)
    return jnp.concatenate(parts, axis=0)


def line_solve(t, weight):
    high = t.astype(BF16)
    low = (t - high.astype(F32)).astype(BF16)
    out = lax.dot_general(
        jnp.concatenate([high, low], axis=1),
        weight,
        (((1,), (0,)), ((), ())),
        preferred_element_type=F32,
    )
    return out[:, :128] + out[:, 128:]


def relax(q, weight, west, south, turn):
    y = line_solve(q, weight)
    for _ in range(2):
        y = y + line_solve(q - tile_part(y, west, south, turn), weight)
    return y


NONE = 99
CODE_W = 72


def make_tables(ocean, table, codes):
    def clear(i, carry):
        table[i] = -1
        return carry

    def clear_codes(i, carry):
        codes[i] = NONE
        return carry

    def place(s, carry):
        t = ocean[s]
        j = jnp.where(t >= 0, (t >> 5) & 31, 32)
        held = table[2 * j]
        before = ocean[jnp.maximum(held, 0)]
        keep = (held >= 0) & (before < t)
        table[2 * j] = jnp.where(keep, held, s)
        table[2 * j + 1] = jnp.where(keep, s, held)
        return carry

    def code(p, carry):
        s = table[p]
        t = ocean[jnp.maximum(s, 0)]
        column, row = t & 7, (t >> 3) & 3
        codes[p + 2] = jnp.where((s >= 0) & (column == 7), row, NONE)
        codes[CODE_W + p] = jnp.where((s >= 0) & (column == 0), row + 4, NONE)
        return carry

    lax.fori_loop(0, TABLE, clear, 0, unroll=8)
    lax.fori_loop(0, CODES, clear_codes, 0, unroll=8)
    lax.fori_loop(0, SLOTS, place, 0, unroll=4)
    lax.fori_loop(0, 2 * PAIRS, code, 0, unroll=8)


def put_extras(codes, turned, message_ref, first, stride):
    row = iota((8, 128), 0)

    def body(m, carry):
        before, after = 2 * jnp.maximum(m - 1, 0), 2 * jnp.minimum(m + 1, PAIRS - 1)
        total = jnp.zeros((8, 128), F32)
        for r in range(2):
            east = turned[pl.ds(before + (64, 0)[r], 1), :]
            west = turned[pl.ds(after + (1, 65)[r], 1), :]
            total = jnp.where(row == codes[2 * m + r], east, total)
            total = jnp.where(row == codes[CODE_W + 2 * m + 2 + r], west, total)
        message_ref[pl.ds(pl.multiple_of(m * stride + first, 8), 8), :] = total
        return carry

    lax.fori_loop(0, PAIRS, body, 0, unroll=8)


def chunk(ref, i):
    return ref.at[pl.ds(i * CHUNK, CHUNK)]


def first_edges(
    ocean, u_hbm, z_hbm,
    message_ref, table, codes, pairs_hbm,
    u_ref, z_ref, pairs, acc_v, acc_z, turned, sem_in, sem_out,
):
    copies = [
        pltpu.make_async_copy(u_hbm, u_ref, sem_in.at[0]),
        pltpu.make_async_copy(z_hbm, z_ref, sem_in.at[1]),
    ]
    for copy in copies:
        copy.start()
    make_tables(ocean, table, codes)
    for copy in copies:
        copy.wait()

    def body(i, carry):
        for k in range(CHUNK):
            j = i * CHUNK + k
            u, v = load_vector(u_ref, table, j)
            z = load_field(z_ref, table, j, 0.0)
            vector = jnp.concatenate([u, v], axis=0)
            visc = jnp.concatenate([z, z], axis=0)
            pairs[j, 0:128, :] = vector
            pairs[j, 128:192, :] = z
            put_columns(acc_v, vector, j)
            put_columns(acc_z, visc, j)
            put_rows(message_ref, vector, 32 * j)
            put_rows(message_ref, visc, 32 * j + 8)
        pltpu.make_async_copy(chunk(pairs, i), chunk(pairs_hbm, i), sem_out.at[i]).start()
        return carry

    lax.fori_loop(0, CHUNKS, body, 0)
    columns_to_message(acc_v, turned, message_ref, 0, 32)
    put_extras(codes, turned, message_ref, 16, 32)
    columns_to_message(acc_z, turned, message_ref, 8, 32)
    put_extras(codes, turned, message_ref, 24, 32)
    for i in range(CHUNKS):
        pltpu.make_async_copy(chunk(pairs, i), chunk(pairs_hbm, i), sem_out.at[i]).wait()


def pair_fields(table, b_ref, a_ref, f_ref, out_hbm, pairs, sem):
    def body(i, carry):
        for k in range(CHUNK):
            j = i * CHUNK + k
            bu, bv = load_vector(b_ref, table, j)
            pairs[j, 0:64, :] = bu
            pairs[j, 64:128, :] = bv
            pairs[j, 128:192, :] = load_field(a_ref, table, j, 1.0)
            pairs[j, 192:256, :] = load_field(f_ref, table, j, 0.0)
        pltpu.make_async_copy(chunk(pairs, i), chunk(out_hbm, i), sem.at[i]).start()
        return carry

    lax.fori_loop(0, CHUNKS, body, 0)
    for i in range(CHUNKS):
        pltpu.make_async_copy(chunk(pairs, i), chunk(out_hbm, i), sem.at[i]).wait()


def line_weights(table, p_ref, out_hbm, weight, natural, sem):
    low = iota((32, 128), 1) < 64

    def body(i, carry):
        for k in range(CHUNK):
            j = i * CHUNK + k
            tiles = []
            for r in range(2):
                s = table[2 * j + r]
                t = jnp.maximum(s, 0)
                x = p_ref[t // 8, pl.ds(t % 8, 32, stride=8), :]
                tiles.append(jnp.where(s >= 0, x, 0.0))
            t0, t1 = tiles
            natural[k, pl.ds(0, 32, stride=2), :] = jnp.where(low, t0, 0.0)
            natural[k, pl.ds(1, 32, stride=2), :] = jnp.where(low, roll(t0, 64, 1), 0.0)
            natural[k, pl.ds(64, 32, stride=2), :] = jnp.where(low, 0.0, roll(t1, 64, 1))
            natural[k, pl.ds(65, 32, stride=2), :] = jnp.where(low, 0.0, t1)
            turned = natural[k].T
            high = turned.astype(BF16)
            rest = (turned - high.astype(F32)).astype(BF16)
            both = jnp.concatenate([high, rest], axis=1)
            weight[j, 0:128, :] = both
            weight[j, 128:256, :] = both
        pltpu.make_async_copy(chunk(weight, i), chunk(out_hbm, i), sem.at[i]).start()
        return carry

    lax.fori_loop(0, CHUNKS, body, 0)
    for i in range(CHUNKS):
        pltpu.make_async_copy(chunk(weight, i), chunk(out_hbm, i), sem.at[i]).wait()


def side_masks():
    x = iota((64, 128), 1) % 64
    return x == 0, x == 63


KX = (1.25, 0.25)
KY = (0.25, 1.25)


def first_step(
    codes, halo_ref, pairs_hbm, fields_hbm, weight_hbm,
    state_hbm, message_ref, rowcoef_ref, colcoef_ref,
    pairs, fields, weight, state, acc_z, acc_r, hv, hz, turned, sem_in, sem_out,
):
    def incoming(i):
        return [
            pltpu.make_async_copy(chunk(source, i), chunk(target, i), sem_in.at[n, i])
            for n, (source, target) in enumerate(((pairs_hbm, pairs), (fields_hbm, fields), (weight_hbm, weight)))
        ]

    for i in range(CHUNKS):
        for copy in incoming(i):
            copy.start()
    message_to_columns(halo_ref, turned, hv, 0, 16)
    message_to_columns(halo_ref, turned, hz, 8, 16)
    at_west, at_east = side_masks()

    def one(j):
        u0 = pairs[j, 0:64, :], pairs[j, 64:128, :]
        z = pairs[j, 128:192, :]
        b = fields[j, 0:64, :], fields[j, 64:128, :]
        a, f = fields[j, 128:192, :], fields[j, 192:256, :]
        side_v = get_columns(hv[...], j)
        side_z = get_columns(hz[0:64, :], j)
        rows = halo_ref[pl.ds(pl.multiple_of(16 * j, 16), 16), :]
        face_w = 0.5 * (z + jnp.where(at_west, side_z, roll(z, 1, 1)))
        face_e = 0.5 * (z + jnp.where(at_east, side_z, roll(z, 127, 1)))
        face_s = 0.5 * (z + south_of(z, rows[12:13]))
        face_n = 0.5 * (z + north_of(z, rows[13:14]))
        scale, diag = [], []
        for c in range(2):
            d = a + KX[c] * (face_w + face_e) + KY[c] * (face_s + face_n)
            diag.append(d)
            scale.append(lax.rsqrt(d))
        turn = f * scale[0] * scale[1]
        rhat, west, south, column, plain = [], [], [], [], []
        for c in range(2):
            x, s = u0[c], scale[c]
            side = side_v[64 * c : 64 * c + 64]
            x_w = jnp.where(at_west, side, roll(x, 1, 1))
            x_e = jnp.where(at_east, side, roll(x, 127, 1))
            x_s = south_of(x, rows[4 + 2 * c : 5 + 2 * c])
            x_n = north_of(x, rows[5 + 2 * c : 6 + 2 * c])
            spin = -f * u0[1] if c == 0 else f * u0[0]
            applied = (
                diag[c] * x + spin
                - KX[c] * (face_w * x_w + face_e * x_e)
                - KY[c] * (face_s * x_s + face_n * x_n)
            )
            residual = b[c] - applied
            plain.append(residual)
            rhat.append(s * residual)
            k_w = KX[c] * s * face_w
            k_e = KX[c] * s * face_e
            k_s = KY[c] * s * face_s
            west.append(jnp.where(at_west, 0.0, k_w * roll(s, 1, 1)))
            south.append(k_s * south_of(s, jnp.zeros((1, 128), F32)))
            column.append(jnp.where(at_west, k_w, k_e))
            rowcoef_ref[pl.ds(8 * j + 4 + 2 * c, 1), :] = k_s[0:1]
            rowcoef_ref[pl.ds(8 * j + 5 + 2 * c, 1), :] = KY[c] * s[63:64] * face_n[63:64]
        rhat = jnp.concatenate(rhat, axis=0)
        plain = jnp.concatenate(plain, axis=0)
        west = jnp.concatenate(west, axis=0)
        south = jnp.concatenate(south, axis=0)
        put_columns(colcoef_ref, jnp.concatenate(column, axis=0), j)
        put_columns(acc_r, plain, j)
        put_rows(message_ref, plain, 24 * j + 8)
        state[j, 0:128, :] = west
        state[j, 128:256, :] = south
        state[j, 256:384, :] = jnp.concatenate(diag, axis=0)
        state[j, 384:512, :] = rhat
        state[j, 512:576, :] = turn
        y = relax(rhat, weight[j], west, south, turn)
        z0 = jnp.concatenate(scale, axis=0) * y
        state[j, 576:704, :] = z0
        put_columns(acc_z, z0, j)
        put_rows(message_ref, z0, 24 * j)

    def body(i, carry):
        for copy in incoming(i):
            copy.wait()
        for k in range(CHUNK):
            one(i * CHUNK + k)
        pltpu.make_async_copy(chunk(state, i), chunk(state_hbm, i), sem_out.at[i]).start()
        return carry

    lax.fori_loop(0, CHUNKS, body, 0)
    columns_to_message(acc_r, turned, message_ref, 8, 24)
    columns_to_message(acc_z, turned, message_ref, 0, 24)
    put_extras(codes, turned, message_ref, 16, 24)
    for i in range(CHUNKS):
        pltpu.make_async_copy(chunk(state, i), chunk(state_hbm, i), sem_out.at[i]).wait()


def second_step(
    codes, halo_ref, rowcoef_ref, colcoef_ref, state_hbm, weight_hbm,
    z1_hbm, message_ref, sums_ref,
    state, weight, z1s, acc_z, acc_p, acc_d, hv, turned, sem_in, sem_out,
):
    def incoming(i):
        return [
            pltpu.make_async_copy(chunk(source, i), chunk(target, i), sem_in.at[n, i])
            for n, (source, target) in enumerate(((state_hbm, state), (weight_hbm, weight)))
        ]

    for i in range(CHUNKS):
        for copy in incoming(i):
            copy.start()
    message_to_columns(halo_ref, turned, hv, 0, 8)
    hv[...] = hv[...] * colcoef_ref[...]
    lane = iota((128, 128), 1) % 64
    at_side = (lane == 0) | (lane == 63)
    first, last = iota((8, 128), 0) == 0, iota((8, 128), 0) == 7
    sums_ref[...] = jnp.zeros((6, 8, 128), F32)

    def one(j):
        west, south, turn = state[j, 0:128, :], state[j, 128:256, :], state[j, 512:576, :]
        diag = state[j, 256:384, :]
        rhat = state[j, 384:512, :]
        scale = lax.rsqrt(diag)
        root = diag * scale
        y0 = root * state[j, 576:704, :]
        what = tile_part(y0, west, south, turn)
        what = what - jnp.where(at_side, get_columns(hv[...], j), 0.0)
        base = pl.multiple_of(8 * j, 8)
        rows = halo_ref[pl.ds(base, 8), :] * rowcoef_ref[pl.ds(base, 8), :]
        fixed = []
        for c in range(2):
            part = what[64 * c : 64 * c + 64]
            low = part[:8] - jnp.where(first, rows[4 + 2 * c : 5 + 2 * c], 0.0)
            high = part[56:] - jnp.where(last, rows[5 + 2 * c : 6 + 2 * c], 0.0)
            fixed += [low, part[8:56], high]
        what = jnp.concatenate(fixed, axis=0)
        dhat = what - rhat
        y1 = relax(dhat, weight[j], west, south, turn)
        phat = tile_part(y1, west, south, turn) - dhat
        z1 = scale * y1
        z1s[j] = z1
        r, d, p = root * rhat, root * dhat, root * phat
        for index, (left, right) in enumerate(((r, r), (r, d), (d, d), (r, p), (d, p), (p, p))):
            product = left * right
            total = product[0:8]
            for k in range(1, 16):
                total = total + product[8 * k : 8 * k + 8]
            sums_ref[index] += total
        for k, (acc, x) in enumerate(((acc_z, z1), (acc_p, p), (acc_d, d))):
            put_columns(acc, x, j)
            put_rows(message_ref, x, 32 * j + 8 * k)

    def body(i, carry):
        for copy in incoming(i):
            copy.wait()
        for k in range(CHUNK):
            one(i * CHUNK + k)
        pltpu.make_async_copy(chunk(z1s, i), chunk(z1_hbm, i), sem_out.at[i]).start()
        return carry

    lax.fori_loop(0, CHUNKS, body, 0)
    columns_to_message(acc_p, turned, message_ref, 8, 32)
    columns_to_message(acc_d, turned, message_ref, 16, 32)
    columns_to_message(acc_z, turned, message_ref, 0, 32)
    put_extras(codes, turned, message_ref, 24, 32)
    for i in range(CHUNKS):
        pltpu.make_async_copy(chunk(z1s, i), chunk(z1_hbm, i), sem_out.at[i]).wait()


def to_normal(x, r):
    row = iota((8, 128), 0)
    return jnp.where(r == 1, jnp.where(row < 4, roll(x, 6, 0), roll(x, 64, 1)), x)


def halo_of(west, east, south, north):
    row = iota((8, 128), 0)
    side = jnp.where(row == 0, roll(west, 7, 0), roll(east, 1, 0))
    end = jnp.where(row % 2 == 0, roll(south, 7, 0), roll(north, 1, 0))
    return jnp.where(row < 2, side, jnp.where(row >= 4, end, 0.0))


def tile_block(arrival, received_ref, t, k):
    at = arrival[t]
    return to_normal(received_ref[at // 2, 8 * k : 8 * k + 8, :], at % 2)


def boundary(arrival, received_ref, south_ref, north_ref):
    for k in range(south_ref.shape[1] // 8):
        rows = slice(8 * k, 8 * k + 8)
        for x in range(8):
            south_ref[x, rows, :] = tile_block(arrival, received_ref, x, k)
            north_ref[x, rows, :] = tile_block(arrival, received_ref, 24 + x, k)


def tile_halos(arrival, received_ref, from_south, from_north, k, extra):
    group = lax.axis_index("grp")
    blocks = [tile_block(arrival, received_ref, t, k) for t in range(TILES)]
    sides = received_ref[0, 8 * extra : 8 * extra + 8, :]
    for o in range(1, PAIRS):
        sides = sides + received_ref[o, 8 * extra : 8 * extra + 8, :]
    rows = slice(8 * k, 8 * k + 8)
    last = lax.axis_size("grp") - 1
    below = [jnp.where(group > 0, from_south[x, rows, :], 0.0) for x in range(8)]
    above = [jnp.where(group < last, from_north[x, rows, :], 0.0) for x in range(8)]
    halos = []
    for t in range(TILES):
        ty, tx = t // 8, t % 8
        halos.append(
            halo_of(
                blocks[t - 1] if tx > 0 else roll(sides, (1 - ty) % 8, 0),
                blocks[t + 1] if tx < 7 else roll(sides, 4 - ty, 0),
                blocks[t - 8] if ty > 0 else below[tx],
                blocks[t + 8] if ty < 3 else above[tx],
            )
        )
    return blocks, halos


def hand_back(arrival, t, k, halo, out_ref):
    at = arrival[t]
    r = at % 2
    row, lane = iota((8, 128), 0), iota((8, 128), 1)
    placed = jnp.where(r == 1, jnp.where(row < 4, roll(halo, 2, 0), roll(halo, 64, 1)), halo)
    mine = ((row < 4) & (row // 2 == r)) | ((row >= 4) & (lane // 64 == r))
    rows = slice(8 * k, 8 * k + 8)
    out_ref[at // 2, rows, :] += jnp.where(mine, placed, 0.0)


def first_return(arrival, received_ref, south, north, out_ref, face_ref):
    row, lane = iota((8, 128), 0), iota((8, 128), 1)
    along_x = jnp.where(lane < 64, KX[0], KX[1])
    along_y = jnp.where(row < 6, KY[0], KY[1])
    factor = 0.5 * jnp.where(row < 4, along_x, along_y)
    out_ref[...] = jnp.zeros(out_ref.shape, F32)
    for k in range(2):
        blocks, halos = tile_halos(arrival, received_ref, south, north, k, 2 + k)
        for t in range(TILES):
            hand_back(arrival, t, k, halos[t], out_ref)
            if k == 1:
                face_ref[t] = factor * (blocks[t] + halos[t])


def second_return(arrival, received_ref, south, north, out_ref):
    out_ref[...] = jnp.zeros(out_ref.shape, F32)
    blocks, halos = tile_halos(arrival, received_ref, south, north, 0, 2)
    for t in range(TILES):
        hand_back(arrival, t, 0, halos[t], out_ref)


def edge_sums(arrival, received_ref, south, north, earlier_ref, face_ref, sums_ref, out_ref):
    row, lane = iota((8, 128), 0), iota((8, 128), 1)
    valid = (row < 2) | ((row >= 4) & (lane < 64))
    total_r = jnp.zeros((8, 128), F32)
    total_d = jnp.zeros((8, 128), F32)
    total_p = jnp.zeros((8, 128), F32)
    blocks, halos = tile_halos(arrival, received_ref, south, north, 0, 3)
    for t in range(TILES):
        h = jnp.where(valid, -face_ref[t] * halos[t], 0.0)
        p = tile_block(arrival, received_ref, t, 1)
        d = tile_block(arrival, received_ref, t, 2)
        r = tile_block(arrival, earlier_ref, t, 1)
        total_r = total_r + jnp.where(valid, h * r, 0.0)
        total_d = total_d + jnp.where(valid, h * d, 0.0)
        wide_w = jnp.broadcast_to(h[0:1], (8, 128))
        wide_e = jnp.broadcast_to(h[1:2], (8, 128))
        corner_w = jnp.where(
            row == 4, wide_w,
            jnp.where(row == 5, roll(wide_w, 65, 1), jnp.where(row == 6, roll(wide_w, 64, 1), roll(wide_w, 1, 1))),
        )
        corner_e = jnp.where(
            row == 4, roll(wide_e, 63, 1),
            jnp.where(row == 5, wide_e, jnp.where(row == 6, roll(wide_e, 127, 1), roll(wide_e, 64, 1))),
        )
        corner = jnp.where(lane == 0, corner_w, jnp.where(lane == 63, corner_e, 0.0))
        corner = jnp.where(row >= 4, corner, 0.0)
        total_p = total_p + jnp.where(valid, h * (2.0 * (p + corner) + h), 0.0)
    lane = iota((1, 128), 1)
    out = jnp.zeros((1, 128), F32)
    for index in range(6):
        total = sums_ref[index]
        if index == 3:
            total = total + total_r
        if index == 4:
            total = total + total_d
        if index == 5:
            total = total + total_p
        value = jnp.sum(jnp.sum(total, axis=0, keepdims=True), axis=1, keepdims=True)
        out = jnp.where(lane == index, value, out)
    out_ref[...] = jnp.broadcast_to(out, (128, 128))


def least_squares(magnitude, upper_first, below_first, upper_cross, upper_second, below_second):
    radius_first = jnp.sqrt(upper_first * upper_first + below_first * below_first)
    cosine_first = upper_first / radius_first
    sine_first = below_first / radius_first
    lifted_top = cosine_first * upper_cross + sine_first * upper_second
    lifted_low = cosine_first * upper_second - sine_first * upper_cross
    radius_second = jnp.sqrt(lifted_low * lifted_low + below_second * below_second)
    weight_second = -(sine_first * magnitude) * (lifted_low / radius_second) / radius_second
    weight_first = (cosine_first * magnitude - lifted_top * weight_second) / radius_first
    return (weight_first, weight_second)


def final_weights(gathered):
    total = jnp.sum(gathered, axis=0, keepdims=True)
    lane = iota((1, 128), 1)
    rr, rd, dd, re, de, ee = [
        jnp.sum(jnp.where(lane == index, total, 0.0), axis=1, keepdims=True) for index in range(6)
    ]
    square = rr + EPSILON
    magnitude = jnp.sqrt(square)
    h11 = (rr + rd) / square
    gap = -(rd - EPSILON) / square
    h21_square = jnp.maximum((dd + 2.0 * gap * rd + gap * gap * rr) / square, 0.0) + EPSILON
    h21 = jnp.sqrt(h21_square)
    unit = 1.0 / (magnitude * h21)
    h12 = (gap * rr + (1.0 + gap) * rd + re) * unit / magnitude
    h22 = (
        gap * (gap * rr + rd) + (1.0 + gap) * (gap * rd + dd) + (gap * re + de)
    ) * unit * unit
    c_r = gap * unit - h12 / magnitude - h22 * gap * unit
    c_d = (1.0 + gap - h22) * unit
    c_e = unit
    h32_square = (
        c_r * c_r * rr + c_d * c_d * dd + c_e * c_e * ee
        + 2.0 * (c_r * c_d * rd + c_r * c_e * re + c_d * c_e * de)
    )
    h32 = jnp.sqrt(jnp.maximum(h32_square, 0.0) + EPSILON)
    y1, y2 = least_squares(magnitude, h11, h21, h12, h22, h32)
    return y1 / magnitude + y2 * gap * unit, y2 * unit


def last_step(
    table, gathered_ref, pairs_hbm, state_hbm, z1_hbm,
    out_hbm,
    u, z0, z1, out, sem_in, sem_out,
):
    def incoming(i):
        return [
            pltpu.make_async_copy(source, chunk(target, i), sem_in.at[n, i])
            for n, (source, target) in enumerate(
                (
                    (chunk(pairs_hbm, i).at[:, pl.ds(0, 128)], u),
                    (chunk(state_hbm, i).at[:, pl.ds(576, 128)], z0),
                    (chunk(z1_hbm, i), z1),
                )
            )
        ]

    for i in range(CHUNKS):
        for copy in incoming(i):
            copy.start()
    out[...] = jnp.zeros(out.shape, F32)
    weight0, weight1 = final_weights(gathered_ref[...])

    def body(i, carry):
        for copy in incoming(i):
            copy.wait()
        for k in range(CHUNK):
            j = i * CHUNK + k
            new = u[j] + weight0 * z0[j] + weight1 * z1[j]
            slots = [jnp.where(table[2 * j + r] >= 0, table[2 * j + r], SLOTS) for r in range(2)]
            for c in range(2):
                for r, x in enumerate(split_up(new[64 * c : 64 * c + 64])):
                    out[slots[r], pl.ds(c, 32, stride=2), :] = x
        return carry

    lax.fori_loop(0, CHUNKS, body, 0)
    copy = pltpu.make_async_copy(out.at[pl.ds(0, SLOTS)], out_hbm, sem_out)
    copy.start()
    copy.wait()


def call(kernel, outs, specs, scratch=(), out_specs=None):
    return pl.pallas_call(
        kernel,
        out_shape=outs,
        in_specs=specs,
        out_specs=out_specs if out_specs is not None else jax.tree.map(lambda _: vmem(), outs),
        scratch_shapes=list(scratch),
        compiler_params=params(),
    )


def hbm():
    return pl.BlockSpec(memory_space=pl.ANY)


def square(rows=128):
    return pltpu.VMEM((rows, 128), F32)


def buffer(*shape, dtype=F32):
    return pltpu.VMEM(shape, dtype)


def sems(*shape):
    return pltpu.SemaphoreType.DMA(shape)


def vector_view(x):
    return x.reshape(64, 2, 32, 128).transpose(0, 2, 1, 3).reshape(64, 64, 128)


def field_view(x):
    return x.reshape(8, 8, 32, 128).transpose(0, 2, 1, 3).reshape(8, 256, 128)


def exchange(x):
    return lax.all_to_all(x, "dev", split_axis=0, concat_axis=0, tiled=True)


def from_groups(arrival, received, count):
    side = struct(8, 8 * count, 128)
    south, north = call(boundary, (side, side), [smem(), vmem()])(arrival, received)
    size = lax.axis_size("grp")
    ahead = [(i, (i + 1) % size) for i in range(size)]
    return lax.ppermute(north, "grp", ahead), lax.ppermute(south, "grp", [(j, i) for i, j in ahead])


def shards(velocity, forcing, mass, coriolis, viscosity, lines, tile_source_slot, ocean_tile):
    owner = tile_source_slot // SLOTS % PAIRS
    order = jnp.arange(TILES)
    sooner = (owner[None, :] == owner[:, None]) & (order[None, :] < order[:, None])
    arrival = owner * 2 + jnp.sum(sooner.astype(jnp.int32), axis=1)

    u, b = vector_view(velocity), vector_view(forcing)
    a, f, z, p = [field_view(x) for x in (mass, coriolis, viscosity, lines)]

    message, table, codes, pairs = call(
        first_edges,
        (
            struct(PAIRS * 32, 128), struct(TABLE, dtype=jnp.int32), struct(CODES, dtype=jnp.int32),
            struct(PAIRS, 192, 128),
        ),
        [smem(), hbm(), hbm()],
        [
            buffer(64, 64, 128), buffer(8, 256, 128), buffer(PAIRS, 192, 128),
            square(), square(), square(), sems(2), sems(CHUNKS),
        ],
        (vmem(), smem(), smem(), hbm()),
    )(ocean_tile, u, z)
    weight = call(
        line_weights, struct(PAIRS, 256, 256, dtype=BF16), [smem(), vmem()],
        [buffer(PAIRS, 256, 256, dtype=BF16), buffer(CHUNK, 128, 128), sems(CHUNKS)], hbm(),
    )(table, p)
    fields = call(
        pair_fields, struct(PAIRS, 256, 128), [smem(), vmem(), vmem(), vmem()],
        [buffer(PAIRS, 256, 128), sems(CHUNKS)], hbm(),
    )(table, b, a, f)

    received = exchange(message.reshape(PAIRS, 32, 128))
    halo, face = call(
        first_return, (struct(PAIRS, 16, 128), struct(TILES, 8, 128)), [smem()] + [vmem()] * 3
    )(arrival, received, *from_groups(arrival, received, 2))
    halo = exchange(halo).reshape(PAIRS * 16, 128)

    state, message, rowcoef, colcoef = call(
        first_step,
        (struct(PAIRS, STATE, 128), struct(PAIRS * 24, 128), struct(PAIRS * 8, 128), struct(128, 128)),
        [smem(), vmem(), hbm(), hbm(), hbm()],
        [
            buffer(PAIRS, 192, 128), buffer(PAIRS, 256, 128), buffer(PAIRS, 256, 256, dtype=BF16),
            buffer(PAIRS, STATE, 128), square(), square(), square(), square(), square(),
            sems(3, CHUNKS), sems(CHUNKS),
        ],
        (hbm(), vmem(), vmem(), vmem()),
    )(codes, halo, pairs, fields, weight)
    earlier = exchange(message.reshape(PAIRS, 24, 128))
    halo = call(second_return, struct(PAIRS, 8, 128), [smem()] + [vmem()] * 3)(
        arrival, earlier, *from_groups(arrival, earlier, 1)
    )
    halo = exchange(halo).reshape(PAIRS * 8, 128)

    z1, message, sums = call(
        second_step,
        (struct(PAIRS, 128, 128), struct(PAIRS * 32, 128), struct(6, 8, 128)),
        [smem(), vmem(), vmem(), vmem(), hbm(), hbm()],
        [
            buffer(PAIRS, STATE, 128), buffer(PAIRS, 256, 256, dtype=BF16), buffer(PAIRS, 128, 128),
            square(), square(), square(), square(), square(), sems(2, CHUNKS), sems(CHUNKS),
        ],
        (hbm(), vmem(), vmem()),
    )(codes, halo, rowcoef, colcoef, state, weight)
    received = exchange(message.reshape(PAIRS, 32, 128))
    partial = call(edge_sums, struct(128, 128), [smem()] + [vmem()] * 6)(
        arrival, received, *from_groups(arrival, received, 1), earlier, face, sums
    )
    gathered = lax.all_to_all(partial, ("grp", "dev"), split_axis=0, concat_axis=0, tiled=True)

    out = call(
        last_step, struct(SLOTS, 64, 128), [smem(), vmem(), hbm(), hbm(), hbm()],
        [buffer(PAIRS, 128, 128), buffer(PAIRS, 128, 128), buffer(PAIRS, 128, 128), buffer(SLOTS + 1, 64, 128),
         sems(3, CHUNKS), pltpu.SemaphoreType.DMA],
        hbm(),
    )(table, gathered, pairs, state, z1)
    return out.reshape(64, 32, 2, 128).transpose(0, 2, 1, 3).reshape(64, 2, 4096)


def solution(mesh):
    return jax.shard_map(
        shards,
        mesh=mesh,
        in_specs=(
            P(("grp", "dev"), None, None),
            P(("grp", "dev"), None, None),
            P(("grp", "dev"), None),
            P(("grp", "dev"), None),
            P(("grp", "dev"), None),
            P(("grp", "dev"), None),
            P(("grp", "dev")),
            P(("grp", "dev")),
        ),
        out_specs=P(("grp", "dev"), None, None),
        check_vma=False,
    )
```

```python
import jax
import jax.numpy as jnp
from jax import lax
from jax.experimental import pallas as pl
from jax.experimental.pallas import tpu as pltpu
from jax.sharding import PartitionSpec as P

F32 = jnp.float32
BF16 = jnp.bfloat16
SLOTS = 64
PAIRS = 32
TILES = 32
CHUNK = 8
CHUNKS = PAIRS // CHUNK
TABLE = 72
CODES = 144
STATE = 704
EPSILON = 1e-06


def params(mebibytes):
    return pltpu.CompilerParams(vmem_limit_bytes=mebibytes * 1024 * 1024)


def vmem():
    return pl.BlockSpec(memory_space=pltpu.VMEM)


def smem():
    return pl.BlockSpec(memory_space=pltpu.SMEM)


def struct(*shape, dtype=F32):
    return jax.ShapeDtypeStruct(shape, dtype)


def resident(*shape, dtype=F32):
    return pltpu.VMEM(shape, dtype)


def held(x):
    return pltpu.with_memory_space_constraint(x, pltpu.VMEM)


def stored(*shape, dtype=F32):
    return pltpu.HBM(shape, dtype)


def kept(x):
    return pltpu.with_memory_space_constraint(x, pltpu.HBM)


def iota(shape, dim):
    return lax.broadcasted_iota(jnp.int32, shape, dim)


def roll(x, shift, axis):
    return pltpu.roll(x, shift, axis)


def pair_up(t0, t1):
    low = iota(t0.shape, 1) < 64
    crossed = roll(jnp.where(low, t1, t0), 64, 1)
    return jnp.concatenate([jnp.where(low, t0, crossed), jnp.where(low, crossed, t1)], axis=0)


def split_up(q):
    even, odd = q[:32], q[32:]
    low = iota(even.shape, 1) < 64
    crossed = roll(jnp.where(low, odd, even), 64, 1)
    return jnp.where(low, even, crossed), jnp.where(low, crossed, odd)


def load_tile(ref, index, offset, step):
    rows = [ref[index, pl.ds(offset + step * q, 8, stride=4 * step), :] for q in range(4)]
    return jnp.concatenate(rows, axis=0)


def load_field(ref, table, j, empty):
    tiles = []
    for r in range(2):
        s = table[2 * j + r]
        t = jnp.maximum(s, 0)
        tiles.append(jnp.where(s >= 0, load_tile(ref, t // 8, t % 8, 8), empty))
    return pair_up(*tiles)


def load_vector(ref, table, j):
    parts = []
    for c in range(2):
        tiles = []
        for r in range(2):
            s = table[2 * j + r]
            tiles.append(jnp.where(s >= 0, load_tile(ref, jnp.maximum(s, 0), c, 2), 0.0))
        parts.append(pair_up(*tiles))
    return parts


def put_columns(acc_ref, x, j):
    mine = ((iota(x.shape, 1) % 64) // 2) == j
    rows = slice(0, x.shape[0])
    acc_ref[rows, :] = jnp.where(mine, roll(x, 2 * j + 1, 1), acc_ref[rows, :])


def get_columns(acc, j):
    return roll(acc, 128 - (2 * j + 1), 1)


COLUMN_ROWS = (1, 64, 65, 0)


def columns_to_message(acc_ref, turned_ref, message_ref, first, stride):
    turned_ref[...] = acc_ref[...].T
    for row, source in enumerate(COLUMN_ROWS):
        message_ref[pl.ds(first + row, 32, stride=stride), :] = turned_ref[pl.ds(source, 32, stride=2), :]


def message_to_columns(message_ref, turned_ref, acc_ref, first, stride):
    for row, source in enumerate(COLUMN_ROWS):
        turned_ref[pl.ds(source, 32, stride=2), :] = message_ref[pl.ds(first + row, 32, stride=stride), :]
    acc_ref[...] = turned_ref[...].T


def put_rows(message_ref, x, base):
    for row, source in enumerate((0, 63, 64, 127)):
        message_ref[pl.ds(base + 4 + row, 1), :] = x[source : source + 1, :]


def south_of(x, halo=None):
    even, odd = x[:32], x[32:]
    below = roll(odd[24:], 1, 0)
    if halo is not None:
        below = jnp.where(iota(below.shape, 0) == 0, halo, below)
    return jnp.concatenate([below, odd[:24], even], axis=0)


def north_of(x, halo=None):
    even, odd = x[:32], x[32:]
    above = roll(even[:8], 7, 0)
    if halo is not None:
        above = jnp.where(iota(above.shape, 0) == 7, halo, above)
    return jnp.concatenate([odd, even[8:], above], axis=0)


def tile_part(y, west, south, turn):
    parts = []
    for c in range(2):
        rows = slice(64 * c, 64 * c + 64)
        x, w, s = y[rows], west[rows], south[rows]
        even, odd = x[:32], x[32:]
        s_even, s_odd = s[:32], s[32:]
        across = w * roll(x, 1, 1) + roll(w * x, 127, 1)
        up = s_even * even
        along = jnp.concatenate(
            [
                s_even[:8] * roll(odd[24:], 1, 0) + s_odd[:8] * odd[:8],
                s_even[8:] * odd[:24] + s_odd[8:] * odd[8:],
                s_odd[:24] * even[:24] + up[8:],
                s_odd[24:] * even[24:] + roll(up[:8], 7, 0),
            ],
            axis=0,
        )
        other = y[64:] if c == 0 else y[:64]
        spin = turn * other
        parts.append(x - across - along - spin if c == 0 else x - across - along + spin)
    return jnp.concatenate(parts, axis=0)


def line_solve(t, weight):
    high = t.astype(BF16)
    low = (t - high.astype(F32)).astype(BF16)
    out = lax.dot_general(
        jnp.concatenate([high, low], axis=1),
        weight,
        (((1,), (0,)), ((), ())),
        preferred_element_type=F32,
    )
    return out[:, :128] + out[:, 128:]


def relax(q, weight, west, south, turn):
    y = line_solve(q, weight)
    for _ in range(2):
        y = y + line_solve(q - tile_part(y, west, south, turn), weight)
    return y


NONE = 99
CODE_W = 72


def make_tables(ocean, table, codes):
    def clear(i, carry):
        table[i] = -1
        return carry

    def clear_codes(i, carry):
        codes[i] = NONE
        return carry

    def place(s, carry):
        t = ocean[s]
        j = jnp.where(t >= 0, (t >> 5) & 31, 32)
        held = table[2 * j]
        before = ocean[jnp.maximum(held, 0)]
        keep = (held >= 0) & (before < t)
        table[2 * j] = jnp.where(keep, held, s)
        table[2 * j + 1] = jnp.where(keep, s, held)
        return carry

    def code(p, carry):
        s = table[p]
        t = ocean[jnp.maximum(s, 0)]
        column, row = t & 7, (t >> 3) & 3
        codes[p + 2] = jnp.where((s >= 0) & (column == 7), row, NONE)
        codes[CODE_W + p] = jnp.where((s >= 0) & (column == 0), row + 4, NONE)
        return carry

    lax.fori_loop(0, TABLE, clear, 0, unroll=8)
    lax.fori_loop(0, CODES, clear_codes, 0, unroll=8)
    lax.fori_loop(0, SLOTS, place, 0, unroll=4)
    lax.fori_loop(0, 2 * PAIRS, code, 0, unroll=8)


def put_extras(codes, turned, message_ref, first, stride):
    row = iota((8, 128), 0)

    def body(m, carry):
        before, after = 2 * jnp.maximum(m - 1, 0), 2 * jnp.minimum(m + 1, PAIRS - 1)
        total = jnp.zeros((8, 128), F32)
        for r in range(2):
            east = turned[pl.ds(before + (64, 0)[r], 1), :]
            west = turned[pl.ds(after + (1, 65)[r], 1), :]
            total = jnp.where(row == codes[2 * m + r], east, total)
            total = jnp.where(row == codes[CODE_W + 2 * m + 2 + r], west, total)
        message_ref[pl.ds(pl.multiple_of(m * stride + first, 8), 8), :] = total
        return carry

    lax.fori_loop(0, PAIRS, body, 0, unroll=8)


def chunk(ref, i):
    return ref.at[pl.ds(i * CHUNK, CHUNK)]


def outgoing(source, target, sem, i):
    return pltpu.make_async_copy(chunk(source, i), chunk(target, i), sem.at[i])


def first_edges(
    ocean, u_hbm, z_hbm,
    message_ref, table, codes, pairs,
    u_ref, z_ref, acc_v, acc_z, turned, sem_in,
):
    copies = [
        pltpu.make_async_copy(u_hbm, u_ref, sem_in.at[0]),
        pltpu.make_async_copy(z_hbm, z_ref, sem_in.at[1]),
    ]
    for copy in copies:
        copy.start()
    make_tables(ocean, table, codes)
    for copy in copies:
        copy.wait()

    def body(i, carry):
        for k in range(CHUNK):
            j = i * CHUNK + k
            u, v = load_vector(u_ref, table, j)
            z = load_field(z_ref, table, j, 0.0)
            vector = jnp.concatenate([u, v], axis=0)
            pairs[j, 0:128, :] = vector
            pairs[j, 128:192, :] = z
            put_columns(acc_v, vector, j)
            put_columns(acc_z, z, j)
            put_rows(message_ref, vector, 32 * j)
            put_rows(message_ref, jnp.concatenate([z, z], axis=0), 32 * j + 8)
        return carry

    lax.fori_loop(0, CHUNKS, body, 0)
    columns_to_message(acc_v, turned, message_ref, 0, 32)
    put_extras(codes, turned, message_ref, 16, 32)
    acc_z[64:128, :] = acc_z[0:64, :]
    columns_to_message(acc_z, turned, message_ref, 8, 32)
    put_extras(codes, turned, message_ref, 24, 32)


def pair_fields(table, b_hbm, a_hbm, f_hbm, out_hbm, b_ref, a_ref, f_ref, pairs, sem_in, sem_out):
    copies = [
        pltpu.make_async_copy(source, target, sem_in.at[n])
        for n, (source, target) in enumerate(((b_hbm, b_ref), (a_hbm, a_ref), (f_hbm, f_ref)))
    ]
    for copy in copies:
        copy.start()
    for copy in copies:
        copy.wait()

    def body(i, carry):
        for k in range(CHUNK):
            j = i * CHUNK + k
            bu, bv = load_vector(b_ref, table, j)
            pairs[j, 0:64, :] = bu
            pairs[j, 64:128, :] = bv
            pairs[j, 128:192, :] = load_field(a_ref, table, j, 1.0)
            pairs[j, 192:256, :] = load_field(f_ref, table, j, 0.0)
        outgoing(pairs, out_hbm, sem_out, i).start()
        return carry

    lax.fori_loop(0, CHUNKS, body, 0)
    for i in range(CHUNKS):
        outgoing(pairs, out_hbm, sem_out, i).wait()


def line_weights(table, p_hbm, out_hbm, p_ref, weight, natural, sem_in, sem_out):
    copy = pltpu.make_async_copy(p_hbm, p_ref, sem_in)
    copy.start()
    copy.wait()
    low = iota((32, 128), 1) < 64

    def body(i, carry):
        for k in range(CHUNK):
            j = i * CHUNK + k
            tiles = []
            for r in range(2):
                s = table[2 * j + r]
                t = jnp.maximum(s, 0)
                x = p_ref[t // 8, pl.ds(t % 8, 32, stride=8), :]
                tiles.append(jnp.where(s >= 0, x, 0.0))
            t0, t1 = tiles
            natural[k, pl.ds(0, 32, stride=2), :] = jnp.where(low, t0, 0.0)
            natural[k, pl.ds(1, 32, stride=2), :] = jnp.where(low, roll(t0, 64, 1), 0.0)
            natural[k, pl.ds(64, 32, stride=2), :] = jnp.where(low, 0.0, roll(t1, 64, 1))
            natural[k, pl.ds(65, 32, stride=2), :] = jnp.where(low, 0.0, t1)
            turned = natural[k].T
            high = turned.astype(BF16)
            rest = (turned - high.astype(F32)).astype(BF16)
            both = jnp.concatenate([high, rest], axis=1)
            weight[j, 0:128, :] = both
            weight[j, 128:256, :] = both
        outgoing(weight, out_hbm, sem_out, i).start()
        return carry

    lax.fori_loop(0, CHUNKS, body, 0)
    for i in range(CHUNKS):
        outgoing(weight, out_hbm, sem_out, i).wait()


def side_masks():
    x = iota((64, 128), 1) % 64
    return x == 0, x == 63


KX = (1.25, 0.25)
KY = (0.25, 1.25)


def first_step(
    codes, halo_ref, pairs, fields_hbm, weight_hbm,
    state, weight, message_ref, edges_ref, rowcoef_ref, colcoef_ref,
    fields, acc_z, acc_r, hv, hz, turned, sem,
):
    def incoming(i):
        return [
            pltpu.make_async_copy(chunk(source, i), chunk(target, i), sem.at[n, i])
            for n, (source, target) in enumerate(((fields_hbm, fields), (weight_hbm, weight)))
        ]

    for i in range(CHUNKS):
        for copy in incoming(i):
            copy.start()
    message_to_columns(halo_ref, turned, hv, 0, 16)
    message_to_columns(halo_ref, turned, hz, 8, 16)
    at_west, at_east = side_masks()

    def one(j):
        u0 = pairs[j, 0:64, :], pairs[j, 64:128, :]
        z = pairs[j, 128:192, :]
        b = fields[j, 0:64, :], fields[j, 64:128, :]
        a, f = fields[j, 128:192, :], fields[j, 192:256, :]
        side_v = get_columns(hv[...], j)
        side_z = get_columns(hz[0:64, :], j)
        rows = halo_ref[pl.ds(pl.multiple_of(16 * j, 16), 16), :]
        face_w = 0.5 * (z + jnp.where(at_west, side_z, roll(z, 1, 1)))
        face_e = 0.5 * (z + jnp.where(at_east, side_z, roll(z, 127, 1)))
        face_s = 0.5 * (z + south_of(z, rows[12:13]))
        face_n = 0.5 * (z + north_of(z, rows[13:14]))
        scale, diag = [], []
        for c in range(2):
            d = a + KX[c] * (face_w + face_e) + KY[c] * (face_s + face_n)
            diag.append(d)
            scale.append(lax.rsqrt(d))
        turn = f * scale[0] * scale[1]
        rhat, west, south, column, plain = [], [], [], [], []
        for c in range(2):
            x, s = u0[c], scale[c]
            side = side_v[64 * c : 64 * c + 64]
            x_w = jnp.where(at_west, side, roll(x, 1, 1))
            x_e = jnp.where(at_east, side, roll(x, 127, 1))
            x_s = south_of(x, rows[4 + 2 * c : 5 + 2 * c])
            x_n = north_of(x, rows[5 + 2 * c : 6 + 2 * c])
            spin = -f * u0[1] if c == 0 else f * u0[0]
            applied = (
                diag[c] * x + spin
                - KX[c] * (face_w * x_w + face_e * x_e)
                - KY[c] * (face_s * x_s + face_n * x_n)
            )
            residual = b[c] - applied
            plain.append(residual)
            rhat.append(s * residual)
            k_w = KX[c] * s * face_w
            k_e = KX[c] * s * face_e
            k_s = KY[c] * s * face_s
            west.append(jnp.where(at_west, 0.0, k_w * roll(s, 1, 1)))
            south.append(k_s * south_of(s, jnp.zeros((1, 128), F32)))
            column.append(jnp.where(at_west, k_w, k_e))
            rowcoef_ref[pl.ds(8 * j + 4 + 2 * c, 1), :] = k_s[0:1]
            rowcoef_ref[pl.ds(8 * j + 5 + 2 * c, 1), :] = KY[c] * s[63:64] * face_n[63:64]
        rhat = jnp.concatenate(rhat, axis=0)
        plain = jnp.concatenate(plain, axis=0)
        west = jnp.concatenate(west, axis=0)
        south = jnp.concatenate(south, axis=0)
        put_columns(colcoef_ref, jnp.concatenate(column, axis=0), j)
        put_columns(acc_r, plain, j)
        put_rows(edges_ref, plain, 8 * j)
        state[j, 0:128, :] = west
        state[j, 128:256, :] = south
        state[j, 256:384, :] = jnp.concatenate(diag, axis=0)
        state[j, 384:512, :] = rhat
        state[j, 512:576, :] = turn
        y = relax(rhat, weight[j], west, south, turn)
        z0 = jnp.concatenate(scale, axis=0) * y
        state[j, 576:704, :] = z0
        put_columns(acc_z, z0, j)
        put_rows(message_ref, z0, 16 * j)

    def body(i, carry):
        for copy in incoming(i):
            copy.wait()
        for k in range(CHUNK):
            one(i * CHUNK + k)
        return carry

    lax.fori_loop(0, CHUNKS, body, 0)
    columns_to_message(acc_r, turned, edges_ref, 0, 8)
    columns_to_message(acc_z, turned, message_ref, 0, 16)
    put_extras(codes, turned, message_ref, 8, 16)


def second_step(
    codes, halo_ref, rowcoef_ref, colcoef_ref, state, weight,
    z1s, message_ref, sums_ref,
    acc_z, acc_p, acc_d, hv, turned,
):
    message_to_columns(halo_ref, turned, hv, 0, 16)
    hv[...] = hv[...] * colcoef_ref[...]
    lane = iota((128, 128), 1) % 64
    at_side = (lane == 0) | (lane == 63)
    first, last = iota((8, 128), 0) == 0, iota((8, 128), 0) == 7
    sums_ref[...] = jnp.zeros((6, 8, 128), F32)

    def one(j):
        west, south, turn = state[j, 0:128, :], state[j, 128:256, :], state[j, 512:576, :]
        diag = state[j, 256:384, :]
        rhat = state[j, 384:512, :]
        scale = lax.rsqrt(diag)
        root = diag * scale
        y0 = root * state[j, 576:704, :]
        what = tile_part(y0, west, south, turn)
        what = what - jnp.where(at_side, get_columns(hv[...], j), 0.0)
        base = pl.multiple_of(8 * j, 8)
        rows = halo_ref[pl.ds(pl.multiple_of(16 * j, 16), 8), :] * rowcoef_ref[pl.ds(base, 8), :]
        fixed = []
        for c in range(2):
            part = what[64 * c : 64 * c + 64]
            low = part[:8] - jnp.where(first, rows[4 + 2 * c : 5 + 2 * c], 0.0)
            high = part[56:] - jnp.where(last, rows[5 + 2 * c : 6 + 2 * c], 0.0)
            fixed += [low, part[8:56], high]
        what = jnp.concatenate(fixed, axis=0)
        dhat = what - rhat
        y1 = relax(dhat, weight[j], west, south, turn)
        phat = tile_part(y1, west, south, turn) - dhat
        z1 = scale * y1
        z1s[j] = z1
        r, d, p = root * rhat, root * dhat, root * phat
        for index, (left, right) in enumerate(((r, r), (r, d), (d, d), (r, p), (d, p), (p, p))):
            product = left * right
            total = product[0:8]
            for k in range(1, 16):
                total = total + product[8 * k : 8 * k + 8]
            sums_ref[index] += total
        for k, (acc, x) in enumerate(((acc_z, z1), (acc_p, p), (acc_d, d))):
            put_columns(acc, x, j)
            put_rows(message_ref, x, 32 * j + 8 * k)

    def body(i, carry):
        for k in range(CHUNK):
            one(i * CHUNK + k)
        return carry

    lax.fori_loop(0, CHUNKS, body, 0)
    columns_to_message(acc_p, turned, message_ref, 8, 32)
    columns_to_message(acc_d, turned, message_ref, 16, 32)
    columns_to_message(acc_z, turned, message_ref, 0, 32)
    put_extras(codes, turned, message_ref, 24, 32)


def to_normal(x, r):
    row = iota((8, 128), 0)
    return jnp.where(r == 1, jnp.where(row < 4, roll(x, 6, 0), roll(x, 64, 1)), x)


def halo_of(west, east, south, north):
    row = iota((8, 128), 0)
    side = jnp.where(row == 0, roll(west, 7, 0), roll(east, 1, 0))
    end = jnp.where(row % 2 == 0, roll(south, 7, 0), roll(north, 1, 0))
    return jnp.where(row < 2, side, jnp.where(row >= 4, end, 0.0))


def tile_block(arrival, received_ref, t, k):
    at = arrival[t]
    return to_normal(received_ref[at // 2, 8 * k : 8 * k + 8, :], at % 2)


def boundary(arrival, received_ref, south_ref, north_ref):
    for k in range(south_ref.shape[1] // 8):
        rows = slice(8 * k, 8 * k + 8)
        for x in range(8):
            south_ref[x, rows, :] = tile_block(arrival, received_ref, x, k)
            north_ref[x, rows, :] = tile_block(arrival, received_ref, 24 + x, k)


def tile_halos(arrival, received_ref, from_south, from_north, k, extra):
    group = lax.axis_index("grp")
    blocks = [tile_block(arrival, received_ref, t, k) for t in range(TILES)]
    sides = received_ref[0, 8 * extra : 8 * extra + 8, :]
    for o in range(1, PAIRS):
        sides = sides + received_ref[o, 8 * extra : 8 * extra + 8, :]
    rows = slice(8 * k, 8 * k + 8)
    last = lax.axis_size("grp") - 1
    below = [jnp.where(group > 0, from_south[x, rows, :], 0.0) for x in range(8)]
    above = [jnp.where(group < last, from_north[x, rows, :], 0.0) for x in range(8)]
    halos = []
    for t in range(TILES):
        ty, tx = t // 8, t % 8
        halos.append(
            halo_of(
                blocks[t - 1] if tx > 0 else roll(sides, (1 - ty) % 8, 0),
                blocks[t + 1] if tx < 7 else roll(sides, 4 - ty, 0),
                blocks[t - 8] if ty > 0 else below[tx],
                blocks[t + 8] if ty < 3 else above[tx],
            )
        )
    return blocks, halos


def hand_back(arrival, t, k, halo, out_ref):
    at = arrival[t]
    r = at % 2
    row, lane = iota((8, 128), 0), iota((8, 128), 1)
    placed = jnp.where(r == 1, jnp.where(row < 4, roll(halo, 2, 0), roll(halo, 64, 1)), halo)
    mine = ((row < 4) & (row // 2 == r)) | ((row >= 4) & (lane // 64 == r))
    rows = slice(8 * k, 8 * k + 8)
    out_ref[at // 2, rows, :] += jnp.where(mine, placed, 0.0)


def first_return(arrival, received_ref, south, north, out_ref, face_ref):
    row, lane = iota((8, 128), 0), iota((8, 128), 1)
    along_x = jnp.where(lane < 64, KX[0], KX[1])
    along_y = jnp.where(row < 6, KY[0], KY[1])
    factor = 0.5 * jnp.where(row < 4, along_x, along_y)
    out_ref[...] = jnp.zeros(out_ref.shape, F32)
    for k in range(2):
        blocks, halos = tile_halos(arrival, received_ref, south, north, k, 2 + k)
        for t in range(TILES):
            hand_back(arrival, t, k, halos[t], out_ref)
            if k == 1:
                face_ref[t] = factor * (blocks[t] + halos[t])


def second_return(arrival, received_ref, south, north, edges_ref, out_ref):
    out_ref[:, 0:8, :] = jnp.zeros((PAIRS, 8, 128), F32)
    out_ref[:, 8:16, :] = edges_ref[...]
    blocks, halos = tile_halos(arrival, received_ref, south, north, 0, 1)
    for t in range(TILES):
        hand_back(arrival, t, 0, halos[t], out_ref)


def edge_sums(arrival, received_ref, south, north, earlier_ref, face_ref, sums_ref, out_ref):
    row, lane = iota((8, 128), 0), iota((8, 128), 1)
    valid = (row < 2) | ((row >= 4) & (lane < 64))
    total_r = jnp.zeros((8, 128), F32)
    total_d = jnp.zeros((8, 128), F32)
    total_p = jnp.zeros((8, 128), F32)
    blocks, halos = tile_halos(arrival, received_ref, south, north, 0, 3)
    for t in range(TILES):
        h = jnp.where(valid, -face_ref[t] * halos[t], 0.0)
        p = tile_block(arrival, received_ref, t, 1)
        d = tile_block(arrival, received_ref, t, 2)
        r = tile_block(arrival, earlier_ref, t, 1)
        total_r = total_r + jnp.where(valid, h * r, 0.0)
        total_d = total_d + jnp.where(valid, h * d, 0.0)
        wide_w = jnp.broadcast_to(h[0:1], (8, 128))
        wide_e = jnp.broadcast_to(h[1:2], (8, 128))
        corner_w = jnp.where(
            row == 4, wide_w,
            jnp.where(row == 5, roll(wide_w, 65, 1), jnp.where(row == 6, roll(wide_w, 64, 1), roll(wide_w, 1, 1))),
        )
        corner_e = jnp.where(
            row == 4, roll(wide_e, 63, 1),
            jnp.where(row == 5, wide_e, jnp.where(row == 6, roll(wide_e, 127, 1), roll(wide_e, 64, 1))),
        )
        corner = jnp.where(lane == 0, corner_w, jnp.where(lane == 63, corner_e, 0.0))
        corner = jnp.where(row >= 4, corner, 0.0)
        total_p = total_p + jnp.where(valid, h * (2.0 * (p + corner) + h), 0.0)
    lane = iota((1, 128), 1)
    out = jnp.zeros((1, 128), F32)
    for index in range(6):
        total = sums_ref[index]
        if index == 3:
            total = total + total_r
        if index == 4:
            total = total + total_d
        if index == 5:
            total = total + total_p
        value = jnp.sum(jnp.sum(total, axis=0, keepdims=True), axis=1, keepdims=True)
        out = jnp.where(lane == index, value, out)
    out_ref[...] = jnp.broadcast_to(out, (128, 128))


def least_squares(magnitude, upper_first, below_first, upper_cross, upper_second, below_second):
    radius_first = jnp.sqrt(upper_first * upper_first + below_first * below_first)
    cosine_first = upper_first / radius_first
    sine_first = below_first / radius_first
    lifted_top = cosine_first * upper_cross + sine_first * upper_second
    lifted_low = cosine_first * upper_second - sine_first * upper_cross
    radius_second = jnp.sqrt(lifted_low * lifted_low + below_second * below_second)
    weight_second = -(sine_first * magnitude) * (lifted_low / radius_second) / radius_second
    weight_first = (cosine_first * magnitude - lifted_top * weight_second) / radius_first
    return (weight_first, weight_second)


def final_weights(gathered):
    total = jnp.sum(gathered, axis=0, keepdims=True)
    lane = iota((1, 128), 1)
    rr, rd, dd, re, de, ee = [
        jnp.sum(jnp.where(lane == index, total, 0.0), axis=1, keepdims=True) for index in range(6)
    ]
    square = rr + EPSILON
    magnitude = jnp.sqrt(square)
    h11 = (rr + rd) / square
    gap = -(rd - EPSILON) / square
    h21_square = jnp.maximum((dd + 2.0 * gap * rd + gap * gap * rr) / square, 0.0) + EPSILON
    h21 = jnp.sqrt(h21_square)
    unit = 1.0 / (magnitude * h21)
    h12 = (gap * rr + (1.0 + gap) * rd + re) * unit / magnitude
    h22 = (
        gap * (gap * rr + rd) + (1.0 + gap) * (gap * rd + dd) + (gap * re + de)
    ) * unit * unit
    c_r = gap * unit - h12 / magnitude - h22 * gap * unit
    c_d = (1.0 + gap - h22) * unit
    c_e = unit
    h32_square = (
        c_r * c_r * rr + c_d * c_d * dd + c_e * c_e * ee
        + 2.0 * (c_r * c_d * rd + c_r * c_e * re + c_d * c_e * de)
    )
    h32 = jnp.sqrt(jnp.maximum(h32_square, 0.0) + EPSILON)
    y1, y2 = least_squares(magnitude, h11, h21, h12, h22, h32)
    return y1 / magnitude + y2 * gap * unit, y2 * unit


def last_step(
    table, gathered_ref, pairs, state, z1,
    out_hbm,
    out, sem_out,
):
    out[...] = jnp.zeros(out.shape, F32)
    weight0, weight1 = final_weights(gathered_ref[...])

    def body(i, carry):
        for k in range(CHUNK):
            j = i * CHUNK + k
            new = pairs[j, 0:128, :] + weight0 * state[j, 576:704, :] + weight1 * z1[j]
            slots = [jnp.where(table[2 * j + r] >= 0, table[2 * j + r], SLOTS) for r in range(2)]
            for c in range(2):
                for r, x in enumerate(split_up(new[64 * c : 64 * c + 64])):
                    for q in range(4):
                        out[slots[r], pl.ds(c + 2 * q, 8, stride=8), :] = x[8 * q : 8 * q + 8]
        return carry

    lax.fori_loop(0, CHUNKS, body, 0)
    copy = pltpu.make_async_copy(out.at[pl.ds(0, SLOTS)], out_hbm, sem_out)
    copy.start()
    copy.wait()


def call(kernel, outs, specs, scratch=(), out_specs=None, mebibytes=4):
    return pl.pallas_call(
        kernel,
        out_shape=outs,
        in_specs=specs,
        out_specs=out_specs if out_specs is not None else jax.tree.map(lambda _: vmem(), outs),
        scratch_shapes=list(scratch),
        compiler_params=params(mebibytes),
    )


def hbm():
    return pl.BlockSpec(memory_space=pl.ANY)


def square(rows=128):
    return pltpu.VMEM((rows, 128), F32)


def buffer(*shape, dtype=F32):
    return pltpu.VMEM(shape, dtype)


def sems(*shape):
    return pltpu.SemaphoreType.DMA(shape)


def vector_view(x):
    return x.reshape(64, 2, 32, 128).transpose(0, 2, 1, 3).reshape(64, 64, 128)


def field_view(x):
    return x.reshape(8, 8, 32, 128).transpose(0, 2, 1, 3).reshape(8, 256, 128)


def exchange(x):
    return lax.all_to_all(x, "dev", split_axis=0, concat_axis=0, tiled=True)


def from_groups(arrival, received, count):
    side = struct(8, 8 * count, 128)
    south, north = call(boundary, (side, side), [smem(), vmem()])(arrival, received)
    size = lax.axis_size("grp")
    ahead = [(i, (i + 1) % size) for i in range(size)]
    return lax.ppermute(north, "grp", ahead), lax.ppermute(south, "grp", [(j, i) for i, j in ahead])


def shards(velocity, forcing, mass, coriolis, viscosity, lines, tile_source_slot, ocean_tile):
    owner = tile_source_slot // SLOTS % PAIRS
    order = jnp.arange(TILES)
    sooner = (owner[None, :] == owner[:, None]) & (order[None, :] < order[:, None])
    arrival = owner * 2 + jnp.sum(sooner.astype(jnp.int32), axis=1)

    u, b = vector_view(velocity), vector_view(forcing)
    a, f, z, p = [field_view(x) for x in (mass, coriolis, viscosity, lines)]

    message, table, codes, pairs = call(
        first_edges,
        (
            struct(PAIRS * 32, 128), struct(TABLE, dtype=jnp.int32), struct(CODES, dtype=jnp.int32),
            resident(PAIRS, 192, 128),
        ),
        [smem(), hbm(), hbm()],
        [buffer(64, 64, 128), buffer(8, 256, 128), square(), square(), square(), sems(2)],
        (vmem(), smem(), smem(), vmem()),
        8,
    )(kept(ocean_tile), kept(u), kept(z))
    weight = call(
        line_weights, stored(PAIRS, 256, 256, dtype=BF16), [smem(), hbm()],
        [
            buffer(8, 256, 128), buffer(PAIRS, 256, 256, dtype=BF16), buffer(CHUNK, 128, 128),
            pltpu.SemaphoreType.DMA, sems(CHUNKS),
        ],
        hbm(), 8,
    )(table, kept(p))
    fields = call(
        pair_fields, stored(PAIRS, 256, 128), [smem(), hbm(), hbm(), hbm()],
        [
            buffer(64, 64, 128), buffer(8, 256, 128), buffer(8, 256, 128), buffer(PAIRS, 256, 128),
            sems(3), sems(CHUNKS),
        ],
        hbm(), 12,
    )(table, kept(b), kept(a), kept(f))

    received = exchange(message.reshape(PAIRS, 32, 128))
    received, weight = lax.optimization_barrier((received, weight))
    halo, face = call(
        first_return, (struct(PAIRS, 16, 128), struct(TILES, 8, 128)), [smem()] + [vmem()] * 3
    )(arrival, received, *from_groups(arrival, received, 2))
    halo = exchange(halo).reshape(PAIRS * 16, 128)

    state, weight, message, edges, rowcoef, colcoef = call(
        first_step,
        (
            resident(PAIRS, STATE, 128), resident(PAIRS, 256, 256, dtype=BF16), struct(PAIRS * 16, 128), struct(PAIRS * 8, 128),
            struct(PAIRS * 8, 128), struct(128, 128),
        ),
        [smem(), vmem(), vmem(), hbm(), hbm()],
        [buffer(PAIRS, 256, 128)] + [square()] * 5 + [sems(2, CHUNKS)],
        [vmem()] * 6,
        mebibytes=16,
    )(codes, halo, held(pairs), kept(fields), kept(weight))
    received = exchange(message.reshape(PAIRS, 16, 128))
    halo = call(second_return, struct(PAIRS, 16, 128), [smem()] + [vmem()] * 4)(
        arrival, received, *from_groups(arrival, received, 1), edges.reshape(PAIRS, 8, 128)
    )
    earlier = exchange(halo)
    halo = earlier.reshape(PAIRS * 16, 128)

    z1, message, sums = call(
        second_step,
        (resident(PAIRS, 128, 128), struct(PAIRS * 32, 128), struct(6, 8, 128)),
        [smem()] + [vmem()] * 5,
        [square()] * 5,
        mebibytes=8,
    )(codes, halo, rowcoef, colcoef, held(state), held(weight))
    received = exchange(message.reshape(PAIRS, 32, 128))
    partial = call(edge_sums, struct(128, 128), [smem()] + [vmem()] * 6)(
        arrival, received, *from_groups(arrival, received, 1), earlier, face, sums
    )
    gathered = lax.all_to_all(partial, ("grp", "dev"), split_axis=0, concat_axis=0, tiled=True)

    out = call(
        last_step, struct(SLOTS, 64, 128), [smem()] + [vmem()] * 4,
        [buffer(SLOTS + 1, 64, 128), pltpu.SemaphoreType.DMA],
        hbm(),
        8,
    )(table, gathered, held(pairs), held(state), held(z1))
    return out.reshape(64, 32, 2, 128).transpose(0, 2, 1, 3).reshape(64, 2, 4096)


def solution(mesh):
    return jax.shard_map(
        shards,
        mesh=mesh,
        in_specs=(
            P(("grp", "dev"), None, None),
            P(("grp", "dev"), None, None),
            P(("grp", "dev"), None),
            P(("grp", "dev"), None),
            P(("grp", "dev"), None),
            P(("grp", "dev"), None),
            P(("grp", "dev")),
            P(("grp", "dev")),
        ),
        out_specs=P(("grp", "dev"), None, None),
        check_vma=False,
    )
```

```python
import jax
import jax.numpy as jnp
from jax import lax
from jax.experimental import pallas as pl
from jax.experimental.pallas import tpu as pltpu
from jax.sharding import PartitionSpec as P

F32 = jnp.float32
BF16 = jnp.bfloat16
SLOTS = 64
PAIRS = 32
TILES = 32
CHUNK = 8
LONG = 16
CHUNKS = PAIRS // CHUNK
TABLE = 72
CODES = 144
STATE = 704
EPSILON = 1e-06


def params(mebibytes):
    return pltpu.CompilerParams(vmem_limit_bytes=mebibytes * 1024 * 1024)


def vmem():
    return pl.BlockSpec(memory_space=pltpu.VMEM)


def smem():
    return pl.BlockSpec(memory_space=pltpu.SMEM)


def struct(*shape, dtype=F32):
    return jax.ShapeDtypeStruct(shape, dtype)


def resident(*shape, dtype=F32):
    return pltpu.VMEM(shape, dtype)


def held(x):
    return pltpu.with_memory_space_constraint(x, pltpu.VMEM)


def kept(x):
    return pltpu.with_memory_space_constraint(x, pltpu.HBM)


def iota(shape, dim):
    return lax.broadcasted_iota(jnp.int32, shape, dim)


def roll(x, shift, axis):
    return pltpu.roll(x, shift, axis)


def pair_up(t0, t1):
    low = iota(t0.shape, 1) < 64
    crossed = roll(jnp.where(low, t1, t0), 64, 1)
    return jnp.concatenate([jnp.where(low, t0, crossed), jnp.where(low, crossed, t1)], axis=0)


def split_up(q):
    even, odd = q[:32], q[32:]
    low = iota(even.shape, 1) < 64
    crossed = roll(jnp.where(low, odd, even), 64, 1)
    return jnp.where(low, even, crossed), jnp.where(low, crossed, odd)


def load_tile(ref, index, offset, step):
    rows = [ref[index, pl.ds(offset + step * q, 8, stride=4 * step), :] for q in range(4)]
    return jnp.concatenate(rows, axis=0)


def load_field(ref, table, j, empty):
    tiles = []
    for r in range(2):
        s = table[2 * j + r]
        t = jnp.maximum(s, 0)
        tiles.append(jnp.where(s >= 0, load_tile(ref, t // 8, t % 8, 8), empty))
    return pair_up(*tiles)


def load_vector(ref, table, j):
    parts = []
    for c in range(2):
        tiles = []
        for r in range(2):
            s = table[2 * j + r]
            tiles.append(jnp.where(s >= 0, load_tile(ref, jnp.maximum(s, 0), c, 2), 0.0))
        parts.append(pair_up(*tiles))
    return parts


def put_columns(acc_ref, x, j):
    mine = ((iota(x.shape, 1) % 64) // 2) == j
    rows = slice(0, x.shape[0])
    acc_ref[rows, :] = jnp.where(mine, roll(x, 2 * j + 1, 1), acc_ref[rows, :])


def get_columns(acc, j):
    return roll(acc, 128 - (2 * j + 1), 1)


COLUMN_ROWS = (1, 64, 65, 0)


def columns_to_message(acc_ref, turned_ref, message_ref, first, stride):
    turned_ref[...] = acc_ref[...].T
    for row, source in enumerate(COLUMN_ROWS):
        message_ref[pl.ds(first + row, 32, stride=stride), :] = turned_ref[pl.ds(source, 32, stride=2), :]


def message_to_columns(message_ref, turned_ref, acc_ref, first, stride):
    for row, source in enumerate(COLUMN_ROWS):
        turned_ref[pl.ds(source, 32, stride=2), :] = message_ref[pl.ds(first + row, 32, stride=stride), :]
    acc_ref[...] = turned_ref[...].T


def put_rows(message_ref, x, base):
    for row, source in enumerate((0, 63, 64, 127)):
        message_ref[pl.ds(base + 4 + row, 1), :] = x[source : source + 1, :]


def south_of(x, halo=None):
    even, odd = x[:32], x[32:]
    below = roll(odd[24:], 1, 0)
    if halo is not None:
        below = jnp.where(iota(below.shape, 0) == 0, halo, below)
    return jnp.concatenate([below, odd[:24], even], axis=0)


def north_of(x, halo=None):
    even, odd = x[:32], x[32:]
    above = roll(even[:8], 7, 0)
    if halo is not None:
        above = jnp.where(iota(above.shape, 0) == 7, halo, above)
    return jnp.concatenate([odd, even[8:], above], axis=0)


def tile_part(y, west, south, turn):
    parts = []
    for c in range(2):
        rows = slice(64 * c, 64 * c + 64)
        x, w, s = y[rows], west[rows], south[rows]
        even, odd = x[:32], x[32:]
        s_even, s_odd = s[:32], s[32:]
        across = w * roll(x, 1, 1) + roll(w * x, 127, 1)
        up = s_even * even
        along = jnp.concatenate(
            [
                s_even[:8] * roll(odd[24:], 1, 0) + s_odd[:8] * odd[:8],
                s_even[8:] * odd[:24] + s_odd[8:] * odd[8:],
                s_odd[:24] * even[:24] + up[8:],
                s_odd[24:] * even[24:] + roll(up[:8], 7, 0),
            ],
            axis=0,
        )
        other = y[64:] if c == 0 else y[:64]
        spin = turn * other
        parts.append(x - across - along - spin if c == 0 else x - across - along + spin)
    return jnp.concatenate(parts, axis=0)


def line_solve(t, weight):
    high = t.astype(BF16)
    low = (t - high.astype(F32)).astype(BF16)
    out = lax.dot_general(
        jnp.concatenate([high, low], axis=1),
        jnp.concatenate([weight, weight], axis=0),
        (((1,), (0,)), ((), ())),
        preferred_element_type=F32,
    )
    return out[:, :128] + out[:, 128:]


def relax(q, weight, west, south, turn):
    y = line_solve(q, weight)
    for _ in range(2):
        y = y + line_solve(q - tile_part(y, west, south, turn), weight)
    return y


NONE = 99
CODE_W = 72


def make_table(ocean, table, count):
    def clear(i, carry):
        table[i] = -1
        return carry

    def clear_count(i, carry):
        count[i] = 0
        return carry

    def place(s, carry):
        t = ocean[s]
        j = jnp.where(t >= 0, (t >> 5) & 31, PAIRS)
        held = count[j] & 1
        table[2 * j + held] = s
        count[j] = held + 1
        return carry

    lax.fori_loop(0, TABLE, clear, 0, unroll=8)
    lax.fori_loop(0, PAIRS + 8, clear_count, 0, unroll=8)
    lax.fori_loop(0, SLOTS, place, 0, unroll=8)


def column_codes(ocean, table, codes, j):
    for r in range(2):
        p = 2 * j + r
        s = table[p]
        t = ocean[jnp.maximum(s, 0)]
        column, row = t & 7, (t >> 3) & 3
        codes[p + 2] = jnp.where((s >= 0) & (column == 7), row, NONE)
        codes[CODE_W + p] = jnp.where((s >= 0) & (column == 0), row + 4, NONE)


def land(source, arrival, first, t):
    slot = source[t]
    owner = (slot >> 6) & 31
    held = first[owner]
    later = (held >= 0) & (source[jnp.maximum(held, 0)] < slot)
    arrival[t] = 2 * owner + later.astype(jnp.int32)
    other = jnp.where(held >= 0, held, TILES)
    arrival[other] = 2 * owner + 1 - later.astype(jnp.int32)
    first[owner] = t


def put_extras(codes, turned, message_ref, first, stride):
    row = iota((8, 128), 0)

    def body(m, carry):
        before, after = 2 * jnp.maximum(m - 1, 0), 2 * jnp.minimum(m + 1, PAIRS - 1)
        total = jnp.zeros((8, 128), F32)
        for r in range(2):
            east = turned[pl.ds(before + (64, 0)[r], 1), :]
            west = turned[pl.ds(after + (1, 65)[r], 1), :]
            total = jnp.where(row == codes[2 * m + r], east, total)
            total = jnp.where(row == codes[CODE_W + 2 * m + 2 + r], west, total)
        message_ref[pl.ds(pl.multiple_of(m * stride + first, 8), 8), :] = total
        return carry

    lax.fori_loop(0, PAIRS, body, 0, unroll=8)


def first_edges(
    ocean, source, u_hbm, z_hbm,
    message_ref, table, codes, arrival, pairs,
    u_ref, z_ref, acc_v, acc_z, turned, count, landed, sem_in,
):
    z_copy = pltpu.make_async_copy(z_hbm, z_ref, sem_in.at[0])
    u_copy = pltpu.make_async_copy(u_hbm, u_ref, sem_in.at[1])
    z_copy.start()
    u_copy.start()
    make_table(ocean, table, count)
    for i in (0, 1, CODE_W + 64, CODE_W + 65):
        codes[i] = NONE
    for i in range(PAIRS):
        landed[i] = -1
    z_copy.wait()

    def scalars(i, carry):
        for k in range(CHUNK):
            j = i * CHUNK + k
            z = load_field(z_ref, table, j, 0.0)
            pairs[j, 128:192, :] = z
            put_columns(acc_z, z, j)
            put_rows(message_ref, jnp.concatenate([z, z], axis=0), 32 * j + 8)
            column_codes(ocean, table, codes, j)
        return carry

    def vectors(i, carry):
        for k in range(CHUNK):
            j = i * CHUNK + k
            u, v = load_vector(u_ref, table, j)
            vector = jnp.concatenate([u, v], axis=0)
            pairs[j, 0:128, :] = vector
            put_columns(acc_v, vector, j)
            put_rows(message_ref, vector, 32 * j)
            land(source, arrival, landed, j)
        return carry

    lax.fori_loop(0, CHUNKS, scalars, 0)
    u_copy.wait()
    lax.fori_loop(0, CHUNKS, vectors, 0)
    columns_to_message(acc_v, turned, message_ref, 0, 32)
    put_extras(codes, turned, message_ref, 16, 32)
    acc_z[64:128, :] = acc_z[0:64, :]
    columns_to_message(acc_z, turned, message_ref, 8, 32)
    put_extras(codes, turned, message_ref, 24, 32)


def prepare(
    table, p_hbm, b_hbm, a_hbm, f_hbm,
    weight, b_ref, a_ref, f_ref,
    p_ref, natural, sem,
):
    copies = [
        pltpu.make_async_copy(source, target, sem.at[n])
        for n, (source, target) in enumerate(
            ((p_hbm, p_ref), (b_hbm, b_ref), (a_hbm, a_ref), (f_hbm, f_ref))
        )
    ]
    for copy in copies:
        copy.start()
    low = iota((32, 128), 1) < 64

    def lines(i, carry):
        for k in range(CHUNK):
            j = i * CHUNK + k
            tiles = []
            for r in range(2):
                s = table[2 * j + r]
                t = jnp.maximum(s, 0)
                x = p_ref[t // 8, pl.ds(t % 8, 32, stride=8), :]
                tiles.append(jnp.where(s >= 0, x, 0.0))
            t0, t1 = tiles
            crossed = roll(jnp.where(low, t1, t0), 64, 1)
            natural[k, pl.ds(0, 32, stride=2), :] = jnp.where(low, t0, 0.0)
            natural[k, pl.ds(1, 32, stride=2), :] = jnp.where(low, crossed, 0.0)
            natural[k, pl.ds(64, 32, stride=2), :] = jnp.where(low, 0.0, crossed)
            natural[k, pl.ds(65, 32, stride=2), :] = jnp.where(low, 0.0, t1)
            turned = natural[k].T
            high = turned.astype(BF16)
            weight[j, :, 0:128] = high
            weight[j, :, 128:256] = (turned - high.astype(F32)).astype(BF16)
        return carry

    copies[0].wait()
    lax.fori_loop(0, CHUNKS, lines, 0)
    for copy in copies[1:]:
        copy.wait()


def side_masks():
    x = iota((64, 128), 1) % 64
    return x == 0, x == 63


KX = (1.25, 0.25)
KY = (0.25, 1.25)


def first_step(
    table, codes, halo_ref, pairs, b_ref, a_ref, f_ref, weight,
    state, message_ref, edges_ref,
    acc_z, acc_r, hv, hz, turned,
):
    message_to_columns(halo_ref, turned, hv, 0, 16)
    message_to_columns(halo_ref, turned, hz, 8, 16)
    at_west, at_east = side_masks()

    def one(j):
        u0 = pairs[j, 0:64, :], pairs[j, 64:128, :]
        z = pairs[j, 128:192, :]
        b = load_vector(b_ref, table, j)
        a = load_field(a_ref, table, j, 1.0)
        f = load_field(f_ref, table, j, 0.0)
        side_v = get_columns(hv[...], j)
        side_z = get_columns(hz[0:64, :], j)
        rows = halo_ref[pl.ds(pl.multiple_of(16 * j, 16), 16), :]
        face_w = 0.5 * (z + jnp.where(at_west, side_z, roll(z, 1, 1)))
        face_e = 0.5 * (z + jnp.where(at_east, side_z, roll(z, 127, 1)))
        face_s = 0.5 * (z + south_of(z, rows[12:13]))
        face_n = 0.5 * (z + north_of(z, rows[13:14]))
        scale, diag = [], []
        for c in range(2):
            d = a + KX[c] * (face_w + face_e) + KY[c] * (face_s + face_n)
            diag.append(d)
            scale.append(lax.rsqrt(d))
        turn = f * scale[0] * scale[1]
        rhat, west, south, plain = [], [], [], []
        for c in range(2):
            x, s = u0[c], scale[c]
            side = side_v[64 * c : 64 * c + 64]
            x_w = jnp.where(at_west, side, roll(x, 1, 1))
            x_e = jnp.where(at_east, side, roll(x, 127, 1))
            x_s = south_of(x, rows[4 + 2 * c : 5 + 2 * c])
            x_n = north_of(x, rows[5 + 2 * c : 6 + 2 * c])
            spin = -f * u0[1] if c == 0 else f * u0[0]
            applied = (
                diag[c] * x + spin
                - KX[c] * (face_w * x_w + face_e * x_e)
                - KY[c] * (face_s * x_s + face_n * x_n)
            )
            residual = b[c] - applied
            plain.append(residual)
            rhat.append(s * residual)
            k_w = KX[c] * s * face_w
            k_s = KY[c] * s * face_s
            west.append(jnp.where(at_west, 0.0, k_w * roll(s, 1, 1)))
            south.append(k_s * south_of(s, jnp.zeros((1, 128), F32)))
        rhat = jnp.concatenate(rhat, axis=0)
        plain = jnp.concatenate(plain, axis=0)
        west = jnp.concatenate(west, axis=0)
        south = jnp.concatenate(south, axis=0)
        put_columns(acc_r, plain, j)
        put_rows(edges_ref, plain, 8 * j)
        state[j, 0:128, :] = west
        state[j, 128:256, :] = south
        state[j, 256:384, :] = jnp.concatenate(diag, axis=0)
        state[j, 384:512, :] = rhat
        state[j, 512:576, :] = turn
        y = relax(rhat, weight[j], west, south, turn)
        z0 = jnp.concatenate(scale, axis=0) * y
        state[j, 576:704, :] = z0
        put_columns(acc_z, z0, j)
        put_rows(message_ref, z0, 16 * j)

    def body(i, carry):
        for k in range(LONG):
            one(i * LONG + k)
        return carry

    lax.fori_loop(0, PAIRS // LONG, body, 0)
    columns_to_message(acc_r, turned, edges_ref, 0, 8)
    columns_to_message(acc_z, turned, message_ref, 0, 16)
    put_extras(codes, turned, message_ref, 8, 16)


def second_step(
    codes, halo_ref, state, weight,
    z1s, message_ref, sums_ref,
    acc_z, acc_p, acc_d, hv, turned,
):
    message_to_columns(halo_ref, turned, hv, 0, 16)
    lane = iota((128, 128), 1) % 64
    at_side = (lane == 0) | (lane == 63)
    first, last = iota((8, 128), 0) == 0, iota((8, 128), 0) == 7
    sums_ref[...] = jnp.zeros((6, 8, 128), F32)

    def one(j):
        west, south, turn = state[j, 0:128, :], state[j, 128:256, :], state[j, 512:576, :]
        diag = state[j, 256:384, :]
        rhat = state[j, 384:512, :]
        scale = lax.rsqrt(diag)
        root = diag * scale
        y0 = root * state[j, 576:704, :]
        what = tile_part(y0, west, south, turn)
        what = what - jnp.where(at_side, scale * get_columns(hv[...], j), 0.0)
        rows = halo_ref[pl.ds(pl.multiple_of(16 * j, 16), 8), :]
        fixed = []
        for c in range(2):
            part = what[64 * c : 64 * c + 64]
            s = scale[64 * c : 64 * c + 64]
            low = part[:8] - jnp.where(first, s[:8] * rows[4 + 2 * c : 5 + 2 * c], 0.0)
            high = part[56:] - jnp.where(last, s[56:] * rows[5 + 2 * c : 6 + 2 * c], 0.0)
            fixed += [low, part[8:56], high]
        what = jnp.concatenate(fixed, axis=0)
        dhat = what - rhat
        y1 = relax(dhat, weight[j], west, south, turn)
        phat = tile_part(y1, west, south, turn) - dhat
        z1 = scale * y1
        z1s[j] = z1
        r, d, p = root * rhat, root * dhat, root * phat
        for index, (left, right) in enumerate(((r, r), (r, d), (d, d), (r, p), (d, p), (p, p))):
            product = left * right
            total = product[0:8]
            for k in range(1, 16):
                total = total + product[8 * k : 8 * k + 8]
            sums_ref[index] += total
        for k, (acc, x) in enumerate(((acc_z, z1), (acc_p, p), (acc_d, d))):
            put_columns(acc, x, j)
            put_rows(message_ref, x, 32 * j + 8 * k)

    def body(i, carry):
        for k in range(LONG):
            one(i * LONG + k)
        return carry

    lax.fori_loop(0, PAIRS // LONG, body, 0)
    columns_to_message(acc_p, turned, message_ref, 8, 32)
    columns_to_message(acc_d, turned, message_ref, 16, 32)
    columns_to_message(acc_z, turned, message_ref, 0, 32)
    put_extras(codes, turned, message_ref, 24, 32)


def to_normal(x, r):
    row = iota((8, 128), 0)
    return jnp.where(r == 1, jnp.where(row < 4, roll(x, 6, 0), roll(x, 64, 1)), x)


def halo_of(west, east, south, north):
    row = iota((8, 128), 0)
    side = jnp.where(row == 0, roll(west, 7, 0), roll(east, 1, 0))
    end = jnp.where(row % 2 == 0, roll(south, 7, 0), roll(north, 1, 0))
    return jnp.where(row < 2, side, jnp.where(row >= 4, end, 0.0))


def tile_block(arrival, received_ref, t, k):
    at = arrival[t]
    return to_normal(received_ref[at // 2, 8 * k : 8 * k + 8, :], at % 2)


def boundary(arrival, received_ref, south_ref, north_ref):
    for k in range(south_ref.shape[1] // 8):
        rows = slice(8 * k, 8 * k + 8)
        for x in range(8):
            south_ref[x, rows, :] = tile_block(arrival, received_ref, x, k)
            north_ref[x, rows, :] = tile_block(arrival, received_ref, 24 + x, k)


def tile_halos(arrival, received_ref, from_south, from_north, k, extra):
    group = lax.axis_index("grp")
    blocks = [tile_block(arrival, received_ref, t, k) for t in range(TILES)]
    sides = received_ref[0, 8 * extra : 8 * extra + 8, :]
    for o in range(1, PAIRS):
        sides = sides + received_ref[o, 8 * extra : 8 * extra + 8, :]
    rows = slice(8 * k, 8 * k + 8)
    last = lax.axis_size("grp") - 1
    below = [jnp.where(group > 0, from_south[x, rows, :], 0.0) for x in range(8)]
    above = [jnp.where(group < last, from_north[x, rows, :], 0.0) for x in range(8)]
    halos = []
    for t in range(TILES):
        ty, tx = t // 8, t % 8
        halos.append(
            halo_of(
                blocks[t - 1] if tx > 0 else roll(sides, (1 - ty) % 8, 0),
                blocks[t + 1] if tx < 7 else roll(sides, 4 - ty, 0),
                blocks[t - 8] if ty > 0 else below[tx],
                blocks[t + 8] if ty < 3 else above[tx],
            )
        )
    return blocks, halos


def hand_back(arrival, t, k, halo, out_ref):
    at = arrival[t]
    r = at % 2
    row, lane = iota((8, 128), 0), iota((8, 128), 1)
    placed = jnp.where(r == 1, jnp.where(row < 4, roll(halo, 2, 0), roll(halo, 64, 1)), halo)
    mine = ((row < 4) & (row // 2 == r)) | ((row >= 4) & (lane // 64 == r))
    rows = slice(8 * k, 8 * k + 8)
    out_ref[at // 2, rows, :] += jnp.where(mine, placed, 0.0)


def first_return(arrival, received_ref, south, north, out_ref, face_ref):
    row, lane = iota((8, 128), 0), iota((8, 128), 1)
    along_x = jnp.where(lane < 64, KX[0], KX[1])
    along_y = jnp.where(row < 6, KY[0], KY[1])
    factor = 0.5 * jnp.where(row < 4, along_x, along_y)
    out_ref[...] = jnp.zeros(out_ref.shape, F32)
    for k in range(2):
        blocks, halos = tile_halos(arrival, received_ref, south, north, k, 2 + k)
        for t in range(TILES):
            hand_back(arrival, t, k, halos[t], out_ref)
            if k == 1:
                face_ref[t] = factor * (blocks[t] + halos[t])


def second_return(arrival, received_ref, south, north, edges_ref, face_ref, out_ref):
    out_ref[:, 0:8, :] = jnp.zeros((PAIRS, 8, 128), F32)
    out_ref[:, 8:16, :] = edges_ref[...]
    blocks, halos = tile_halos(arrival, received_ref, south, north, 0, 1)
    for t in range(TILES):
        hand_back(arrival, t, 0, face_ref[t] * halos[t], out_ref)


def edge_sums(arrival, received_ref, south, north, earlier_ref, face_ref, sums_ref, out_ref):
    row, lane = iota((8, 128), 0), iota((8, 128), 1)
    valid = (row < 2) | ((row >= 4) & (lane < 64))
    total_r = jnp.zeros((8, 128), F32)
    total_d = jnp.zeros((8, 128), F32)
    total_p = jnp.zeros((8, 128), F32)
    blocks, halos = tile_halos(arrival, received_ref, south, north, 0, 3)
    for t in range(TILES):
        h = jnp.where(valid, -face_ref[t] * halos[t], 0.0)
        p = tile_block(arrival, received_ref, t, 1)
        d = tile_block(arrival, received_ref, t, 2)
        r = tile_block(arrival, earlier_ref, t, 1)
        total_r = total_r + jnp.where(valid, h * r, 0.0)
        total_d = total_d + jnp.where(valid, h * d, 0.0)
        wide_w = jnp.broadcast_to(h[0:1], (8, 128))
        wide_e = jnp.broadcast_to(h[1:2], (8, 128))
        corner_w = jnp.where(
            row == 4, wide_w,
            jnp.where(row == 5, roll(wide_w, 65, 1), jnp.where(row == 6, roll(wide_w, 64, 1), roll(wide_w, 1, 1))),
        )
        corner_e = jnp.where(
            row == 4, roll(wide_e, 63, 1),
            jnp.where(row == 5, wide_e, jnp.where(row == 6, roll(wide_e, 127, 1), roll(wide_e, 64, 1))),
        )
        corner = jnp.where(lane == 0, corner_w, jnp.where(lane == 63, corner_e, 0.0))
        corner = jnp.where(row >= 4, corner, 0.0)
        total_p = total_p + jnp.where(valid, h * (2.0 * (p + corner) + h), 0.0)
    lane = iota((1, 128), 1)
    out = jnp.zeros((1, 128), F32)
    for index in range(6):
        total = sums_ref[index]
        if index == 3:
            total = total + total_r
        if index == 4:
            total = total + total_d
        if index == 5:
            total = total + total_p
        value = jnp.sum(jnp.sum(total, axis=0, keepdims=True), axis=1, keepdims=True)
        out = jnp.where(lane == index, value, out)
    out_ref[...] = jnp.broadcast_to(out, (128, 128))


def least_squares(magnitude, upper_first, below_first, upper_cross, upper_second, below_second):
    radius_first = jnp.sqrt(upper_first * upper_first + below_first * below_first)
    cosine_first = upper_first / radius_first
    sine_first = below_first / radius_first
    lifted_top = cosine_first * upper_cross + sine_first * upper_second
    lifted_low = cosine_first * upper_second - sine_first * upper_cross
    radius_second = jnp.sqrt(lifted_low * lifted_low + below_second * below_second)
    weight_second = -(sine_first * magnitude) * (lifted_low / radius_second) / radius_second
    weight_first = (cosine_first * magnitude - lifted_top * weight_second) / radius_first
    return (weight_first, weight_second)


def final_weights(gathered):
    total = jnp.sum(gathered, axis=0, keepdims=True)
    lane = iota((1, 128), 1)
    rr, rd, dd, re, de, ee = [
        jnp.sum(jnp.where(lane == index, total, 0.0), axis=1, keepdims=True) for index in range(6)
    ]
    square = rr + EPSILON
    magnitude = jnp.sqrt(square)
    h11 = (rr + rd) / square
    gap = -(rd - EPSILON) / square
    h21_square = jnp.maximum((dd + 2.0 * gap * rd + gap * gap * rr) / square, 0.0) + EPSILON
    h21 = jnp.sqrt(h21_square)
    unit = 1.0 / (magnitude * h21)
    h12 = (gap * rr + (1.0 + gap) * rd + re) * unit / magnitude
    h22 = (
        gap * (gap * rr + rd) + (1.0 + gap) * (gap * rd + dd) + (gap * re + de)
    ) * unit * unit
    c_r = gap * unit - h12 / magnitude - h22 * gap * unit
    c_d = (1.0 + gap - h22) * unit
    c_e = unit
    h32_square = (
        c_r * c_r * rr + c_d * c_d * dd + c_e * c_e * ee
        + 2.0 * (c_r * c_d * rd + c_r * c_e * re + c_d * c_e * de)
    )
    h32 = jnp.sqrt(jnp.maximum(h32_square, 0.0) + EPSILON)
    y1, y2 = least_squares(magnitude, h11, h21, h12, h22, h32)
    return y1 / magnitude + y2 * gap * unit, y2 * unit


def last_step(
    table, gathered_ref, pairs, state, z1,
    out_hbm,
    out, sem_out,
):
    out[...] = jnp.zeros(out.shape, F32)
    weight0, weight1 = final_weights(gathered_ref[...])

    def body(i, carry):
        for k in range(CHUNK):
            j = i * CHUNK + k
            new = pairs[j, 0:128, :] + weight0 * state[j, 576:704, :] + weight1 * z1[j]
            slots = [jnp.where(table[2 * j + r] >= 0, table[2 * j + r], SLOTS) for r in range(2)]
            for c in range(2):
                for r, x in enumerate(split_up(new[64 * c : 64 * c + 64])):
                    for q in range(4):
                        out[slots[r], pl.ds(c + 2 * q, 8, stride=8), :] = x[8 * q : 8 * q + 8]
        return carry

    lax.fori_loop(0, CHUNKS, body, 0)
    copy = pltpu.make_async_copy(out.at[pl.ds(0, SLOTS)], out_hbm, sem_out)
    copy.start()
    copy.wait()


def call(kernel, outs, specs, scratch=(), out_specs=None, mebibytes=4):
    return pl.pallas_call(
        kernel,
        out_shape=outs,
        in_specs=specs,
        out_specs=out_specs if out_specs is not None else jax.tree.map(lambda _: vmem(), outs),
        scratch_shapes=list(scratch),
        compiler_params=params(mebibytes),
    )


def hbm():
    return pl.BlockSpec(memory_space=pl.ANY)


def square(rows=128):
    return pltpu.VMEM((rows, 128), F32)


def buffer(*shape, dtype=F32):
    return pltpu.VMEM(shape, dtype)


def sems(*shape):
    return pltpu.SemaphoreType.DMA(shape)


def vector_view(x):
    return x.reshape(64, 2, 32, 128).transpose(0, 2, 1, 3).reshape(64, 64, 128)


def field_view(x):
    return x.reshape(8, 8, 32, 128).transpose(0, 2, 1, 3).reshape(8, 256, 128)


def exchange(x):
    return lax.all_to_all(x, "dev", split_axis=0, concat_axis=0, tiled=True)


def boundaries(arrival, received, count):
    side = struct(8, 8 * count, 128)
    return call(boundary, (side, side), [smem(), vmem()])(arrival, received)


def from_groups(south, north):
    size = lax.axis_size("grp")
    ahead = [(i, (i + 1) % size) for i in range(size)]
    return lax.ppermute(north, "grp", ahead), lax.ppermute(south, "grp", [(j, i) for i, j in ahead])


def shards(velocity, forcing, mass, coriolis, viscosity, lines, tile_source_slot, ocean_tile):
    u, b = vector_view(velocity), vector_view(forcing)
    a, f, z, p = [field_view(x) for x in (mass, coriolis, viscosity, lines)]

    message, table, codes, arrival, pairs = call(
        first_edges,
        (
            struct(PAIRS * 32, 128), struct(TABLE, dtype=jnp.int32), struct(CODES, dtype=jnp.int32),
            struct(TILES + 8, dtype=jnp.int32), resident(PAIRS, 192, 128),
        ),
        [smem(), smem(), hbm(), hbm()],
        [
            buffer(64, 64, 128), buffer(8, 256, 128), square(), square(), square(),
            pltpu.SMEM((PAIRS + 8,), jnp.int32), pltpu.SMEM((PAIRS,), jnp.int32), sems(2),
        ],
        (vmem(), smem(), smem(), smem(), vmem()),
        8,
    )(kept(ocean_tile), kept(tile_source_slot), kept(u), kept(z))

    received = exchange(message.reshape(PAIRS, 32, 128))
    south, north = boundaries(arrival, received, 2)
    south, north, later = lax.optimization_barrier((south, north, table))
    weight, b, a, f = call(
        prepare,
        (
            resident(PAIRS, 128, 256, dtype=BF16), resident(64, 64, 128),
            resident(8, 256, 128), resident(8, 256, 128),
        ),
        [smem()] + [hbm()] * 4,
        [buffer(8, 256, 128), buffer(CHUNK, 128, 128), sems(4)],
        [vmem()] * 4,
        4,
    )(later, kept(p), kept(b), kept(a), kept(f))
    halo, face = call(
        first_return, (struct(PAIRS, 16, 128), struct(TILES, 8, 128)), [smem()] + [vmem()] * 3
    )(arrival, received, *from_groups(south, north))
    halo, weight, b, a, f = lax.optimization_barrier((halo, weight, b, a, f))
    halo = exchange(halo).reshape(PAIRS * 16, 128)

    state, message, edges = call(
        first_step,
        (resident(PAIRS, STATE, 128), struct(PAIRS * 16, 128), struct(PAIRS * 8, 128)),
        [smem()] * 2 + [vmem()] * 6,
        [square()] * 5,
        mebibytes=8,
    )(table, codes, halo, held(pairs), held(b), held(a), held(f), held(weight))
    received = exchange(message.reshape(PAIRS, 16, 128))
    halo = call(second_return, struct(PAIRS, 16, 128), [smem()] + [vmem()] * 5)(
        arrival, received, *from_groups(*boundaries(arrival, received, 1)), edges.reshape(PAIRS, 8, 128), face
    )
    earlier = exchange(halo)
    halo = earlier.reshape(PAIRS * 16, 128)

    z1, message, sums = call(
        second_step,
        (resident(PAIRS, 128, 128), struct(PAIRS * 32, 128), struct(6, 8, 128)),
        [smem()] + [vmem()] * 3,
        [square()] * 5,
        mebibytes=8,
    )(codes, halo, held(state), held(weight))
    received = exchange(message.reshape(PAIRS, 32, 128))
    partial = call(edge_sums, struct(128, 128), [smem()] + [vmem()] * 6)(
        arrival, received, *from_groups(*boundaries(arrival, received, 1)), earlier, face, sums
    )
    gathered = lax.all_to_all(partial, ("grp", "dev"), split_axis=0, concat_axis=0, tiled=True)

    out = call(
        last_step, struct(SLOTS, 64, 128), [smem()] + [vmem()] * 4,
        [buffer(SLOTS + 1, 64, 128), pltpu.SemaphoreType.DMA],
        hbm(),
        8,
    )(table, gathered, held(pairs), held(state), held(z1))
    return out.reshape(64, 32, 2, 128).transpose(0, 2, 1, 3).reshape(64, 2, 4096)


def solution(mesh):
    return jax.shard_map(
        shards,
        mesh=mesh,
        in_specs=(
            P(("grp", "dev"), None, None),
            P(("grp", "dev"), None, None),
            P(("grp", "dev"), None),
            P(("grp", "dev"), None),
            P(("grp", "dev"), None),
            P(("grp", "dev"), None),
            P(("grp", "dev")),
            P(("grp", "dev")),
        ),
        out_specs=P(("grp", "dev"), None, None),
        check_vma=False,
    )
```

```python
import jax
import jax.numpy as jnp
from jax import lax
from jax.experimental import pallas as pl
from jax.experimental.pallas import tpu as pltpu
from jax.sharding import PartitionSpec as P

F32 = jnp.float32
BF16 = jnp.bfloat16
SLOTS = 64
PAIRS = 32
TILES = 32
CHUNK = 8
LONG = 32
CHUNKS = PAIRS // CHUNK
TABLE = 72
CODES = 144
STATE = 704
EPSILON = 1e-06


def params(mebibytes):
    return pltpu.CompilerParams(vmem_limit_bytes=mebibytes * 1024 * 1024)


def vmem():
    return pl.BlockSpec(memory_space=pltpu.VMEM)


def smem():
    return pl.BlockSpec(memory_space=pltpu.SMEM)


def struct(*shape, dtype=F32):
    return jax.ShapeDtypeStruct(shape, dtype)


def resident(*shape, dtype=F32):
    return pltpu.VMEM(shape, dtype)


def held(x):
    return pltpu.with_memory_space_constraint(x, pltpu.VMEM)


def kept(x):
    return pltpu.with_memory_space_constraint(x, pltpu.HBM)


def iota(shape, dim):
    return lax.broadcasted_iota(jnp.int32, shape, dim)


def roll(x, shift, axis):
    return pltpu.roll(x, shift, axis)


def pair_up(t0, t1):
    low = iota(t0.shape, 1) < 64
    crossed = roll(jnp.where(low, t1, t0), 64, 1)
    return jnp.concatenate([jnp.where(low, t0, crossed), jnp.where(low, crossed, t1)], axis=0)


def split_up(q):
    even, odd = q[:32], q[32:]
    low = iota(even.shape, 1) < 64
    crossed = roll(jnp.where(low, odd, even), 64, 1)
    return jnp.where(low, even, crossed), jnp.where(low, crossed, odd)


def load_tile(ref, index, offset, step):
    rows = [ref[index, pl.ds(offset + step * q, 8, stride=4 * step), :] for q in range(4)]
    return jnp.concatenate(rows, axis=0)


def load_field(ref, table, j, empty):
    tiles = []
    for r in range(2):
        s = table[2 * j + r]
        t = jnp.maximum(s, 0)
        tiles.append(jnp.where(s >= 0, load_tile(ref, t // 8, t % 8, 8), empty))
    return pair_up(*tiles)


def load_vector(ref, table, j):
    parts = []
    for c in range(2):
        tiles = []
        for r in range(2):
            s = table[2 * j + r]
            tiles.append(jnp.where(s >= 0, load_tile(ref, jnp.maximum(s, 0), c, 2), 0.0))
        parts.append(pair_up(*tiles))
    return parts


def put_columns(acc_ref, x, j):
    mine = ((iota(x.shape, 1) % 64) // 2) == j
    pltpu.store(acc_ref.at[pl.ds(0, x.shape[0])], roll(x, 2 * j + 1, 1), mask=mine)


def get_columns(acc, j):
    return roll(acc, 128 - (2 * j + 1), 1)


COLUMN_ROWS = (1, 64, 65, 0)


def columns_to_message(acc_ref, turned_ref, message_ref, first, stride):
    turned_ref[...] = acc_ref[...].T
    for row, source in enumerate(COLUMN_ROWS):
        message_ref[pl.ds(first + row, 32, stride=stride), :] = turned_ref[pl.ds(source, 32, stride=2), :]


def message_to_columns(message_ref, turned_ref, acc_ref, first, stride):
    for row, source in enumerate(COLUMN_ROWS):
        turned_ref[pl.ds(source, 32, stride=2), :] = message_ref[pl.ds(first + row, 32, stride=stride), :]
    acc_ref[...] = turned_ref[...].T


def put_rows(message_ref, x, base):
    for row, source in enumerate((0, 63, 64, 127)):
        message_ref[pl.ds(base + 4 + row, 1), :] = x[source : source + 1, :]


def south_of(x, halo=None):
    even, odd = x[:32], x[32:]
    below = roll(odd[24:], 1, 0)
    if halo is not None:
        below = jnp.where(iota(below.shape, 0) == 0, halo, below)
    return jnp.concatenate([below, odd[:24], even], axis=0)


def north_of(x, halo=None):
    even, odd = x[:32], x[32:]
    above = roll(even[:8], 7, 0)
    if halo is not None:
        above = jnp.where(iota(above.shape, 0) == 7, halo, above)
    return jnp.concatenate([odd, even[8:], above], axis=0)


def tile_part(y, west, south, turn):
    parts = []
    for c in range(2):
        rows = slice(64 * c, 64 * c + 64)
        x, w, s = y[rows], west[rows], south[rows]
        even, odd = x[:32], x[32:]
        s_even, s_odd = s[:32], s[32:]
        across = w * roll(x, 1, 1) + roll(w * x, 127, 1)
        up = s_even * even
        along = jnp.concatenate(
            [
                s_even[:8] * roll(odd[24:], 1, 0) + s_odd[:8] * odd[:8],
                s_even[8:] * odd[:24] + s_odd[8:] * odd[8:],
                s_odd[:24] * even[:24] + up[8:],
                s_odd[24:] * even[24:] + roll(up[:8], 7, 0),
            ],
            axis=0,
        )
        other = y[64:] if c == 0 else y[:64]
        spin = turn * other
        parts.append(x - across - along - spin if c == 0 else x - across - along + spin)
    return jnp.concatenate(parts, axis=0)


def line_solve(t, weight):
    high = t.astype(BF16)
    low = (t - high.astype(F32)).astype(BF16)
    out = lax.dot_general(
        jnp.concatenate([high, low], axis=1),
        jnp.concatenate([weight, weight], axis=0),
        (((1,), (0,)), ((), ())),
        preferred_element_type=F32,
    )
    return out[:, :128] + out[:, 128:]


def relax(q, weight, west, south, turn):
    y = line_solve(q, weight)
    for _ in range(2):
        y = y + line_solve(q - tile_part(y, west, south, turn), weight)
    return y


NONE = 99
CODE_W = 72


def make_table(ocean, table, count):
    def clear(i, carry):
        table[i] = -1
        return carry

    def clear_count(i, carry):
        count[i] = 0
        return carry

    def place(s, carry):
        t = ocean[s]
        j = jnp.where(t >= 0, (t >> 5) & 31, PAIRS)
        held = count[j] & 1
        table[2 * j + held] = s
        count[j] = held + 1
        return carry

    lax.fori_loop(0, TABLE, clear, 0, unroll=8)
    lax.fori_loop(0, PAIRS + 8, clear_count, 0, unroll=8)
    lax.fori_loop(0, SLOTS, place, 0, unroll=8)


def column_codes(ocean, table, codes, j):
    for r in range(2):
        p = 2 * j + r
        s = table[p]
        t = ocean[jnp.maximum(s, 0)]
        column, row = t & 7, (t >> 3) & 3
        codes[p + 2] = jnp.where((s >= 0) & (column == 7), row, NONE)
        codes[CODE_W + p] = jnp.where((s >= 0) & (column == 0), row + 4, NONE)


def land(source, arrival, first, t):
    slot = source[t]
    owner = (slot >> 6) & 31
    held = first[owner]
    later = (held >= 0) & (source[jnp.maximum(held, 0)] < slot)
    arrival[t] = 2 * owner + later.astype(jnp.int32)
    other = jnp.where(held >= 0, held, TILES)
    arrival[other] = 2 * owner + 1 - later.astype(jnp.int32)
    first[owner] = t


def put_extras(codes, turned, message_ref, first, stride):
    row = iota((8, 128), 0)

    def body(m, carry):
        before, after = 2 * jnp.maximum(m - 1, 0), 2 * jnp.minimum(m + 1, PAIRS - 1)
        total = jnp.zeros((8, 128), F32)
        for r in range(2):
            east = turned[pl.ds(before + (64, 0)[r], 1), :]
            west = turned[pl.ds(after + (1, 65)[r], 1), :]
            total = jnp.where(row == codes[2 * m + r], east, total)
            total = jnp.where(row == codes[CODE_W + 2 * m + 2 + r], west, total)
        message_ref[pl.ds(pl.multiple_of(m * stride + first, 8), 8), :] = total
        return carry

    lax.fori_loop(0, PAIRS, body, 0, unroll=8)


def first_edges(
    ocean, source, u_hbm, z_hbm,
    message_ref, table, codes, arrival, pairs,
    u_ref, z_ref, acc_v, acc_z, turned, count, landed, sem_in,
):
    z_copy = pltpu.make_async_copy(z_hbm, z_ref, sem_in.at[0])
    u_copy = pltpu.make_async_copy(u_hbm, u_ref, sem_in.at[1])
    z_copy.start()
    u_copy.start()
    make_table(ocean, table, count)
    for i in (0, 1, CODE_W + 64, CODE_W + 65):
        codes[i] = NONE
    for i in range(PAIRS):
        landed[i] = -1
    z_copy.wait()

    def scalars(i, carry):
        for k in range(CHUNK):
            j = i * CHUNK + k
            z = load_field(z_ref, table, j, 0.0)
            pairs[j, 128:192, :] = z
            put_columns(acc_z, z, j)
            put_rows(message_ref, jnp.concatenate([z, z], axis=0), 32 * j + 8)
            column_codes(ocean, table, codes, j)
        return carry

    def vectors(i, carry):
        for k in range(CHUNK):
            j = i * CHUNK + k
            u, v = load_vector(u_ref, table, j)
            vector = jnp.concatenate([u, v], axis=0)
            pairs[j, 0:128, :] = vector
            put_columns(acc_v, vector, j)
            put_rows(message_ref, vector, 32 * j)
            land(source, arrival, landed, j)
        return carry

    lax.fori_loop(0, CHUNKS, scalars, 0)
    u_copy.wait()
    lax.fori_loop(0, CHUNKS, vectors, 0)
    columns_to_message(acc_v, turned, message_ref, 0, 32)
    put_extras(codes, turned, message_ref, 16, 32)
    acc_z[64:128, :] = acc_z[0:64, :]
    columns_to_message(acc_z, turned, message_ref, 8, 32)
    put_extras(codes, turned, message_ref, 24, 32)


def prepare(
    table, p_hbm, b_hbm, a_hbm, f_hbm,
    weight, b_ref, a_ref, f_ref,
    p_ref, natural, sem,
):
    copies = [
        pltpu.make_async_copy(source, target, sem.at[n])
        for n, (source, target) in enumerate(
            ((p_hbm, p_ref), (b_hbm, b_ref), (a_hbm, a_ref), (f_hbm, f_ref))
        )
    ]
    for copy in copies:
        copy.start()
    low = iota((32, 128), 1) < 64

    def lines(i, carry):
        for k in range(CHUNK):
            j = i * CHUNK + k
            tiles = []
            for r in range(2):
                s = table[2 * j + r]
                t = jnp.maximum(s, 0)
                x = p_ref[t // 8, pl.ds(t % 8, 32, stride=8), :]
                tiles.append(jnp.where(s >= 0, x, 0.0))
            t0, t1 = tiles
            crossed = roll(jnp.where(low, t1, t0), 64, 1)
            natural[k, pl.ds(0, 32, stride=2), :] = jnp.where(low, t0, 0.0)
            natural[k, pl.ds(1, 32, stride=2), :] = jnp.where(low, crossed, 0.0)
            natural[k, pl.ds(64, 32, stride=2), :] = jnp.where(low, 0.0, crossed)
            natural[k, pl.ds(65, 32, stride=2), :] = jnp.where(low, 0.0, t1)
            turned = natural[k].T
            high = turned.astype(BF16)
            weight[j, :, 0:128] = high
            weight[j, :, 128:256] = (turned - high.astype(F32)).astype(BF16)
        return carry

    copies[0].wait()
    lax.fori_loop(0, CHUNKS, lines, 0)
    for copy in copies[1:]:
        copy.wait()


def side_masks():
    x = iota((64, 128), 1) % 64
    return x == 0, x == 63


KX = (1.25, 0.25)
KY = (0.25, 1.25)


def first_step(
    table, codes, halo_ref, pairs, b_ref, a_ref, f_ref, weight,
    state, message_ref, edges_ref,
    acc_z, acc_r, hv, hz, turned,
):
    message_to_columns(halo_ref, turned, hv, 0, 16)
    message_to_columns(halo_ref, turned, hz, 8, 16)
    at_west, at_east = side_masks()

    def one(j):
        u0 = pairs[j, 0:64, :], pairs[j, 64:128, :]
        z = pairs[j, 128:192, :]
        b = load_vector(b_ref, table, j)
        a = load_field(a_ref, table, j, 1.0)
        f = load_field(f_ref, table, j, 0.0)
        side_v = get_columns(hv[...], j)
        side_z = get_columns(hz[0:64, :], j)
        rows = halo_ref[pl.ds(pl.multiple_of(16 * j, 16), 16), :]
        face_w = 0.5 * (z + jnp.where(at_west, side_z, roll(z, 1, 1)))
        face_e = 0.5 * (z + jnp.where(at_east, side_z, roll(z, 127, 1)))
        face_s = 0.5 * (z + south_of(z, rows[12:13]))
        face_n = 0.5 * (z + north_of(z, rows[13:14]))
        scale, diag = [], []
        for c in range(2):
            d = a + KX[c] * (face_w + face_e) + KY[c] * (face_s + face_n)
            diag.append(d)
            scale.append(lax.rsqrt(d))
        turn = f * scale[0] * scale[1]
        rhat, west, south, plain = [], [], [], []
        for c in range(2):
            x, s = u0[c], scale[c]
            side = side_v[64 * c : 64 * c + 64]
            x_w = jnp.where(at_west, side, roll(x, 1, 1))
            x_e = jnp.where(at_east, side, roll(x, 127, 1))
            x_s = south_of(x, rows[4 + 2 * c : 5 + 2 * c])
            x_n = north_of(x, rows[5 + 2 * c : 6 + 2 * c])
            spin = -f * u0[1] if c == 0 else f * u0[0]
            applied = (
                diag[c] * x + spin
                - KX[c] * (face_w * x_w + face_e * x_e)
                - KY[c] * (face_s * x_s + face_n * x_n)
            )
            residual = b[c] - applied
            plain.append(residual)
            rhat.append(s * residual)
            k_w = KX[c] * s * face_w
            k_s = KY[c] * s * face_s
            west.append(jnp.where(at_west, 0.0, k_w * roll(s, 1, 1)))
            south.append(k_s * south_of(s, jnp.zeros((1, 128), F32)))
        rhat = jnp.concatenate(rhat, axis=0)
        plain = jnp.concatenate(plain, axis=0)
        west = jnp.concatenate(west, axis=0)
        south = jnp.concatenate(south, axis=0)
        put_columns(acc_r, plain, j)
        put_rows(edges_ref, plain, 8 * j)
        state[j, 0:128, :] = west
        state[j, 128:256, :] = south
        state[j, 256:384, :] = jnp.concatenate(diag, axis=0)
        state[j, 384:512, :] = rhat
        state[j, 512:576, :] = turn
        y = relax(rhat, weight[j], west, south, turn)
        z0 = jnp.concatenate(scale, axis=0) * y
        state[j, 576:704, :] = z0
        put_columns(acc_z, z0, j)
        put_rows(message_ref, z0, 16 * j)

    def body(i, carry):
        for k in range(LONG):
            one(i * LONG + k)
        return carry

    lax.fori_loop(0, PAIRS // LONG, body, 0)
    columns_to_message(acc_r, turned, edges_ref, 0, 8)
    columns_to_message(acc_z, turned, message_ref, 0, 16)
    put_extras(codes, turned, message_ref, 8, 16)


def local_part(state, local):
    def body(i, carry):
        for k in range(CHUNK):
            j = i * CHUNK + k
            diag = state[j, 256:384, :]
            y0 = diag * lax.rsqrt(diag) * state[j, 576:704, :]
            value = tile_part(y0, state[j, 0:128, :], state[j, 128:256, :], state[j, 512:576, :])
            local[j] = value - state[j, 384:512, :]
        return carry

    lax.fori_loop(0, CHUNKS, body, 0)


def owner_sums(state, d_ref, p_ref, sums_ref):
    def body(i, carry):
        totals = [jnp.zeros((8, 128), F32) for _ in range(6)]
        for k in range(CHUNK):
            j = i * CHUNK + k
            diag = state[j, 256:384, :]
            r = diag * lax.rsqrt(diag) * state[j, 384:512, :]
            d, p = d_ref[j], p_ref[j]
            for index, (left, right) in enumerate(((r, r), (r, d), (d, d), (r, p), (d, p), (p, p))):
                product = left * right
                for n in range(16):
                    totals[index] = totals[index] + product[8 * n : 8 * n + 8]
        for index in range(6):
            sums_ref[index] += totals[index]
        return carry

    sums_ref[...] = jnp.zeros((6, 8, 128), F32)
    lax.fori_loop(0, CHUNKS, body, 0)


def second_step(
    codes, halo_ref, state, local, weight,
    z1s, d_ref, p_ref, message_ref,
    acc_z, acc_p, acc_d, hv, turned,
):
    message_to_columns(halo_ref, turned, hv, 0, 16)
    lane = iota((128, 128), 1) % 64
    at_side = (lane == 0) | (lane == 63)
    first, last = iota((8, 128), 0) == 0, iota((8, 128), 0) == 7

    def one(j):
        west, south, turn = state[j, 0:128, :], state[j, 128:256, :], state[j, 512:576, :]
        diag = state[j, 256:384, :]
        scale = lax.rsqrt(diag)
        root = diag * scale
        what = local[j] - jnp.where(at_side, scale * get_columns(hv[...], j), 0.0)
        rows = halo_ref[pl.ds(pl.multiple_of(16 * j, 16), 8), :]
        fixed = []
        for c in range(2):
            part = what[64 * c : 64 * c + 64]
            s = scale[64 * c : 64 * c + 64]
            low = part[:8] - jnp.where(first, s[:8] * rows[4 + 2 * c : 5 + 2 * c], 0.0)
            high = part[56:] - jnp.where(last, s[56:] * rows[5 + 2 * c : 6 + 2 * c], 0.0)
            fixed += [low, part[8:56], high]
        dhat = jnp.concatenate(fixed, axis=0)
        y1 = relax(dhat, weight[j], west, south, turn)
        phat = tile_part(y1, west, south, turn) - dhat
        z1 = scale * y1
        z1s[j] = z1
        d, p = root * dhat, root * phat
        d_ref[j] = d
        p_ref[j] = p
        for k, (acc, x) in enumerate(((acc_z, z1), (acc_p, p), (acc_d, d))):
            put_columns(acc, x, j)
            put_rows(message_ref, x, 32 * j + 8 * k)

    def body(i, carry):
        for k in range(LONG):
            one(i * LONG + k)
        return carry

    lax.fori_loop(0, PAIRS // LONG, body, 0)
    columns_to_message(acc_p, turned, message_ref, 8, 32)
    columns_to_message(acc_d, turned, message_ref, 16, 32)
    columns_to_message(acc_z, turned, message_ref, 0, 32)
    put_extras(codes, turned, message_ref, 24, 32)


def to_normal(x, r):
    row = iota((8, 128), 0)
    return jnp.where(r == 1, jnp.where(row < 4, roll(x, 6, 0), roll(x, 64, 1)), x)


def halo_of(west, east, south, north):
    row = iota((8, 128), 0)
    side = jnp.where(row == 0, roll(west, 7, 0), roll(east, 1, 0))
    end = jnp.where(row % 2 == 0, roll(south, 7, 0), roll(north, 1, 0))
    return jnp.where(row < 2, side, jnp.where(row >= 4, end, 0.0))


def tile_block(arrival, received_ref, t, k):
    at = arrival[t]
    return to_normal(received_ref[at // 2, 8 * k : 8 * k + 8, :], at % 2)


def boundary(arrival, received_ref, south_ref, north_ref):
    for k in range(south_ref.shape[1] // 8):
        rows = slice(8 * k, 8 * k + 8)
        for x in range(8):
            south_ref[x, rows, :] = tile_block(arrival, received_ref, x, k)
            north_ref[x, rows, :] = tile_block(arrival, received_ref, 24 + x, k)


def tile_halos(arrival, received_ref, from_south, from_north, k, extra):
    group = lax.axis_index("grp")
    blocks = [tile_block(arrival, received_ref, t, k) for t in range(TILES)]
    sides = received_ref[0, 8 * extra : 8 * extra + 8, :]
    for o in range(1, PAIRS):
        sides = sides + received_ref[o, 8 * extra : 8 * extra + 8, :]
    rows = slice(8 * k, 8 * k + 8)
    last = lax.axis_size("grp") - 1
    below = [jnp.where(group > 0, from_south[x, rows, :], 0.0) for x in range(8)]
    above = [jnp.where(group < last, from_north[x, rows, :], 0.0) for x in range(8)]
    halos = []
    for t in range(TILES):
        ty, tx = t // 8, t % 8
        halos.append(
            halo_of(
                blocks[t - 1] if tx > 0 else roll(sides, (1 - ty) % 8, 0),
                blocks[t + 1] if tx < 7 else roll(sides, 4 - ty, 0),
                blocks[t - 8] if ty > 0 else below[tx],
                blocks[t + 8] if ty < 3 else above[tx],
            )
        )
    return blocks, halos


def hand_back(arrival, t, k, halo, out_ref):
    at = arrival[t]
    r = at % 2
    row, lane = iota((8, 128), 0), iota((8, 128), 1)
    placed = jnp.where(r == 1, jnp.where(row < 4, roll(halo, 2, 0), roll(halo, 64, 1)), halo)
    mine = ((row < 4) & (row // 2 == r)) | ((row >= 4) & (lane // 64 == r))
    rows = slice(8 * k, 8 * k + 8)
    out_ref[at // 2, rows, :] += jnp.where(mine, placed, 0.0)


def first_return(arrival, received_ref, south, north, out_ref, face_ref):
    row, lane = iota((8, 128), 0), iota((8, 128), 1)
    along_x = jnp.where(lane < 64, KX[0], KX[1])
    along_y = jnp.where(row < 6, KY[0], KY[1])
    factor = 0.5 * jnp.where(row < 4, along_x, along_y)
    out_ref[...] = jnp.zeros(out_ref.shape, F32)
    for k in range(2):
        blocks, halos = tile_halos(arrival, received_ref, south, north, k, 2 + k)
        for t in range(TILES):
            hand_back(arrival, t, k, halos[t], out_ref)
            if k == 1:
                face_ref[t] = factor * (blocks[t] + halos[t])


def second_return(arrival, received_ref, south, north, edges_ref, face_ref, out_ref):
    out_ref[:, 0:8, :] = jnp.zeros((PAIRS, 8, 128), F32)
    out_ref[:, 8:16, :] = edges_ref[...]
    blocks, halos = tile_halos(arrival, received_ref, south, north, 0, 1)
    for t in range(TILES):
        hand_back(arrival, t, 0, face_ref[t] * halos[t], out_ref)


def edge_sums(arrival, received_ref, south, north, earlier_ref, face_ref, sums_ref, out_ref):
    row, lane = iota((8, 128), 0), iota((8, 128), 1)
    valid = (row < 2) | ((row >= 4) & (lane < 64))
    total_r = jnp.zeros((8, 128), F32)
    total_d = jnp.zeros((8, 128), F32)
    total_p = jnp.zeros((8, 128), F32)
    blocks, halos = tile_halos(arrival, received_ref, south, north, 0, 3)
    for t in range(TILES):
        h = jnp.where(valid, -face_ref[t] * halos[t], 0.0)
        p = tile_block(arrival, received_ref, t, 1)
        d = tile_block(arrival, received_ref, t, 2)
        r = tile_block(arrival, earlier_ref, t, 1)
        total_r = total_r + jnp.where(valid, h * r, 0.0)
        total_d = total_d + jnp.where(valid, h * d, 0.0)
        wide_w = jnp.broadcast_to(h[0:1], (8, 128))
        wide_e = jnp.broadcast_to(h[1:2], (8, 128))
        corner_w = jnp.where(
            row == 4, wide_w,
            jnp.where(row == 5, roll(wide_w, 65, 1), jnp.where(row == 6, roll(wide_w, 64, 1), roll(wide_w, 1, 1))),
        )
        corner_e = jnp.where(
            row == 4, roll(wide_e, 63, 1),
            jnp.where(row == 5, wide_e, jnp.where(row == 6, roll(wide_e, 127, 1), roll(wide_e, 64, 1))),
        )
        corner = jnp.where(lane == 0, corner_w, jnp.where(lane == 63, corner_e, 0.0))
        corner = jnp.where(row >= 4, corner, 0.0)
        total_p = total_p + jnp.where(valid, h * (2.0 * (p + corner) + h), 0.0)
    lane = iota((1, 128), 1)
    out = jnp.zeros((1, 128), F32)
    for index in range(6):
        total = sums_ref[index]
        if index == 3:
            total = total + total_r
        if index == 4:
            total = total + total_d
        if index == 5:
            total = total + total_p
        value = jnp.sum(jnp.sum(total, axis=0, keepdims=True), axis=1, keepdims=True)
        out = jnp.where(lane == index, value, out)
    out_ref[...] = jnp.broadcast_to(out, (128, 128))


def least_squares(magnitude, upper_first, below_first, upper_cross, upper_second, below_second):
    radius_first = jnp.sqrt(upper_first * upper_first + below_first * below_first)
    cosine_first = upper_first / radius_first
    sine_first = below_first / radius_first
    lifted_top = cosine_first * upper_cross + sine_first * upper_second
    lifted_low = cosine_first * upper_second - sine_first * upper_cross
    radius_second = jnp.sqrt(lifted_low * lifted_low + below_second * below_second)
    weight_second = -(sine_first * magnitude) * (lifted_low / radius_second) / radius_second
    weight_first = (cosine_first * magnitude - lifted_top * weight_second) / radius_first
    return (weight_first, weight_second)


def final_weights(gathered):
    total = jnp.sum(gathered, axis=0, keepdims=True)
    lane = iota((1, 128), 1)
    rr, rd, dd, re, de, ee = [
        jnp.sum(jnp.where(lane == index, total, 0.0), axis=1, keepdims=True) for index in range(6)
    ]
    square = rr + EPSILON
    magnitude = jnp.sqrt(square)
    h11 = (rr + rd) / square
    gap = -(rd - EPSILON) / square
    h21_square = jnp.maximum((dd + 2.0 * gap * rd + gap * gap * rr) / square, 0.0) + EPSILON
    h21 = jnp.sqrt(h21_square)
    unit = 1.0 / (magnitude * h21)
    h12 = (gap * rr + (1.0 + gap) * rd + re) * unit / magnitude
    h22 = (
        gap * (gap * rr + rd) + (1.0 + gap) * (gap * rd + dd) + (gap * re + de)
    ) * unit * unit
    c_r = gap * unit - h12 / magnitude - h22 * gap * unit
    c_d = (1.0 + gap - h22) * unit
    c_e = unit
    h32_square = (
        c_r * c_r * rr + c_d * c_d * dd + c_e * c_e * ee
        + 2.0 * (c_r * c_d * rd + c_r * c_e * re + c_d * c_e * de)
    )
    h32 = jnp.sqrt(jnp.maximum(h32_square, 0.0) + EPSILON)
    y1, y2 = least_squares(magnitude, h11, h21, h12, h22, h32)
    return y1 / magnitude + y2 * gap * unit, y2 * unit


def last_step(
    table, gathered_ref, pairs, state, z1,
    out_hbm,
    out, sem_out,
):
    out[...] = jnp.zeros(out.shape, F32)
    weight0, weight1 = final_weights(gathered_ref[...])

    def body(i, carry):
        for k in range(CHUNK):
            j = i * CHUNK + k
            new = pairs[j, 0:128, :] + weight0 * state[j, 576:704, :] + weight1 * z1[j]
            slots = [jnp.where(table[2 * j + r] >= 0, table[2 * j + r], SLOTS) for r in range(2)]
            for c in range(2):
                for r, x in enumerate(split_up(new[64 * c : 64 * c + 64])):
                    for q in range(4):
                        out[slots[r], pl.ds(c + 2 * q, 8, stride=8), :] = x[8 * q : 8 * q + 8]
        return carry

    lax.fori_loop(0, CHUNKS, body, 0)
    copy = pltpu.make_async_copy(out.at[pl.ds(0, SLOTS)], out_hbm, sem_out)
    copy.start()
    copy.wait()


def call(kernel, outs, specs, scratch=(), out_specs=None, mebibytes=4):
    return pl.pallas_call(
        kernel,
        out_shape=outs,
        in_specs=specs,
        out_specs=out_specs if out_specs is not None else jax.tree.map(lambda _: vmem(), outs),
        scratch_shapes=list(scratch),
        compiler_params=params(mebibytes),
    )


def hbm():
    return pl.BlockSpec(memory_space=pl.ANY)


def square(rows=128):
    return pltpu.VMEM((rows, 128), F32)


def buffer(*shape, dtype=F32):
    return pltpu.VMEM(shape, dtype)


def sems(*shape):
    return pltpu.SemaphoreType.DMA(shape)


def vector_view(x):
    return x.reshape(64, 2, 32, 128).transpose(0, 2, 1, 3).reshape(64, 64, 128)


def field_view(x):
    return x.reshape(8, 8, 32, 128).transpose(0, 2, 1, 3).reshape(8, 256, 128)


def exchange(x):
    return lax.all_to_all(x, "dev", split_axis=0, concat_axis=0, tiled=True)


def boundaries(arrival, received, count):
    side = struct(8, 8 * count, 128)
    return call(boundary, (side, side), [smem(), vmem()])(arrival, received)


def from_groups(south, north):
    size = lax.axis_size("grp")
    ahead = [(i, (i + 1) % size) for i in range(size)]
    return lax.ppermute(north, "grp", ahead), lax.ppermute(south, "grp", [(j, i) for i, j in ahead])


def shards(velocity, forcing, mass, coriolis, viscosity, lines, tile_source_slot, ocean_tile):
    u, b = vector_view(velocity), vector_view(forcing)
    a, f, z, p = [field_view(x) for x in (mass, coriolis, viscosity, lines)]

    message, table, codes, arrival, pairs = call(
        first_edges,
        (
            struct(PAIRS * 32, 128), struct(TABLE, dtype=jnp.int32), struct(CODES, dtype=jnp.int32),
            struct(TILES + 8, dtype=jnp.int32), resident(PAIRS, 192, 128),
        ),
        [smem(), smem(), hbm(), hbm()],
        [
            buffer(64, 64, 128), buffer(8, 256, 128), square(), square(), square(),
            pltpu.SMEM((PAIRS + 8,), jnp.int32), pltpu.SMEM((PAIRS,), jnp.int32), sems(2),
        ],
        (vmem(), smem(), smem(), smem(), vmem()),
        8,
    )(kept(ocean_tile), kept(tile_source_slot), kept(u), kept(z))

    received = exchange(message.reshape(PAIRS, 32, 128))
    south, north = boundaries(arrival, received, 2)
    south, north, later = lax.optimization_barrier((south, north, table))
    weight, b, a, f = call(
        prepare,
        (
            resident(PAIRS, 128, 256, dtype=BF16), resident(64, 64, 128),
            resident(8, 256, 128), resident(8, 256, 128),
        ),
        [smem()] + [hbm()] * 4,
        [buffer(8, 256, 128), buffer(CHUNK, 128, 128), sems(4)],
        [vmem()] * 4,
        4,
    )(later, kept(p), kept(b), kept(a), kept(f))
    halo, face = call(
        first_return, (struct(PAIRS, 16, 128), struct(TILES, 8, 128)), [smem()] + [vmem()] * 3
    )(arrival, received, *from_groups(south, north))
    halo, weight, b, a, f = lax.optimization_barrier((halo, weight, b, a, f))
    halo = exchange(halo).reshape(PAIRS * 16, 128)

    state, message, edges = call(
        first_step,
        (resident(PAIRS, STATE, 128), struct(PAIRS * 16, 128), struct(PAIRS * 8, 128)),
        [smem()] * 2 + [vmem()] * 6,
        [square()] * 5,
        mebibytes=8,
    )(table, codes, halo, held(pairs), held(b), held(a), held(f), held(weight))
    received = exchange(message.reshape(PAIRS, 16, 128))
    south, north = boundaries(arrival, received, 1)
    south, north, state = lax.optimization_barrier((south, north, state))
    whole = resident(PAIRS, 128, 128)
    local = call(local_part, whole, [vmem()], (), vmem())(held(state))
    halo = call(second_return, struct(PAIRS, 16, 128), [smem()] + [vmem()] * 5)(
        arrival, received, *from_groups(south, north), edges.reshape(PAIRS, 8, 128), face
    )
    halo, local = lax.optimization_barrier((halo, local))
    earlier = exchange(halo)
    halo = earlier.reshape(PAIRS * 16, 128)

    z1, d, p, message = call(
        second_step,
        (whole, whole, whole, struct(PAIRS * 32, 128)),
        [smem()] + [vmem()] * 4,
        [square()] * 5,
        mebibytes=8,
    )(codes, halo, held(state), held(local), held(weight))
    received = exchange(message.reshape(PAIRS, 32, 128))
    south, north = boundaries(arrival, received, 1)
    south, north, d = lax.optimization_barrier((south, north, d))
    sums = call(owner_sums, struct(6, 8, 128), [vmem()] * 3)(held(state), held(d), held(p))
    partial = call(edge_sums, struct(128, 128), [smem()] + [vmem()] * 6)(
        arrival, received, *from_groups(south, north), earlier, face, sums
    )
    gathered = lax.all_to_all(partial, ("grp", "dev"), split_axis=0, concat_axis=0, tiled=True)

    out = call(
        last_step, struct(SLOTS, 64, 128), [smem()] + [vmem()] * 4,
        [buffer(SLOTS + 1, 64, 128), pltpu.SemaphoreType.DMA],
        hbm(),
        8,
    )(table, gathered, held(pairs), held(state), held(z1))
    return out.reshape(64, 32, 2, 128).transpose(0, 2, 1, 3).reshape(64, 2, 4096)


def solution(mesh):
    return jax.shard_map(
        shards,
        mesh=mesh,
        in_specs=(
            P(("grp", "dev"), None, None),
            P(("grp", "dev"), None, None),
            P(("grp", "dev"), None),
            P(("grp", "dev"), None),
            P(("grp", "dev"), None),
            P(("grp", "dev"), None),
            P(("grp", "dev")),
            P(("grp", "dev")),
        ),
        out_specs=P(("grp", "dev"), None, None),
        check_vma=False,
    )
```

```python
import jax
import jax.numpy as jnp
from jax import lax
from jax.experimental import pallas as pl
from jax.experimental.pallas import tpu as pltpu
from jax.sharding import PartitionSpec as P

F32 = jnp.float32
BF16 = jnp.bfloat16
SLOTS = 64
PAIRS = 32
TILES = 32
CHUNK = 8
LONG = 32
CHUNKS = PAIRS // CHUNK
TABLE = 72
CODES = 144
STATE = 704
EPSILON = 1e-06


def params(mebibytes):
    return pltpu.CompilerParams(vmem_limit_bytes=mebibytes * 1024 * 1024)


def vmem():
    return pl.BlockSpec(memory_space=pltpu.VMEM)


def smem():
    return pl.BlockSpec(memory_space=pltpu.SMEM)


def struct(*shape, dtype=F32):
    return jax.ShapeDtypeStruct(shape, dtype)


def resident(*shape, dtype=F32):
    return pltpu.VMEM(shape, dtype)


def held(x):
    return pltpu.with_memory_space_constraint(x, pltpu.VMEM)


def kept(x):
    return pltpu.with_memory_space_constraint(x, pltpu.HBM)


def iota(shape, dim):
    return lax.broadcasted_iota(jnp.int32, shape, dim)


def roll(x, shift, axis):
    return pltpu.roll(x, shift, axis)


def pair_up(t0, t1):
    low = iota(t0.shape, 1) < 64
    crossed = roll(jnp.where(low, t1, t0), 64, 1)
    return jnp.concatenate([jnp.where(low, t0, crossed), jnp.where(low, crossed, t1)], axis=0)


def split_up(q):
    even, odd = q[:32], q[32:]
    low = iota(even.shape, 1) < 64
    crossed = roll(jnp.where(low, odd, even), 64, 1)
    return jnp.where(low, even, crossed), jnp.where(low, crossed, odd)


def load_tile(ref, index, offset, step):
    rows = [ref[index, pl.ds(offset + step * q, 8, stride=4 * step), :] for q in range(4)]
    return jnp.concatenate(rows, axis=0)


def load_field(ref, table, j, empty):
    tiles = []
    for r in range(2):
        s = table[2 * j + r]
        t = jnp.maximum(s, 0)
        tiles.append(jnp.where(s >= 0, load_tile(ref, t // 8, t % 8, 8), empty))
    return pair_up(*tiles)


def load_vector(ref, table, j):
    parts = []
    for c in range(2):
        tiles = []
        for r in range(2):
            s = table[2 * j + r]
            tiles.append(jnp.where(s >= 0, load_tile(ref, jnp.maximum(s, 0), c, 2), 0.0))
        parts.append(pair_up(*tiles))
    return parts


def put_columns(acc_ref, x, j):
    mine = ((iota(x.shape, 1) % 64) // 2) == j
    pltpu.store(acc_ref.at[pl.ds(0, x.shape[0])], roll(x, 2 * j + 1, 1), mask=mine)


def get_columns(acc, j):
    return roll(acc, 128 - (2 * j + 1), 1)


COLUMN_ROWS = (1, 64, 65, 0)


def columns_to_message(acc_ref, turned_ref, message_ref, first, stride):
    turned_ref[...] = acc_ref[...].T
    for row, source in enumerate(COLUMN_ROWS):
        message_ref[pl.ds(first + row, 32, stride=stride), :] = turned_ref[pl.ds(source, 32, stride=2), :]


def message_to_columns(message_ref, turned_ref, acc_ref, first, stride):
    for row, source in enumerate(COLUMN_ROWS):
        turned_ref[pl.ds(source, 32, stride=2), :] = message_ref[pl.ds(first + row, 32, stride=stride), :]
    acc_ref[...] = turned_ref[...].T


def put_rows(message_ref, x, base):
    for row, source in enumerate((0, 63, 64, 127)):
        message_ref[pl.ds(base + 4 + row, 1), :] = x[source : source + 1, :]


def south_of(x, halo=None):
    even, odd = x[:32], x[32:]
    below = roll(odd[24:], 1, 0)
    if halo is not None:
        below = jnp.where(iota(below.shape, 0) == 0, halo, below)
    return jnp.concatenate([below, odd[:24], even], axis=0)


def north_of(x, halo=None):
    even, odd = x[:32], x[32:]
    above = roll(even[:8], 7, 0)
    if halo is not None:
        above = jnp.where(iota(above.shape, 0) == 7, halo, above)
    return jnp.concatenate([odd, even[8:], above], axis=0)


def tile_part(y, west, south, turn):
    parts = []
    for c in range(2):
        rows = slice(64 * c, 64 * c + 64)
        x, w, s = y[rows], west[rows], south[rows]
        even, odd = x[:32], x[32:]
        s_even, s_odd = s[:32], s[32:]
        across = w * roll(x, 1, 1) + roll(w * x, 127, 1)
        up = s_even * even
        along = jnp.concatenate(
            [
                s_even[:8] * roll(odd[24:], 1, 0) + s_odd[:8] * odd[:8],
                s_even[8:] * odd[:24] + s_odd[8:] * odd[8:],
                s_odd[:24] * even[:24] + up[8:],
                s_odd[24:] * even[24:] + roll(up[:8], 7, 0),
            ],
            axis=0,
        )
        other = y[64:] if c == 0 else y[:64]
        spin = turn * other
        parts.append(x - across - along - spin if c == 0 else x - across - along + spin)
    return jnp.concatenate(parts, axis=0)


def line_solve(t, weight):
    high = t.astype(BF16)
    low = (t - high.astype(F32)).astype(BF16)
    out = lax.dot_general(
        jnp.concatenate([high, low], axis=1),
        jnp.concatenate([weight, weight], axis=0),
        (((1,), (0,)), ((), ())),
        preferred_element_type=F32,
    )
    return out[:, :128] + out[:, 128:]


def relax(q, weight, west, south, turn):
    y = line_solve(q, weight)
    for _ in range(2):
        y = y + line_solve(q - tile_part(y, west, south, turn), weight)
    return y


NONE = 99
CODE_W = 72


def make_table(ocean, table, count):
    def clear(i, carry):
        table[i] = -1
        return carry

    def clear_count(i, carry):
        count[i] = 0
        return carry

    def place(s, carry):
        t = ocean[s]
        j = jnp.where(t >= 0, (t >> 5) & 31, PAIRS)
        held = count[j] & 1
        table[2 * j + held] = s
        count[j] = held + 1
        return carry

    lax.fori_loop(0, TABLE, clear, 0, unroll=8)
    lax.fori_loop(0, PAIRS + 8, clear_count, 0, unroll=8)
    lax.fori_loop(0, SLOTS, place, 0, unroll=8)


def column_codes(ocean, table, codes, j):
    for r in range(2):
        p = 2 * j + r
        s = table[p]
        t = ocean[jnp.maximum(s, 0)]
        column, row = t & 7, (t >> 3) & 3
        codes[p + 2] = jnp.where((s >= 0) & (column == 7), row, NONE)
        codes[CODE_W + p] = jnp.where((s >= 0) & (column == 0), row + 4, NONE)


def land(source, arrival, first, t):
    slot = source[t]
    owner = (slot >> 6) & 31
    held = first[owner]
    later = (held >= 0) & (source[jnp.maximum(held, 0)] < slot)
    arrival[t] = 2 * owner + later.astype(jnp.int32)
    other = jnp.where(held >= 0, held, TILES)
    arrival[other] = 2 * owner + 1 - later.astype(jnp.int32)
    first[owner] = t


def put_extras(codes, turned, message_ref, first, stride):
    row = iota((8, 128), 0)

    def body(m, carry):
        before, after = 2 * jnp.maximum(m - 1, 0), 2 * jnp.minimum(m + 1, PAIRS - 1)
        total = jnp.zeros((8, 128), F32)
        for r in range(2):
            east = turned[pl.ds(before + (64, 0)[r], 1), :]
            west = turned[pl.ds(after + (1, 65)[r], 1), :]
            total = jnp.where(row == codes[2 * m + r], east, total)
            total = jnp.where(row == codes[CODE_W + 2 * m + 2 + r], west, total)
        message_ref[pl.ds(pl.multiple_of(m * stride + first, 8), 8), :] = total
        return carry

    lax.fori_loop(0, PAIRS, body, 0, unroll=8)


def first_edges(
    ocean, source, u_hbm, z_hbm, p_hbm, b_hbm, a_hbm, f_hbm,
    message_ref, table, codes, arrival, pairs, p_ref, b_ref, a_ref, f_ref,
    u_ref, z_ref, acc_v, acc_z, turned, count, landed, sem_in,
):
    z_copy = pltpu.make_async_copy(z_hbm, z_ref, sem_in.at[0])
    u_copy = pltpu.make_async_copy(u_hbm, u_ref, sem_in.at[1])
    z_copy.start()
    u_copy.start()
    make_table(ocean, table, count)
    for i in (0, 1, CODE_W + 64, CODE_W + 65):
        codes[i] = NONE
    for i in range(PAIRS):
        landed[i] = -1
    z_copy.wait()

    def scalars(i, carry):
        for k in range(CHUNK):
            j = i * CHUNK + k
            z = load_field(z_ref, table, j, 0.0)
            pairs[j, 128:192, :] = z
            put_columns(acc_z, z, j)
            put_rows(message_ref, jnp.concatenate([z, z], axis=0), 32 * j + 8)
            column_codes(ocean, table, codes, j)
        return carry

    def vectors(i, carry):
        for k in range(CHUNK):
            j = i * CHUNK + k
            u, v = load_vector(u_ref, table, j)
            vector = jnp.concatenate([u, v], axis=0)
            pairs[j, 0:128, :] = vector
            put_columns(acc_v, vector, j)
            put_rows(message_ref, vector, 32 * j)
            land(source, arrival, landed, j)
        return carry

    lax.fori_loop(0, CHUNKS, scalars, 0)
    u_copy.wait()
    later = [
        pltpu.make_async_copy(origin, target, sem_in.at[2 + n])
        for n, (origin, target) in enumerate(
            ((p_hbm, p_ref), (b_hbm, b_ref), (a_hbm, a_ref), (f_hbm, f_ref))
        )
    ]
    for copy in later:
        copy.start()
    lax.fori_loop(0, CHUNKS, vectors, 0)
    columns_to_message(acc_v, turned, message_ref, 0, 32)
    put_extras(codes, turned, message_ref, 16, 32)
    acc_z[64:128, :] = acc_z[0:64, :]
    columns_to_message(acc_z, turned, message_ref, 8, 32)
    put_extras(codes, turned, message_ref, 24, 32)
    for copy in later:
        copy.wait()


def prepare(table, p_ref, weight, natural):
    low = iota((32, 128), 1) < 64

    def lines(i, carry):
        for k in range(CHUNK):
            j = i * CHUNK + k
            tiles = []
            for r in range(2):
                s = table[2 * j + r]
                t = jnp.maximum(s, 0)
                x = p_ref[t // 8, pl.ds(t % 8, 32, stride=8), :]
                tiles.append(jnp.where(s >= 0, x, 0.0))
            t0, t1 = tiles
            crossed = roll(jnp.where(low, t1, t0), 64, 1)
            natural[k, pl.ds(0, 32, stride=2), :] = jnp.where(low, t0, 0.0)
            natural[k, pl.ds(1, 32, stride=2), :] = jnp.where(low, crossed, 0.0)
            natural[k, pl.ds(64, 32, stride=2), :] = jnp.where(low, 0.0, crossed)
            natural[k, pl.ds(65, 32, stride=2), :] = jnp.where(low, 0.0, t1)
            turned = natural[k].T
            high = turned.astype(BF16)
            weight[j, :, 0:128] = high
            weight[j, :, 128:256] = (turned - high.astype(F32)).astype(BF16)
        return carry

    lax.fori_loop(0, CHUNKS, lines, 0)


def side_masks():
    x = iota((64, 128), 1) % 64
    return x == 0, x == 63


KX = (1.25, 0.25)
KY = (0.25, 1.25)


def first_step(
    table, codes, halo_ref, pairs, b_ref, a_ref, f_ref, weight,
    state, message_ref,
    acc_z, hv, hz, turned,
):
    message_to_columns(halo_ref, turned, hv, 0, 16)
    message_to_columns(halo_ref, turned, hz, 8, 16)
    at_west, at_east = side_masks()

    def one(j):
        u0 = pairs[j, 0:64, :], pairs[j, 64:128, :]
        z = pairs[j, 128:192, :]
        b = load_vector(b_ref, table, j)
        a = load_field(a_ref, table, j, 1.0)
        f = load_field(f_ref, table, j, 0.0)
        side_v = get_columns(hv[...], j)
        side_z = get_columns(hz[0:64, :], j)
        rows = halo_ref[pl.ds(pl.multiple_of(16 * j, 16), 16), :]
        face_w = 0.5 * (z + jnp.where(at_west, side_z, roll(z, 1, 1)))
        face_e = 0.5 * (z + jnp.where(at_east, side_z, roll(z, 127, 1)))
        face_s = 0.5 * (z + south_of(z, rows[12:13]))
        face_n = 0.5 * (z + north_of(z, rows[13:14]))
        scale, diag = [], []
        for c in range(2):
            d = a + KX[c] * (face_w + face_e) + KY[c] * (face_s + face_n)
            diag.append(d)
            scale.append(lax.rsqrt(d))
        turn = f * scale[0] * scale[1]
        rhat, west, south = [], [], []
        for c in range(2):
            x, s = u0[c], scale[c]
            side = side_v[64 * c : 64 * c + 64]
            x_w = jnp.where(at_west, side, roll(x, 1, 1))
            x_e = jnp.where(at_east, side, roll(x, 127, 1))
            x_s = south_of(x, rows[4 + 2 * c : 5 + 2 * c])
            x_n = north_of(x, rows[5 + 2 * c : 6 + 2 * c])
            spin = -f * u0[1] if c == 0 else f * u0[0]
            applied = (
                diag[c] * x + spin
                - KX[c] * (face_w * x_w + face_e * x_e)
                - KY[c] * (face_s * x_s + face_n * x_n)
            )
            rhat.append(s * (b[c] - applied))
            k_w = KX[c] * s * face_w
            k_s = KY[c] * s * face_s
            west.append(jnp.where(at_west, 0.0, k_w * roll(s, 1, 1)))
            south.append(k_s * south_of(s, jnp.zeros((1, 128), F32)))
        rhat = jnp.concatenate(rhat, axis=0)
        west = jnp.concatenate(west, axis=0)
        south = jnp.concatenate(south, axis=0)
        state[j, 0:128, :] = west
        state[j, 128:256, :] = south
        state[j, 256:384, :] = jnp.concatenate(diag, axis=0)
        state[j, 384:512, :] = rhat
        state[j, 512:576, :] = turn
        y = relax(rhat, weight[j], west, south, turn)
        z0 = jnp.concatenate(scale, axis=0) * y
        state[j, 576:704, :] = z0
        put_columns(acc_z, z0, j)
        put_rows(message_ref, z0, 16 * j)

    def body(i, carry):
        for k in range(LONG):
            one(i * LONG + k)
        return carry

    lax.fori_loop(0, PAIRS // LONG, body, 0)
    columns_to_message(acc_z, turned, message_ref, 0, 16)
    put_extras(codes, turned, message_ref, 8, 16)


def local_part(state, local, edges_ref, acc, turned):
    def body(i, carry):
        for k in range(CHUNK):
            j = i * CHUNK + k
            diag = state[j, 256:384, :]
            root = diag * lax.rsqrt(diag)
            rhat = state[j, 384:512, :]
            y0 = root * state[j, 576:704, :]
            local[j] = tile_part(y0, state[j, 0:128, :], state[j, 128:256, :], state[j, 512:576, :]) - rhat
            r = root * rhat
            put_columns(acc, r, j)
            put_rows(edges_ref, r, 8 * j)
        return carry

    lax.fori_loop(0, CHUNKS, body, 0)
    columns_to_message(acc, turned, edges_ref, 0, 8)


def owner_sums(state, d_ref, p_ref, sums_ref):
    def body(i, carry):
        totals = [jnp.zeros((8, 128), F32) for _ in range(6)]
        for k in range(CHUNK):
            j = i * CHUNK + k
            diag = state[j, 256:384, :]
            r = diag * lax.rsqrt(diag) * state[j, 384:512, :]
            d, p = d_ref[j], p_ref[j]
            for index, (left, right) in enumerate(((r, r), (r, d), (d, d), (r, p), (d, p), (p, p))):
                product = left * right
                for n in range(16):
                    totals[index] = totals[index] + product[8 * n : 8 * n + 8]
        for index in range(6):
            sums_ref[index] += totals[index]
        return carry

    sums_ref[...] = jnp.zeros((6, 8, 128), F32)
    lax.fori_loop(0, CHUNKS, body, 0)


def second_step(
    codes, halo_ref, state, local, weight,
    z1s, d_ref, p_ref, message_ref,
    acc_z, acc_p, acc_d, hv, turned,
):
    message_to_columns(halo_ref, turned, hv, 0, 16)
    lane = iota((128, 128), 1) % 64
    at_side = (lane == 0) | (lane == 63)
    first, last = iota((8, 128), 0) == 0, iota((8, 128), 0) == 7

    def one(j):
        west, south, turn = state[j, 0:128, :], state[j, 128:256, :], state[j, 512:576, :]
        diag = state[j, 256:384, :]
        scale = lax.rsqrt(diag)
        root = diag * scale
        what = local[j] - jnp.where(at_side, scale * get_columns(hv[...], j), 0.0)
        rows = halo_ref[pl.ds(pl.multiple_of(16 * j, 16), 8), :]
        fixed = []
        for c in range(2):
            part = what[64 * c : 64 * c + 64]
            s = scale[64 * c : 64 * c + 64]
            low = part[:8] - jnp.where(first, s[:8] * rows[4 + 2 * c : 5 + 2 * c], 0.0)
            high = part[56:] - jnp.where(last, s[56:] * rows[5 + 2 * c : 6 + 2 * c], 0.0)
            fixed += [low, part[8:56], high]
        dhat = jnp.concatenate(fixed, axis=0)
        y1 = relax(dhat, weight[j], west, south, turn)
        phat = tile_part(y1, west, south, turn) - dhat
        z1 = scale * y1
        z1s[j] = z1
        d, p = root * dhat, root * phat
        d_ref[j] = d
        p_ref[j] = p
        for k, (acc, x) in enumerate(((acc_z, z1), (acc_p, p), (acc_d, d))):
            put_columns(acc, x, j)
            put_rows(message_ref, x, 32 * j + 8 * k)

    def body(i, carry):
        for k in range(LONG):
            one(i * LONG + k)
        return carry

    lax.fori_loop(0, PAIRS // LONG, body, 0)
    columns_to_message(acc_p, turned, message_ref, 8, 32)
    columns_to_message(acc_d, turned, message_ref, 16, 32)
    columns_to_message(acc_z, turned, message_ref, 0, 32)
    put_extras(codes, turned, message_ref, 24, 32)


def to_normal(x, r):
    row = iota((8, 128), 0)
    return jnp.where(r == 1, jnp.where(row < 4, roll(x, 6, 0), roll(x, 64, 1)), x)


def halo_of(west, east, south, north):
    row = iota((8, 128), 0)
    side = jnp.where(row == 0, roll(west, 7, 0), roll(east, 1, 0))
    end = jnp.where(row % 2 == 0, roll(south, 7, 0), roll(north, 1, 0))
    return jnp.where(row < 2, side, jnp.where(row >= 4, end, 0.0))


def tile_block(arrival, received_ref, t, k):
    at = arrival[t]
    return to_normal(received_ref[at // 2, 8 * k : 8 * k + 8, :], at % 2)


def boundary(arrival, received_ref, south_ref, north_ref):
    for k in range(south_ref.shape[1] // 8):
        rows = slice(8 * k, 8 * k + 8)
        for x in range(8):
            south_ref[x, rows, :] = tile_block(arrival, received_ref, x, k)
            north_ref[x, rows, :] = tile_block(arrival, received_ref, 24 + x, k)


def tile_halos(arrival, received_ref, from_south, from_north, k, extra):
    group = lax.axis_index("grp")
    blocks = [tile_block(arrival, received_ref, t, k) for t in range(TILES)]
    sides = received_ref[0, 8 * extra : 8 * extra + 8, :]
    for o in range(1, PAIRS):
        sides = sides + received_ref[o, 8 * extra : 8 * extra + 8, :]
    rows = slice(8 * k, 8 * k + 8)
    last = lax.axis_size("grp") - 1
    below = [jnp.where(group > 0, from_south[x, rows, :], 0.0) for x in range(8)]
    above = [jnp.where(group < last, from_north[x, rows, :], 0.0) for x in range(8)]
    halos = []
    for t in range(TILES):
        ty, tx = t // 8, t % 8
        halos.append(
            halo_of(
                blocks[t - 1] if tx > 0 else roll(sides, (1 - ty) % 8, 0),
                blocks[t + 1] if tx < 7 else roll(sides, 4 - ty, 0),
                blocks[t - 8] if ty > 0 else below[tx],
                blocks[t + 8] if ty < 3 else above[tx],
            )
        )
    return blocks, halos


def hand_back(arrival, t, k, halo, out_ref):
    at = arrival[t]
    r = at % 2
    row, lane = iota((8, 128), 0), iota((8, 128), 1)
    placed = jnp.where(r == 1, jnp.where(row < 4, roll(halo, 2, 0), roll(halo, 64, 1)), halo)
    mine = ((row < 4) & (row // 2 == r)) | ((row >= 4) & (lane // 64 == r))
    rows = slice(8 * k, 8 * k + 8)
    out_ref[at // 2, rows, :] += jnp.where(mine, placed, 0.0)


def first_return(arrival, received_ref, south, north, out_ref, face_ref):
    row, lane = iota((8, 128), 0), iota((8, 128), 1)
    along_x = jnp.where(lane < 64, KX[0], KX[1])
    along_y = jnp.where(row < 6, KY[0], KY[1])
    factor = 0.5 * jnp.where(row < 4, along_x, along_y)
    out_ref[...] = jnp.zeros(out_ref.shape, F32)
    for k in range(2):
        blocks, halos = tile_halos(arrival, received_ref, south, north, k, 2 + k)
        for t in range(TILES):
            hand_back(arrival, t, k, halos[t], out_ref)
            if k == 1:
                face_ref[t] = factor * (blocks[t] + halos[t])


def second_return(arrival, received_ref, south, north, edges_ref, face_ref, out_ref):
    out_ref[:, 0:8, :] = jnp.zeros((PAIRS, 8, 128), F32)
    out_ref[:, 8:16, :] = edges_ref[...]
    blocks, halos = tile_halos(arrival, received_ref, south, north, 0, 1)
    for t in range(TILES):
        hand_back(arrival, t, 0, face_ref[t] * halos[t], out_ref)


def edge_sums(arrival, received_ref, south, north, earlier_ref, face_ref, sums_ref, out_ref):
    row, lane = iota((8, 128), 0), iota((8, 128), 1)
    valid = (row < 2) | ((row >= 4) & (lane < 64))
    total_r = jnp.zeros((8, 128), F32)
    total_d = jnp.zeros((8, 128), F32)
    total_p = jnp.zeros((8, 128), F32)
    blocks, halos = tile_halos(arrival, received_ref, south, north, 0, 3)
    for t in range(TILES):
        h = jnp.where(valid, -face_ref[t] * halos[t], 0.0)
        p = tile_block(arrival, received_ref, t, 1)
        d = tile_block(arrival, received_ref, t, 2)
        r = tile_block(arrival, earlier_ref, t, 1)
        total_r = total_r + jnp.where(valid, h * r, 0.0)
        total_d = total_d + jnp.where(valid, h * d, 0.0)
        wide_w = jnp.broadcast_to(h[0:1], (8, 128))
        wide_e = jnp.broadcast_to(h[1:2], (8, 128))
        corner_w = jnp.where(
            row == 4, wide_w,
            jnp.where(row == 5, roll(wide_w, 65, 1), jnp.where(row == 6, roll(wide_w, 64, 1), roll(wide_w, 1, 1))),
        )
        corner_e = jnp.where(
            row == 4, roll(wide_e, 63, 1),
            jnp.where(row == 5, wide_e, jnp.where(row == 6, roll(wide_e, 127, 1), roll(wide_e, 64, 1))),
        )
        corner = jnp.where(lane == 0, corner_w, jnp.where(lane == 63, corner_e, 0.0))
        corner = jnp.where(row >= 4, corner, 0.0)
        total_p = total_p + jnp.where(valid, h * (2.0 * (p + corner) + h), 0.0)
    lane = iota((1, 128), 1)
    out = jnp.zeros((1, 128), F32)
    for index in range(6):
        total = sums_ref[index]
        if index == 3:
            total = total + total_r
        if index == 4:
            total = total + total_d
        if index == 5:
            total = total + total_p
        value = jnp.sum(jnp.sum(total, axis=0, keepdims=True), axis=1, keepdims=True)
        out = jnp.where(lane == index, value, out)
    out_ref[...] = jnp.broadcast_to(out, (128, 128))


def least_squares(magnitude, upper_first, below_first, upper_cross, upper_second, below_second):
    radius_first = jnp.sqrt(upper_first * upper_first + below_first * below_first)
    cosine_first = upper_first / radius_first
    sine_first = below_first / radius_first
    lifted_top = cosine_first * upper_cross + sine_first * upper_second
    lifted_low = cosine_first * upper_second - sine_first * upper_cross
    radius_second = jnp.sqrt(lifted_low * lifted_low + below_second * below_second)
    weight_second = -(sine_first * magnitude) * (lifted_low / radius_second) / radius_second
    weight_first = (cosine_first * magnitude - lifted_top * weight_second) / radius_first
    return (weight_first, weight_second)


def final_weights(gathered):
    total = jnp.sum(gathered, axis=0, keepdims=True)
    lane = iota((1, 128), 1)
    rr, rd, dd, re, de, ee = [
        jnp.sum(jnp.where(lane == index, total, 0.0), axis=1, keepdims=True) for index in range(6)
    ]
    square = rr + EPSILON
    magnitude = jnp.sqrt(square)
    h11 = (rr + rd) / square
    gap = -(rd - EPSILON) / square
    h21_square = jnp.maximum((dd + 2.0 * gap * rd + gap * gap * rr) / square, 0.0) + EPSILON
    h21 = jnp.sqrt(h21_square)
    unit = 1.0 / (magnitude * h21)
    h12 = (gap * rr + (1.0 + gap) * rd + re) * unit / magnitude
    h22 = (
        gap * (gap * rr + rd) + (1.0 + gap) * (gap * rd + dd) + (gap * re + de)
    ) * unit * unit
    c_r = gap * unit - h12 / magnitude - h22 * gap * unit
    c_d = (1.0 + gap - h22) * unit
    c_e = unit
    h32_square = (
        c_r * c_r * rr + c_d * c_d * dd + c_e * c_e * ee
        + 2.0 * (c_r * c_d * rd + c_r * c_e * re + c_d * c_e * de)
    )
    h32 = jnp.sqrt(jnp.maximum(h32_square, 0.0) + EPSILON)
    y1, y2 = least_squares(magnitude, h11, h21, h12, h22, h32)
    return y1 / magnitude + y2 * gap * unit, y2 * unit


def last_step(
    table, gathered_ref, pairs, state, z1,
    out_hbm,
    out, sem_out,
):
    out[...] = jnp.zeros(out.shape, F32)
    weight0, weight1 = final_weights(gathered_ref[...])

    def body(i, carry):
        for k in range(CHUNK):
            j = i * CHUNK + k
            new = pairs[j, 0:128, :] + weight0 * state[j, 576:704, :] + weight1 * z1[j]
            slots = [jnp.where(table[2 * j + r] >= 0, table[2 * j + r], SLOTS) for r in range(2)]
            for c in range(2):
                for r, x in enumerate(split_up(new[64 * c : 64 * c + 64])):
                    for q in range(4):
                        out[slots[r], pl.ds(c + 2 * q, 8, stride=8), :] = x[8 * q : 8 * q + 8]
        return carry

    lax.fori_loop(0, CHUNKS, body, 0)
    copy = pltpu.make_async_copy(out.at[pl.ds(0, SLOTS)], out_hbm, sem_out)
    copy.start()
    copy.wait()


def call(kernel, outs, specs, scratch=(), out_specs=None, mebibytes=4):
    return pl.pallas_call(
        kernel,
        out_shape=outs,
        in_specs=specs,
        out_specs=out_specs if out_specs is not None else jax.tree.map(lambda _: vmem(), outs),
        scratch_shapes=list(scratch),
        compiler_params=params(mebibytes),
    )


def hbm():
    return pl.BlockSpec(memory_space=pl.ANY)


def square(rows=128):
    return pltpu.VMEM((rows, 128), F32)


def buffer(*shape, dtype=F32):
    return pltpu.VMEM(shape, dtype)


def sems(*shape):
    return pltpu.SemaphoreType.DMA(shape)


def vector_view(x):
    return x.reshape(64, 2, 32, 128).transpose(0, 2, 1, 3).reshape(64, 64, 128)


def field_view(x):
    return x.reshape(8, 8, 32, 128).transpose(0, 2, 1, 3).reshape(8, 256, 128)


def exchange(x):
    return lax.all_to_all(x, "dev", split_axis=0, concat_axis=0, tiled=True)


def boundaries(arrival, received, count):
    side = struct(8, 8 * count, 128)
    return call(boundary, (side, side), [smem(), vmem()])(arrival, received)


def from_groups(south, north):
    size = lax.axis_size("grp")
    ahead = [(i, (i + 1) % size) for i in range(size)]
    return lax.ppermute(north, "grp", ahead), lax.ppermute(south, "grp", [(j, i) for i, j in ahead])


def shards(velocity, forcing, mass, coriolis, viscosity, lines, tile_source_slot, ocean_tile):
    u, b = vector_view(velocity), vector_view(forcing)
    a, f, z, p = [field_view(x) for x in (mass, coriolis, viscosity, lines)]

    tiles, vectors = resident(8, 256, 128), resident(64, 64, 128)
    message, table, codes, arrival, pairs, p, b, a, f = call(
        first_edges,
        (
            struct(PAIRS * 32, 128), struct(TABLE, dtype=jnp.int32), struct(CODES, dtype=jnp.int32),
            struct(TILES + 8, dtype=jnp.int32), resident(PAIRS, 192, 128), tiles, vectors, tiles, tiles,
        ),
        [smem(), smem()] + [hbm()] * 6,
        [
            buffer(64, 64, 128), buffer(8, 256, 128), square(), square(), square(),
            pltpu.SMEM((PAIRS + 8,), jnp.int32), pltpu.SMEM((PAIRS,), jnp.int32), sems(6),
        ],
        (vmem(), smem(), smem(), smem()) + (vmem(),) * 5,
        8,
    )(*[kept(x) for x in (ocean_tile, tile_source_slot, u, z, p, b, a, f)])

    received = exchange(message.reshape(PAIRS, 32, 128))
    south, north = boundaries(arrival, received, 2)
    south, north, p = lax.optimization_barrier((south, north, p))
    weight = call(
        prepare, resident(PAIRS, 128, 256, dtype=BF16), [smem(), vmem()],
        [buffer(CHUNK, 128, 128)], vmem(),
    )(table, held(p))
    halo, face = call(
        first_return, (struct(PAIRS, 16, 128), struct(TILES, 8, 128)), [smem()] + [vmem()] * 3
    )(arrival, received, *from_groups(south, north))
    halo, weight = lax.optimization_barrier((halo, weight))
    halo = exchange(halo).reshape(PAIRS * 16, 128)

    state, message = call(
        first_step,
        (resident(PAIRS, STATE, 128), struct(PAIRS * 16, 128)),
        [smem()] * 2 + [vmem()] * 6,
        [square()] * 4,
        mebibytes=8,
    )(table, codes, halo, held(pairs), held(b), held(a), held(f), held(weight))
    received = exchange(message.reshape(PAIRS, 16, 128))
    south, north = boundaries(arrival, received, 1)
    south, north, state = lax.optimization_barrier((south, north, state))
    whole = resident(PAIRS, 128, 128)
    local, edges = call(
        local_part, (whole, struct(PAIRS * 8, 128)), [vmem()], [square(), square()]
    )(held(state))
    halo = call(second_return, struct(PAIRS, 16, 128), [smem()] + [vmem()] * 5)(
        arrival, received, *from_groups(south, north), edges.reshape(PAIRS, 8, 128), face
    )
    halo, local = lax.optimization_barrier((halo, local))
    earlier = exchange(halo)
    halo = earlier.reshape(PAIRS * 16, 128)

    z1, d, p, message = call(
        second_step,
        (whole, whole, whole, struct(PAIRS * 32, 128)),
        [smem()] + [vmem()] * 4,
        [square()] * 5,
        mebibytes=8,
    )(codes, halo, held(state), held(local), held(weight))
    received = exchange(message.reshape(PAIRS, 32, 128))
    south, north = boundaries(arrival, received, 1)
    south, north, d = lax.optimization_barrier((south, north, d))
    sums = call(owner_sums, struct(6, 8, 128), [vmem()] * 3)(held(state), held(d), held(p))
    partial = call(edge_sums, struct(128, 128), [smem()] + [vmem()] * 6)(
        arrival, received, *from_groups(south, north), earlier, face, sums
    )
    gathered = lax.all_to_all(partial, ("grp", "dev"), split_axis=0, concat_axis=0, tiled=True)

    out = call(
        last_step, struct(SLOTS, 64, 128), [smem()] + [vmem()] * 4,
        [buffer(SLOTS + 1, 64, 128), pltpu.SemaphoreType.DMA],
        hbm(),
        8,
    )(table, gathered, held(pairs), held(state), held(z1))
    return out.reshape(64, 32, 2, 128).transpose(0, 2, 1, 3).reshape(64, 2, 4096)


def solution(mesh):
    return jax.shard_map(
        shards,
        mesh=mesh,
        in_specs=(
            P(("grp", "dev"), None, None),
            P(("grp", "dev"), None, None),
            P(("grp", "dev"), None),
            P(("grp", "dev"), None),
            P(("grp", "dev"), None),
            P(("grp", "dev"), None),
            P(("grp", "dev")),
            P(("grp", "dev")),
        ),
        out_specs=P(("grp", "dev"), None, None),
        check_vma=False,
    )
```

```python
import jax
import jax.numpy as jnp
from jax import lax
from jax.experimental import pallas as pl
from jax.experimental.pallas import tpu as pltpu
from jax.sharding import PartitionSpec as P

F32 = jnp.float32
BF16 = jnp.bfloat16
SLOTS = 64
PAIRS = 32
TILES = 32
CHUNK = 8
LONG = 32
CHUNKS = PAIRS // CHUNK
TABLE = 72
CODES = 144
STATE = 704
EPSILON = 1e-06


def params(mebibytes):
    return pltpu.CompilerParams(vmem_limit_bytes=mebibytes * 1024 * 1024)


def vmem():
    return pl.BlockSpec(memory_space=pltpu.VMEM)


def smem():
    return pl.BlockSpec(memory_space=pltpu.SMEM)


def struct(*shape, dtype=F32):
    return jax.ShapeDtypeStruct(shape, dtype)


def resident(*shape, dtype=F32):
    return pltpu.VMEM(shape, dtype)


def held(x):
    return pltpu.with_memory_space_constraint(x, pltpu.VMEM)


def kept(x):
    return pltpu.with_memory_space_constraint(x, pltpu.HBM)


def iota(shape, dim):
    return lax.broadcasted_iota(jnp.int32, shape, dim)


def roll(x, shift, axis):
    return pltpu.roll(x, shift, axis)


def pair_up(t0, t1):
    low = iota(t0.shape, 1) < 64
    crossed = roll(jnp.where(low, t1, t0), 64, 1)
    return jnp.concatenate([jnp.where(low, t0, crossed), jnp.where(low, crossed, t1)], axis=0)


def split_up(q):
    even, odd = q[:32], q[32:]
    low = iota(even.shape, 1) < 64
    crossed = roll(jnp.where(low, odd, even), 64, 1)
    return jnp.where(low, even, crossed), jnp.where(low, crossed, odd)


def load_tile(ref, index, offset, step):
    rows = [ref[index, pl.ds(offset + step * q, 8, stride=4 * step), :] for q in range(4)]
    return jnp.concatenate(rows, axis=0)


def load_field(ref, table, j, empty):
    tiles = []
    for r in range(2):
        s = table[2 * j + r]
        t = jnp.maximum(s, 0)
        tiles.append(jnp.where(s >= 0, load_tile(ref, t // 8, t % 8, 8), empty))
    return pair_up(*tiles)


def load_vector(ref, table, j):
    parts = []
    for c in range(2):
        tiles = []
        for r in range(2):
            s = table[2 * j + r]
            tiles.append(jnp.where(s >= 0, load_tile(ref, jnp.maximum(s, 0), c, 2), 0.0))
        parts.append(pair_up(*tiles))
    return parts


def put_columns(acc_ref, x, j):
    mine = ((iota(x.shape, 1) % 64) // 2) == j
    pltpu.store(acc_ref.at[pl.ds(0, x.shape[0])], roll(x, 2 * j + 1, 1), mask=mine)


def get_columns(acc, j):
    return roll(acc, 128 - (2 * j + 1), 1)


COLUMN_ROWS = (1, 64, 65, 0)


def columns_to_message(acc_ref, turned_ref, message_ref, first, stride):
    turned_ref[...] = acc_ref[...].T
    for row, source in enumerate(COLUMN_ROWS):
        message_ref[pl.ds(first + row, 32, stride=stride), :] = turned_ref[pl.ds(source, 32, stride=2), :]


def message_to_columns(message_ref, turned_ref, acc_ref, first, stride):
    for row, source in enumerate(COLUMN_ROWS):
        turned_ref[pl.ds(source, 32, stride=2), :] = message_ref[pl.ds(first + row, 32, stride=stride), :]
    acc_ref[...] = turned_ref[...].T


def put_rows(message_ref, x, base):
    for row, source in enumerate((0, 63, 64, 127)):
        message_ref[pl.ds(base + 4 + row, 1), :] = x[source : source + 1, :]


def south_of(x, halo=None):
    even, odd = x[:32], x[32:]
    below = roll(odd[24:], 1, 0)
    if halo is not None:
        below = jnp.where(iota(below.shape, 0) == 0, halo, below)
    return jnp.concatenate([below, odd[:24], even], axis=0)


def north_of(x, halo=None):
    even, odd = x[:32], x[32:]
    above = roll(even[:8], 7, 0)
    if halo is not None:
        above = jnp.where(iota(above.shape, 0) == 7, halo, above)
    return jnp.concatenate([odd, even[8:], above], axis=0)


def tile_part(y, west, south, turn):
    parts = []
    for c in range(2):
        rows = slice(64 * c, 64 * c + 64)
        x, w, s = y[rows], west[rows], south[rows]
        even, odd = x[:32], x[32:]
        s_even, s_odd = s[:32], s[32:]
        across = w * roll(x, 1, 1) + roll(w * x, 127, 1)
        up = s_even * even
        along = jnp.concatenate(
            [
                s_even[:8] * roll(odd[24:], 1, 0) + s_odd[:8] * odd[:8],
                s_even[8:] * odd[:24] + s_odd[8:] * odd[8:],
                s_odd[:24] * even[:24] + up[8:],
                s_odd[24:] * even[24:] + roll(up[:8], 7, 0),
            ],
            axis=0,
        )
        other = y[64:] if c == 0 else y[:64]
        spin = turn * other
        parts.append(x - across - along - spin if c == 0 else x - across - along + spin)
    return jnp.concatenate(parts, axis=0)


def line_solve(t, weight):
    high = t.astype(BF16)
    low = (t - high.astype(F32)).astype(BF16)
    out = lax.dot_general(
        jnp.concatenate([high, low], axis=1),
        jnp.concatenate([weight, weight], axis=0),
        (((1,), (0,)), ((), ())),
        preferred_element_type=F32,
    )
    return out[:, :128] + out[:, 128:]


def relax(q, weight, west, south, turn):
    y = line_solve(q, weight)
    for _ in range(2):
        y = y + line_solve(q - tile_part(y, west, south, turn), weight)
    return y


NONE = 99
CODE_W = 72


def make_table(ocean, table, count):
    def clear(i, carry):
        table[i] = -1
        return carry

    def clear_count(i, carry):
        count[i] = 0
        return carry

    def place(s, carry):
        t = ocean[s]
        j = jnp.where(t >= 0, (t >> 5) & 31, PAIRS)
        held = count[j] & 1
        table[2 * j + held] = s
        count[j] = held + 1
        return carry

    lax.fori_loop(0, TABLE, clear, 0, unroll=8)
    lax.fori_loop(0, PAIRS + 8, clear_count, 0, unroll=8)
    lax.fori_loop(0, SLOTS, place, 0, unroll=8)


def column_codes(ocean, table, codes, j):
    for r in range(2):
        p = 2 * j + r
        s = table[p]
        t = ocean[jnp.maximum(s, 0)]
        column, row = t & 7, (t >> 3) & 3
        codes[p + 2] = jnp.where((s >= 0) & (column == 7), row, NONE)
        codes[CODE_W + p] = jnp.where((s >= 0) & (column == 0), row + 4, NONE)


def land(source, arrival, first, t):
    slot = source[t]
    owner = (slot >> 6) & 31
    held = first[owner]
    later = (held >= 0) & (source[jnp.maximum(held, 0)] < slot)
    arrival[t] = 2 * owner + later.astype(jnp.int32)
    other = jnp.where(held >= 0, held, TILES)
    arrival[other] = 2 * owner + 1 - later.astype(jnp.int32)
    first[owner] = t


def put_extras(codes, turned, message_ref, first, stride):
    row = iota((8, 128), 0)

    def body(m, carry):
        before, after = 2 * jnp.maximum(m - 1, 0), 2 * jnp.minimum(m + 1, PAIRS - 1)
        total = jnp.zeros((8, 128), F32)
        for r in range(2):
            east = turned[pl.ds(before + (64, 0)[r], 1), :]
            west = turned[pl.ds(after + (1, 65)[r], 1), :]
            total = jnp.where(row == codes[2 * m + r], east, total)
            total = jnp.where(row == codes[CODE_W + 2 * m + 2 + r], west, total)
        message_ref[pl.ds(pl.multiple_of(m * stride + first, 8), 8), :] = total
        return carry

    lax.fori_loop(0, PAIRS, body, 0, unroll=8)


def first_edges(
    ocean, source, u_hbm, z_hbm, p_hbm, b_hbm, a_hbm, f_hbm,
    message_ref, table, codes, arrival, pairs, p_ref, b_ref, a_ref, f_ref,
    u_ref, z_ref, acc_v, acc_z, turned, count, landed, sem_in,
):
    z_copy = pltpu.make_async_copy(z_hbm, z_ref, sem_in.at[0])
    u_copy = pltpu.make_async_copy(u_hbm, u_ref, sem_in.at[1])
    z_copy.start()
    u_copy.start()
    make_table(ocean, table, count)
    for i in (0, 1, CODE_W + 64, CODE_W + 65):
        codes[i] = NONE
    for i in range(PAIRS):
        landed[i] = -1
    z_copy.wait()

    def scalars(i, carry):
        for k in range(CHUNK):
            j = i * CHUNK + k
            z = load_field(z_ref, table, j, 0.0)
            pairs[j, 128:192, :] = z
            put_columns(acc_z, z, j)
            put_rows(message_ref, jnp.concatenate([z, z], axis=0), 32 * j + 8)
            column_codes(ocean, table, codes, j)
        return carry

    def vectors(i, carry):
        for k in range(CHUNK):
            j = i * CHUNK + k
            u, v = load_vector(u_ref, table, j)
            vector = jnp.concatenate([u, v], axis=0)
            pairs[j, 0:128, :] = vector
            put_columns(acc_v, vector, j)
            put_rows(message_ref, vector, 32 * j)
            land(source, arrival, landed, j)
        return carry

    lax.fori_loop(0, CHUNKS, scalars, 0)
    u_copy.wait()
    later = [
        pltpu.make_async_copy(origin, target, sem_in.at[2 + n])
        for n, (origin, target) in enumerate(
            ((p_hbm, p_ref), (b_hbm, b_ref), (a_hbm, a_ref), (f_hbm, f_ref))
        )
    ]
    for copy in later:
        copy.start()
    lax.fori_loop(0, CHUNKS, vectors, 0)
    columns_to_message(acc_v, turned, message_ref, 0, 32)
    put_extras(codes, turned, message_ref, 16, 32)
    acc_z[64:128, :] = acc_z[0:64, :]
    columns_to_message(acc_z, turned, message_ref, 8, 32)
    put_extras(codes, turned, message_ref, 24, 32)
    for copy in later:
        copy.wait()


def prepare(table, p_ref, a_ref, f_ref, weight, fields, natural):
    low = iota((32, 128), 1) < 64

    def lines(i, carry):
        for k in range(CHUNK):
            j = i * CHUNK + k
            tiles = []
            for r in range(2):
                s = table[2 * j + r]
                t = jnp.maximum(s, 0)
                x = p_ref[t // 8, pl.ds(t % 8, 32, stride=8), :]
                tiles.append(jnp.where(s >= 0, x, 0.0))
            t0, t1 = tiles
            crossed = roll(jnp.where(low, t1, t0), 64, 1)
            natural[k, pl.ds(0, 32, stride=2), :] = jnp.where(low, t0, 0.0)
            natural[k, pl.ds(1, 32, stride=2), :] = jnp.where(low, crossed, 0.0)
            natural[k, pl.ds(64, 32, stride=2), :] = jnp.where(low, 0.0, crossed)
            natural[k, pl.ds(65, 32, stride=2), :] = jnp.where(low, 0.0, t1)
            turned = natural[k].T
            high = turned.astype(BF16)
            weight[j, :, 0:128] = high
            weight[j, :, 128:256] = (turned - high.astype(F32)).astype(BF16)
            fields[j, 0:64, :] = load_field(a_ref, table, j, 1.0)
            fields[j, 64:128, :] = load_field(f_ref, table, j, 0.0)
        return carry

    lax.fori_loop(0, CHUNKS, lines, 0)


def side_masks():
    x = iota((64, 128), 1) % 64
    return x == 0, x == 63


KX = (1.25, 0.25)
KY = (0.25, 1.25)


def first_step(
    table, codes, halo_ref, pairs, b_ref, fields, weight,
    state, message_ref,
    acc_z, hv, hz, turned,
):
    message_to_columns(halo_ref, turned, hv, 0, 16)
    message_to_columns(halo_ref, turned, hz, 8, 16)
    at_west, at_east = side_masks()

    def one(j):
        u0 = pairs[j, 0:64, :], pairs[j, 64:128, :]
        z = pairs[j, 128:192, :]
        b = load_vector(b_ref, table, j)
        a, f = fields[j, 0:64, :], fields[j, 64:128, :]
        side_v = get_columns(hv[...], j)
        side_z = get_columns(hz[0:64, :], j)
        rows = halo_ref[pl.ds(pl.multiple_of(16 * j, 16), 16), :]
        face_w = 0.5 * (z + jnp.where(at_west, side_z, roll(z, 1, 1)))
        face_e = 0.5 * (z + jnp.where(at_east, side_z, roll(z, 127, 1)))
        face_s = 0.5 * (z + south_of(z, rows[12:13]))
        face_n = 0.5 * (z + north_of(z, rows[13:14]))
        scale, diag = [], []
        for c in range(2):
            d = a + KX[c] * (face_w + face_e) + KY[c] * (face_s + face_n)
            diag.append(d)
            scale.append(lax.rsqrt(d))
        turn = f * scale[0] * scale[1]
        rhat, west, south = [], [], []
        for c in range(2):
            x, s = u0[c], scale[c]
            side = side_v[64 * c : 64 * c + 64]
            x_w = jnp.where(at_west, side, roll(x, 1, 1))
            x_e = jnp.where(at_east, side, roll(x, 127, 1))
            x_s = south_of(x, rows[4 + 2 * c : 5 + 2 * c])
            x_n = north_of(x, rows[5 + 2 * c : 6 + 2 * c])
            spin = -f * u0[1] if c == 0 else f * u0[0]
            applied = (
                diag[c] * x + spin
                - KX[c] * (face_w * x_w + face_e * x_e)
                - KY[c] * (face_s * x_s + face_n * x_n)
            )
            rhat.append(s * (b[c] - applied))
            k_w = KX[c] * s * face_w
            k_s = KY[c] * s * face_s
            west.append(jnp.where(at_west, 0.0, k_w * roll(s, 1, 1)))
            south.append(k_s * south_of(s, jnp.zeros((1, 128), F32)))
        rhat = jnp.concatenate(rhat, axis=0)
        west = jnp.concatenate(west, axis=0)
        south = jnp.concatenate(south, axis=0)
        state[j, 0:128, :] = west
        state[j, 128:256, :] = south
        state[j, 256:384, :] = jnp.concatenate(diag, axis=0)
        state[j, 384:512, :] = rhat
        state[j, 512:576, :] = turn
        y = relax(rhat, weight[j], west, south, turn)
        z0 = jnp.concatenate(scale, axis=0) * y
        state[j, 576:704, :] = z0
        put_columns(acc_z, z0, j)
        put_rows(message_ref, z0, 16 * j)

    def body(i, carry):
        for k in range(LONG):
            one(i * LONG + k)
        return carry

    lax.fori_loop(0, PAIRS // LONG, body, 0)
    columns_to_message(acc_z, turned, message_ref, 0, 16)
    put_extras(codes, turned, message_ref, 8, 16)


def local_part(state, local, edges_ref, acc, turned):
    def body(i, carry):
        for k in range(CHUNK):
            j = i * CHUNK + k
            diag = state[j, 256:384, :]
            root = diag * lax.rsqrt(diag)
            rhat = state[j, 384:512, :]
            y0 = root * state[j, 576:704, :]
            local[j] = tile_part(y0, state[j, 0:128, :], state[j, 128:256, :], state[j, 512:576, :]) - rhat
            r = root * rhat
            put_columns(acc, r, j)
            put_rows(edges_ref, r, 8 * j)
        return carry

    lax.fori_loop(0, CHUNKS, body, 0)
    columns_to_message(acc, turned, edges_ref, 0, 8)


def owner_sums(state, d_ref, p_ref, sums_ref):
    def body(i, carry):
        totals = [jnp.zeros((8, 128), F32) for _ in range(6)]
        for k in range(CHUNK):
            j = i * CHUNK + k
            diag = state[j, 256:384, :]
            r = diag * lax.rsqrt(diag) * state[j, 384:512, :]
            d, p = d_ref[j], p_ref[j]
            for index, (left, right) in enumerate(((r, r), (r, d), (d, d), (r, p), (d, p), (p, p))):
                product = left * right
                for n in range(16):
                    totals[index] = totals[index] + product[8 * n : 8 * n + 8]
        for index in range(6):
            sums_ref[index] += totals[index]
        return carry

    sums_ref[...] = jnp.zeros((6, 8, 128), F32)
    lax.fori_loop(0, CHUNKS, body, 0)


def second_step(
    codes, halo_ref, state, local, weight,
    z1s, d_ref, p_ref, message_ref,
    acc_z, acc_p, acc_d, hv, turned,
):
    message_to_columns(halo_ref, turned, hv, 0, 16)
    lane = iota((128, 128), 1) % 64
    at_side = (lane == 0) | (lane == 63)
    first, last = iota((8, 128), 0) == 0, iota((8, 128), 0) == 7

    def one(j):
        west, south, turn = state[j, 0:128, :], state[j, 128:256, :], state[j, 512:576, :]
        diag = state[j, 256:384, :]
        scale = lax.rsqrt(diag)
        root = diag * scale
        what = local[j] - jnp.where(at_side, scale * get_columns(hv[...], j), 0.0)
        rows = halo_ref[pl.ds(pl.multiple_of(16 * j, 16), 8), :]
        fixed = []
        for c in range(2):
            part = what[64 * c : 64 * c + 64]
            s = scale[64 * c : 64 * c + 64]
            low = part[:8] - jnp.where(first, s[:8] * rows[4 + 2 * c : 5 + 2 * c], 0.0)
            high = part[56:] - jnp.where(last, s[56:] * rows[5 + 2 * c : 6 + 2 * c], 0.0)
            fixed += [low, part[8:56], high]
        dhat = jnp.concatenate(fixed, axis=0)
        y1 = relax(dhat, weight[j], west, south, turn)
        phat = tile_part(y1, west, south, turn) - dhat
        z1 = scale * y1
        z1s[j] = z1
        d, p = root * dhat, root * phat
        d_ref[j] = d
        p_ref[j] = p
        for k, (acc, x) in enumerate(((acc_z, z1), (acc_p, p), (acc_d, d))):
            put_columns(acc, x, j)
            put_rows(message_ref, x, 32 * j + 8 * k)

    def body(i, carry):
        for k in range(LONG):
            one(i * LONG + k)
        return carry

    lax.fori_loop(0, PAIRS // LONG, body, 0)
    columns_to_message(acc_p, turned, message_ref, 8, 32)
    columns_to_message(acc_d, turned, message_ref, 16, 32)
    columns_to_message(acc_z, turned, message_ref, 0, 32)
    put_extras(codes, turned, message_ref, 24, 32)


def to_normal(x, r):
    row = iota((8, 128), 0)
    return jnp.where(r == 1, jnp.where(row < 4, roll(x, 6, 0), roll(x, 64, 1)), x)


def halo_of(west, east, south, north):
    row = iota((8, 128), 0)
    side = jnp.where(row == 0, roll(west, 7, 0), roll(east, 1, 0))
    end = jnp.where(row % 2 == 0, roll(south, 7, 0), roll(north, 1, 0))
    return jnp.where(row < 2, side, jnp.where(row >= 4, end, 0.0))


def tile_block(arrival, received_ref, t, k):
    at = arrival[t]
    return to_normal(received_ref[at // 2, 8 * k : 8 * k + 8, :], at % 2)


def boundary(arrival, received_ref, south_ref, north_ref):
    for k in range(south_ref.shape[1] // 8):
        rows = slice(8 * k, 8 * k + 8)
        for x in range(8):
            south_ref[x, rows, :] = tile_block(arrival, received_ref, x, k)
            north_ref[x, rows, :] = tile_block(arrival, received_ref, 24 + x, k)


def tile_halos(arrival, received_ref, from_south, from_north, k, extra):
    group = lax.axis_index("grp")
    blocks = [tile_block(arrival, received_ref, t, k) for t in range(TILES)]
    sides = received_ref[0, 8 * extra : 8 * extra + 8, :]
    for o in range(1, PAIRS):
        sides = sides + received_ref[o, 8 * extra : 8 * extra + 8, :]
    rows = slice(8 * k, 8 * k + 8)
    last = lax.axis_size("grp") - 1
    below = [jnp.where(group > 0, from_south[x, rows, :], 0.0) for x in range(8)]
    above = [jnp.where(group < last, from_north[x, rows, :], 0.0) for x in range(8)]
    halos = []
    for t in range(TILES):
        ty, tx = t // 8, t % 8
        halos.append(
            halo_of(
                blocks[t - 1] if tx > 0 else roll(sides, (1 - ty) % 8, 0),
                blocks[t + 1] if tx < 7 else roll(sides, 4 - ty, 0),
                blocks[t - 8] if ty > 0 else below[tx],
                blocks[t + 8] if ty < 3 else above[tx],
            )
        )
    return blocks, halos


def hand_back(arrival, t, k, halo, out_ref):
    at = arrival[t]
    r = at % 2
    row, lane = iota((8, 128), 0), iota((8, 128), 1)
    placed = jnp.where(r == 1, jnp.where(row < 4, roll(halo, 2, 0), roll(halo, 64, 1)), halo)
    mine = ((row < 4) & (row // 2 == r)) | ((row >= 4) & (lane // 64 == r))
    rows = slice(8 * k, 8 * k + 8)
    out_ref[at // 2, rows, :] += jnp.where(mine, placed, 0.0)


def first_return(arrival, received_ref, south, north, out_ref, face_ref):
    row, lane = iota((8, 128), 0), iota((8, 128), 1)
    along_x = jnp.where(lane < 64, KX[0], KX[1])
    along_y = jnp.where(row < 6, KY[0], KY[1])
    factor = 0.5 * jnp.where(row < 4, along_x, along_y)
    out_ref[...] = jnp.zeros(out_ref.shape, F32)
    for k in range(2):
        blocks, halos = tile_halos(arrival, received_ref, south, north, k, 2 + k)
        for t in range(TILES):
            hand_back(arrival, t, k, halos[t], out_ref)
            if k == 1:
                face_ref[t] = factor * (blocks[t] + halos[t])


def second_return(arrival, received_ref, south, north, edges_ref, face_ref, out_ref):
    out_ref[:, 0:8, :] = jnp.zeros((PAIRS, 8, 128), F32)
    out_ref[:, 8:16, :] = edges_ref[...]
    blocks, halos = tile_halos(arrival, received_ref, south, north, 0, 1)
    for t in range(TILES):
        hand_back(arrival, t, 0, face_ref[t] * halos[t], out_ref)


def edge_sums(arrival, received_ref, south, north, earlier_ref, face_ref, sums_ref, out_ref):
    row, lane = iota((8, 128), 0), iota((8, 128), 1)
    valid = (row < 2) | ((row >= 4) & (lane < 64))
    total_r = jnp.zeros((8, 128), F32)
    total_d = jnp.zeros((8, 128), F32)
    total_p = jnp.zeros((8, 128), F32)
    blocks, halos = tile_halos(arrival, received_ref, south, north, 0, 3)
    for t in range(TILES):
        h = jnp.where(valid, -face_ref[t] * halos[t], 0.0)
        p = tile_block(arrival, received_ref, t, 1)
        d = tile_block(arrival, received_ref, t, 2)
        r = tile_block(arrival, earlier_ref, t, 1)
        total_r = total_r + jnp.where(valid, h * r, 0.0)
        total_d = total_d + jnp.where(valid, h * d, 0.0)
        wide_w = jnp.broadcast_to(h[0:1], (8, 128))
        wide_e = jnp.broadcast_to(h[1:2], (8, 128))
        corner_w = jnp.where(
            row == 4, wide_w,
            jnp.where(row == 5, roll(wide_w, 65, 1), jnp.where(row == 6, roll(wide_w, 64, 1), roll(wide_w, 1, 1))),
        )
        corner_e = jnp.where(
            row == 4, roll(wide_e, 63, 1),
            jnp.where(row == 5, wide_e, jnp.where(row == 6, roll(wide_e, 127, 1), roll(wide_e, 64, 1))),
        )
        corner = jnp.where(lane == 0, corner_w, jnp.where(lane == 63, corner_e, 0.0))
        corner = jnp.where(row >= 4, corner, 0.0)
        total_p = total_p + jnp.where(valid, h * (2.0 * (p + corner) + h), 0.0)
    lane = iota((1, 128), 1)
    out = jnp.zeros((1, 128), F32)
    for index in range(6):
        total = sums_ref[index]
        if index == 3:
            total = total + total_r
        if index == 4:
            total = total + total_d
        if index == 5:
            total = total + total_p
        value = jnp.sum(jnp.sum(total, axis=0, keepdims=True), axis=1, keepdims=True)
        out = jnp.where(lane == index, value, out)
    out_ref[...] = jnp.broadcast_to(out, (128, 128))


def least_squares(magnitude, upper_first, below_first, upper_cross, upper_second, below_second):
    radius_first = jnp.sqrt(upper_first * upper_first + below_first * below_first)
    cosine_first = upper_first / radius_first
    sine_first = below_first / radius_first
    lifted_top = cosine_first * upper_cross + sine_first * upper_second
    lifted_low = cosine_first * upper_second - sine_first * upper_cross
    radius_second = jnp.sqrt(lifted_low * lifted_low + below_second * below_second)
    weight_second = -(sine_first * magnitude) * (lifted_low / radius_second) / radius_second
    weight_first = (cosine_first * magnitude - lifted_top * weight_second) / radius_first
    return (weight_first, weight_second)


def final_weights(gathered):
    total = jnp.sum(gathered, axis=0, keepdims=True)
    lane = iota((1, 128), 1)
    rr, rd, dd, re, de, ee = [
        jnp.sum(jnp.where(lane == index, total, 0.0), axis=1, keepdims=True) for index in range(6)
    ]
    square = rr + EPSILON
    magnitude = jnp.sqrt(square)
    h11 = (rr + rd) / square
    gap = -(rd - EPSILON) / square
    h21_square = jnp.maximum((dd + 2.0 * gap * rd + gap * gap * rr) / square, 0.0) + EPSILON
    h21 = jnp.sqrt(h21_square)
    unit = 1.0 / (magnitude * h21)
    h12 = (gap * rr + (1.0 + gap) * rd + re) * unit / magnitude
    h22 = (
        gap * (gap * rr + rd) + (1.0 + gap) * (gap * rd + dd) + (gap * re + de)
    ) * unit * unit
    c_r = gap * unit - h12 / magnitude - h22 * gap * unit
    c_d = (1.0 + gap - h22) * unit
    c_e = unit
    h32_square = (
        c_r * c_r * rr + c_d * c_d * dd + c_e * c_e * ee
        + 2.0 * (c_r * c_d * rd + c_r * c_e * re + c_d * c_e * de)
    )
    h32 = jnp.sqrt(jnp.maximum(h32_square, 0.0) + EPSILON)
    y1, y2 = least_squares(magnitude, h11, h21, h12, h22, h32)
    return y1 / magnitude + y2 * gap * unit, y2 * unit


def last_step(
    table, gathered_ref, pairs, state, z1,
    out_hbm,
    out, sem_out,
):
    out[...] = jnp.zeros(out.shape, F32)
    weight0, weight1 = final_weights(gathered_ref[...])

    def body(i, carry):
        for k in range(CHUNK):
            j = i * CHUNK + k
            new = pairs[j, 0:128, :] + weight0 * state[j, 576:704, :] + weight1 * z1[j]
            slots = [jnp.where(table[2 * j + r] >= 0, table[2 * j + r], SLOTS) for r in range(2)]
            for c in range(2):
                for r, x in enumerate(split_up(new[64 * c : 64 * c + 64])):
                    for q in range(4):
                        out[slots[r], pl.ds(c + 2 * q, 8, stride=8), :] = x[8 * q : 8 * q + 8]
        return carry

    lax.fori_loop(0, CHUNKS, body, 0)
    copy = pltpu.make_async_copy(out.at[pl.ds(0, SLOTS)], out_hbm, sem_out)
    copy.start()
    copy.wait()


def call(kernel, outs, specs, scratch=(), out_specs=None, mebibytes=4):
    return pl.pallas_call(
        kernel,
        out_shape=outs,
        in_specs=specs,
        out_specs=out_specs if out_specs is not None else jax.tree.map(lambda _: vmem(), outs),
        scratch_shapes=list(scratch),
        compiler_params=params(mebibytes),
    )


def hbm():
    return pl.BlockSpec(memory_space=pl.ANY)


def square(rows=128):
    return pltpu.VMEM((rows, 128), F32)


def buffer(*shape, dtype=F32):
    return pltpu.VMEM(shape, dtype)


def sems(*shape):
    return pltpu.SemaphoreType.DMA(shape)


def vector_view(x):
    return x.reshape(64, 2, 32, 128).transpose(0, 2, 1, 3).reshape(64, 64, 128)


def field_view(x):
    return x.reshape(8, 8, 32, 128).transpose(0, 2, 1, 3).reshape(8, 256, 128)


def exchange(x):
    return lax.all_to_all(x, "dev", split_axis=0, concat_axis=0, tiled=True)


def boundaries(arrival, received, count):
    side = struct(8, 8 * count, 128)
    return call(boundary, (side, side), [smem(), vmem()])(arrival, received)


def from_groups(south, north):
    size = lax.axis_size("grp")
    ahead = [(i, (i + 1) % size) for i in range(size)]
    return lax.ppermute(north, "grp", ahead), lax.ppermute(south, "grp", [(j, i) for i, j in ahead])


def shards(velocity, forcing, mass, coriolis, viscosity, lines, tile_source_slot, ocean_tile):
    u, b = vector_view(velocity), vector_view(forcing)
    a, f, z, p = [field_view(x) for x in (mass, coriolis, viscosity, lines)]

    tiles, vectors = resident(8, 256, 128), resident(64, 64, 128)
    message, table, codes, arrival, pairs, p, b, a, f = call(
        first_edges,
        (
            struct(PAIRS * 32, 128), struct(TABLE, dtype=jnp.int32), struct(CODES, dtype=jnp.int32),
            struct(TILES + 8, dtype=jnp.int32), resident(PAIRS, 192, 128), tiles, vectors, tiles, tiles,
        ),
        [smem(), smem()] + [hbm()] * 6,
        [
            buffer(64, 64, 128), buffer(8, 256, 128), square(), square(), square(),
            pltpu.SMEM((PAIRS + 8,), jnp.int32), pltpu.SMEM((PAIRS,), jnp.int32), sems(6),
        ],
        (vmem(), smem(), smem(), smem()) + (vmem(),) * 5,
        8,
    )(*[kept(x) for x in (ocean_tile, tile_source_slot, u, z, p, b, a, f)])

    received = exchange(message.reshape(PAIRS, 32, 128))
    south, north = boundaries(arrival, received, 2)
    south, north, p = lax.optimization_barrier((south, north, p))
    weight, fields = call(
        prepare, (resident(PAIRS, 128, 256, dtype=BF16), resident(PAIRS, 128, 128)), [smem()] + [vmem()] * 3,
        [buffer(CHUNK, 128, 128)],
    )(table, held(p), held(a), held(f))
    halo, face = call(
        first_return, (struct(PAIRS, 16, 128), struct(TILES, 8, 128)), [smem()] + [vmem()] * 3
    )(arrival, received, *from_groups(south, north))
    halo, weight, fields = lax.optimization_barrier((halo, weight, fields))
    halo = exchange(halo).reshape(PAIRS * 16, 128)

    state, message = call(
        first_step,
        (resident(PAIRS, STATE, 128), struct(PAIRS * 16, 128)),
        [smem()] * 2 + [vmem()] * 5,
        [square()] * 4,
        mebibytes=8,
    )(table, codes, halo, held(pairs), held(b), held(fields), held(weight))
    received = exchange(message.reshape(PAIRS, 16, 128))
    south, north = boundaries(arrival, received, 1)
    south, north, state = lax.optimization_barrier((south, north, state))
    whole = resident(PAIRS, 128, 128)
    local, edges = call(
        local_part, (whole, struct(PAIRS * 8, 128)), [vmem()], [square(), square()]
    )(held(state))
    halo = call(second_return, struct(PAIRS, 16, 128), [smem()] + [vmem()] * 5)(
        arrival, received, *from_groups(south, north), edges.reshape(PAIRS, 8, 128), face
    )
    halo, local = lax.optimization_barrier((halo, local))
    earlier = exchange(halo)
    halo = earlier.reshape(PAIRS * 16, 128)

    z1, d, p, message = call(
        second_step,
        (whole, whole, whole, struct(PAIRS * 32, 128)),
        [smem()] + [vmem()] * 4,
        [square()] * 5,
        mebibytes=8,
    )(codes, halo, held(state), held(local), held(weight))
    received = exchange(message.reshape(PAIRS, 32, 128))
    south, north = boundaries(arrival, received, 1)
    south, north, d = lax.optimization_barrier((south, north, d))
    sums = call(owner_sums, struct(6, 8, 128), [vmem()] * 3)(held(state), held(d), held(p))
    partial = call(edge_sums, struct(128, 128), [smem()] + [vmem()] * 6)(
        arrival, received, *from_groups(south, north), earlier, face, sums
    )
    gathered = lax.all_to_all(partial, ("grp", "dev"), split_axis=0, concat_axis=0, tiled=True)

    out = call(
        last_step, struct(SLOTS, 64, 128), [smem()] + [vmem()] * 4,
        [buffer(SLOTS + 1, 64, 128), pltpu.SemaphoreType.DMA],
        hbm(),
        8,
    )(table, gathered, held(pairs), held(state), held(z1))
    return out.reshape(64, 32, 2, 128).transpose(0, 2, 1, 3).reshape(64, 2, 4096)


def solution(mesh):
    return jax.shard_map(
        shards,
        mesh=mesh,
        in_specs=(
            P(("grp", "dev"), None, None),
            P(("grp", "dev"), None, None),
            P(("grp", "dev"), None),
            P(("grp", "dev"), None),
            P(("grp", "dev"), None),
            P(("grp", "dev"), None),
            P(("grp", "dev")),
            P(("grp", "dev")),
        ),
        out_specs=P(("grp", "dev"), None, None),
        check_vma=False,
    )
```

```python
import jax
import jax.numpy as jnp
from jax import lax
from jax.experimental import pallas as pl
from jax.experimental.pallas import tpu as pltpu
from jax.sharding import PartitionSpec as P

F32 = jnp.float32
BF16 = jnp.bfloat16
SLOTS = 64
PAIRS = 32
TILES = 32
CHUNK = 8
MIDDLE = 16
LONG = 32
CHUNKS = PAIRS // CHUNK
TABLE = 72
CODES = 144
STATE = 704
EPSILON = 1e-06


def params(mebibytes):
    return pltpu.CompilerParams(vmem_limit_bytes=mebibytes * 1024 * 1024)


def vmem():
    return pl.BlockSpec(memory_space=pltpu.VMEM)


def smem():
    return pl.BlockSpec(memory_space=pltpu.SMEM)


def struct(*shape, dtype=F32):
    return jax.ShapeDtypeStruct(shape, dtype)


def resident(*shape, dtype=F32):
    return pltpu.VMEM(shape, dtype)


def held(x):
    return pltpu.with_memory_space_constraint(x, pltpu.VMEM)


def kept(x):
    return pltpu.with_memory_space_constraint(x, pltpu.HBM)


def iota(shape, dim):
    return lax.broadcasted_iota(jnp.int32, shape, dim)


def roll(x, shift, axis):
    return pltpu.roll(x, shift, axis)


def pair_up(t0, t1):
    low = iota(t0.shape, 1) < 64
    crossed = roll(jnp.where(low, t1, t0), 64, 1)
    return jnp.concatenate([jnp.where(low, t0, crossed), jnp.where(low, crossed, t1)], axis=0)


def split_up(q):
    even, odd = q[:32], q[32:]
    low = iota(even.shape, 1) < 64
    crossed = roll(jnp.where(low, odd, even), 64, 1)
    return jnp.where(low, even, crossed), jnp.where(low, crossed, odd)


def load_tile(ref, index, offset, step):
    rows = [ref[index, pl.ds(offset + step * q, 8, stride=4 * step), :] for q in range(4)]
    return jnp.concatenate(rows, axis=0)


def load_field(ref, table, j, empty):
    tiles = []
    for r in range(2):
        s = table[2 * j + r]
        t = jnp.maximum(s, 0)
        tiles.append(jnp.where(s >= 0, load_tile(ref, t // 8, t % 8, 8), empty))
    return pair_up(*tiles)


def load_vector(ref, table, j):
    parts = []
    for c in range(2):
        tiles = []
        for r in range(2):
            s = table[2 * j + r]
            tiles.append(jnp.where(s >= 0, load_tile(ref, jnp.maximum(s, 0), c, 2), 0.0))
        parts.append(pair_up(*tiles))
    return parts


def put_columns(acc_ref, x, j):
    mine = ((iota(x.shape, 1) % 64) // 2) == j
    pltpu.store(acc_ref.at[pl.ds(0, x.shape[0])], roll(x, 2 * j + 1, 1), mask=mine)


def get_columns(acc, j):
    return roll(acc, 128 - (2 * j + 1), 1)


COLUMN_ROWS = (1, 64, 65, 0)


def columns_to_message(acc_ref, turned_ref, message_ref, first, stride):
    turned_ref[...] = acc_ref[...].T
    for row, source in enumerate(COLUMN_ROWS):
        message_ref[pl.ds(first + row, 32, stride=stride), :] = turned_ref[pl.ds(source, 32, stride=2), :]


def message_to_columns(message_ref, turned_ref, acc_ref, first, stride):
    for row, source in enumerate(COLUMN_ROWS):
        turned_ref[pl.ds(source, 32, stride=2), :] = message_ref[pl.ds(first + row, 32, stride=stride), :]
    acc_ref[...] = turned_ref[...].T


def put_rows(message_ref, x, base):
    for row, source in enumerate((0, 63, 64, 127)):
        message_ref[pl.ds(base + 4 + row, 1), :] = x[source : source + 1, :]


def south_of(x, halo=None):
    even, odd = x[:32], x[32:]
    below = roll(odd[24:], 1, 0)
    if halo is not None:
        below = jnp.where(iota(below.shape, 0) == 0, halo, below)
    return jnp.concatenate([below, odd[:24], even], axis=0)


def north_of(x, halo=None):
    even, odd = x[:32], x[32:]
    above = roll(even[:8], 7, 0)
    if halo is not None:
        above = jnp.where(iota(above.shape, 0) == 7, halo, above)
    return jnp.concatenate([odd, even[8:], above], axis=0)


def tile_part(y, west, south, turn):
    parts = []
    for c in range(2):
        rows = slice(64 * c, 64 * c + 64)
        x, w, s = y[rows], west[rows], south[rows]
        even, odd = x[:32], x[32:]
        s_even, s_odd = s[:32], s[32:]
        across = w * roll(x, 1, 1) + roll(w * x, 127, 1)
        up = s_even * even
        along = jnp.concatenate(
            [
                s_even[:8] * roll(odd[24:], 1, 0) + s_odd[:8] * odd[:8],
                s_even[8:] * odd[:24] + s_odd[8:] * odd[8:],
                s_odd[:24] * even[:24] + up[8:],
                s_odd[24:] * even[24:] + roll(up[:8], 7, 0),
            ],
            axis=0,
        )
        other = y[64:] if c == 0 else y[:64]
        spin = turn * other
        parts.append(x - across - along - spin if c == 0 else x - across - along + spin)
    return jnp.concatenate(parts, axis=0)


def line_solve(t, weight):
    high = t.astype(BF16)
    low = (t - high.astype(F32)).astype(BF16)
    out = lax.dot_general(
        jnp.concatenate([high, low], axis=1),
        jnp.concatenate([weight, weight], axis=0),
        (((1,), (0,)), ((), ())),
        preferred_element_type=F32,
    )
    return out[:, :128] + out[:, 128:]


def relax(q, weight, west, south, turn):
    y = line_solve(q, weight)
    for _ in range(2):
        y = y + line_solve(q - tile_part(y, west, south, turn), weight)
    return y


NONE = 99
CODE_W = 72


def make_table(ocean, table, count):
    def clear(i, carry):
        table[i] = -1
        return carry

    def clear_count(i, carry):
        count[i] = 0
        return carry

    def place(s, carry):
        t = ocean[s]
        j = jnp.where(t >= 0, (t >> 5) & 31, PAIRS)
        held = count[j] & 1
        table[2 * j + held] = s
        count[j] = held + 1
        return carry

    lax.fori_loop(0, TABLE, clear, 0, unroll=8)
    lax.fori_loop(0, PAIRS + 8, clear_count, 0, unroll=8)
    lax.fori_loop(0, SLOTS, place, 0, unroll=8)


def column_codes(ocean, table, codes, j):
    for r in range(2):
        p = 2 * j + r
        s = table[p]
        t = ocean[jnp.maximum(s, 0)]
        column, row = t & 7, (t >> 3) & 3
        codes[p + 2] = jnp.where((s >= 0) & (column == 7), row, NONE)
        codes[CODE_W + p] = jnp.where((s >= 0) & (column == 0), row + 4, NONE)


def land(source, arrival, first, t):
    slot = source[t]
    owner = (slot >> 6) & 31
    held = first[owner]
    later = (held >= 0) & (source[jnp.maximum(held, 0)] < slot)
    arrival[t] = 2 * owner + later.astype(jnp.int32)
    other = jnp.where(held >= 0, held, TILES)
    arrival[other] = 2 * owner + 1 - later.astype(jnp.int32)
    first[owner] = t


def put_extras(codes, turned, message_ref, first, stride):
    row = iota((8, 128), 0)

    def body(m, carry):
        before, after = 2 * jnp.maximum(m - 1, 0), 2 * jnp.minimum(m + 1, PAIRS - 1)
        total = jnp.zeros((8, 128), F32)
        for r in range(2):
            east = turned[pl.ds(before + (64, 0)[r], 1), :]
            west = turned[pl.ds(after + (1, 65)[r], 1), :]
            total = jnp.where(row == codes[2 * m + r], east, total)
            total = jnp.where(row == codes[CODE_W + 2 * m + 2 + r], west, total)
        message_ref[pl.ds(pl.multiple_of(m * stride + first, 8), 8), :] = total
        return carry

    lax.fori_loop(0, PAIRS, body, 0, unroll=8)


def first_edges(
    ocean, source, u_hbm, z_hbm, p_hbm, b_hbm, a_hbm, f_hbm,
    message_ref, table, codes, arrival, pairs, p_ref, b_ref, a_ref, f_ref,
    u_ref, z_ref, acc_v, acc_z, turned, count, landed, sem_in,
):
    z_copy = pltpu.make_async_copy(z_hbm, z_ref, sem_in.at[0])
    u_copy = pltpu.make_async_copy(u_hbm, u_ref, sem_in.at[1])
    z_copy.start()
    u_copy.start()
    make_table(ocean, table, count)
    for i in (0, 1, CODE_W + 64, CODE_W + 65):
        codes[i] = NONE
    for i in range(PAIRS):
        landed[i] = -1
    z_copy.wait()

    def scalars(i, carry):
        for k in range(CHUNK):
            j = i * CHUNK + k
            z = load_field(z_ref, table, j, 0.0)
            pairs[j, 128:192, :] = z
            put_columns(acc_z, z, j)
            put_rows(message_ref, jnp.concatenate([z, z], axis=0), 32 * j + 8)
            column_codes(ocean, table, codes, j)
        return carry

    def vectors(i, carry):
        for k in range(CHUNK):
            j = i * CHUNK + k
            u, v = load_vector(u_ref, table, j)
            vector = jnp.concatenate([u, v], axis=0)
            pairs[j, 0:128, :] = vector
            put_columns(acc_v, vector, j)
            put_rows(message_ref, vector, 32 * j)
            land(source, arrival, landed, j)
        return carry

    lax.fori_loop(0, CHUNKS, scalars, 0)
    u_copy.wait()
    later = [
        pltpu.make_async_copy(origin, target, sem_in.at[2 + n])
        for n, (origin, target) in enumerate(
            ((p_hbm, p_ref), (b_hbm, b_ref), (a_hbm, a_ref), (f_hbm, f_ref))
        )
    ]
    for copy in later:
        copy.start()
    lax.fori_loop(0, CHUNKS, vectors, 0)
    columns_to_message(acc_v, turned, message_ref, 0, 32)
    put_extras(codes, turned, message_ref, 16, 32)
    acc_z[64:128, :] = acc_z[0:64, :]
    columns_to_message(acc_z, turned, message_ref, 8, 32)
    put_extras(codes, turned, message_ref, 24, 32)
    for copy in later:
        copy.wait()


def prepare(table, p_ref, a_ref, f_ref, weight, fields, natural):
    low = iota((32, 128), 1) < 64

    def lines(i, carry):
        for k in range(MIDDLE):
            j = i * MIDDLE + k
            tiles = []
            for r in range(2):
                s = table[2 * j + r]
                t = jnp.maximum(s, 0)
                x = p_ref[t // 8, pl.ds(t % 8, 32, stride=8), :]
                tiles.append(jnp.where(s >= 0, x, 0.0))
            t0, t1 = tiles
            crossed = roll(jnp.where(low, t1, t0), 64, 1)
            natural[k, pl.ds(0, 32, stride=2), :] = jnp.where(low, t0, 0.0)
            natural[k, pl.ds(1, 32, stride=2), :] = jnp.where(low, crossed, 0.0)
            natural[k, pl.ds(64, 32, stride=2), :] = jnp.where(low, 0.0, crossed)
            natural[k, pl.ds(65, 32, stride=2), :] = jnp.where(low, 0.0, t1)
            turned = natural[k].T
            high = turned.astype(BF16)
            weight[j, :, 0:128] = high
            weight[j, :, 128:256] = (turned - high.astype(F32)).astype(BF16)
            fields[j, 0:64, :] = load_field(a_ref, table, j, 1.0)
            fields[j, 64:128, :] = load_field(f_ref, table, j, 0.0)
        return carry

    lax.fori_loop(0, PAIRS // MIDDLE, lines, 0)


def side_masks():
    x = iota((64, 128), 1) % 64
    return x == 0, x == 63


KX = (1.25, 0.25)
KY = (0.25, 1.25)


def first_step(
    table, codes, halo_ref, pairs, b_ref, fields, weight,
    state, message_ref,
    acc_z, hv, hz, turned,
):
    message_to_columns(halo_ref, turned, hv, 0, 16)
    message_to_columns(halo_ref, turned, hz, 8, 16)
    at_west, at_east = side_masks()

    def one(j):
        u0 = pairs[j, 0:64, :], pairs[j, 64:128, :]
        z = pairs[j, 128:192, :]
        b = load_vector(b_ref, table, j)
        a, f = fields[j, 0:64, :], fields[j, 64:128, :]
        side_v = get_columns(hv[...], j)
        side_z = get_columns(hz[0:64, :], j)
        rows = halo_ref[pl.ds(pl.multiple_of(16 * j, 16), 16), :]
        face_w = 0.5 * (z + jnp.where(at_west, side_z, roll(z, 1, 1)))
        face_e = 0.5 * (z + jnp.where(at_east, side_z, roll(z, 127, 1)))
        face_s = 0.5 * (z + south_of(z, rows[12:13]))
        face_n = 0.5 * (z + north_of(z, rows[13:14]))
        scale, diag = [], []
        for c in range(2):
            d = a + KX[c] * (face_w + face_e) + KY[c] * (face_s + face_n)
            diag.append(d)
            scale.append(lax.rsqrt(d))
        turn = f * scale[0] * scale[1]
        rhat, west, south = [], [], []
        for c in range(2):
            x, s = u0[c], scale[c]
            side = side_v[64 * c : 64 * c + 64]
            x_w = jnp.where(at_west, side, roll(x, 1, 1))
            x_e = jnp.where(at_east, side, roll(x, 127, 1))
            x_s = south_of(x, rows[4 + 2 * c : 5 + 2 * c])
            x_n = north_of(x, rows[5 + 2 * c : 6 + 2 * c])
            spin = -f * u0[1] if c == 0 else f * u0[0]
            applied = (
                diag[c] * x + spin
                - KX[c] * (face_w * x_w + face_e * x_e)
                - KY[c] * (face_s * x_s + face_n * x_n)
            )
            rhat.append(s * (b[c] - applied))
            k_w = KX[c] * s * face_w
            k_s = KY[c] * s * face_s
            west.append(jnp.where(at_west, 0.0, k_w * roll(s, 1, 1)))
            south.append(k_s * south_of(s, jnp.zeros((1, 128), F32)))
        rhat = jnp.concatenate(rhat, axis=0)
        west = jnp.concatenate(west, axis=0)
        south = jnp.concatenate(south, axis=0)
        state[j, 0:128, :] = west
        state[j, 128:256, :] = south
        state[j, 256:384, :] = jnp.concatenate(diag, axis=0)
        state[j, 384:512, :] = rhat
        state[j, 512:576, :] = turn
        y = relax(rhat, weight[j], west, south, turn)
        z0 = jnp.concatenate(scale, axis=0) * y
        state[j, 576:704, :] = z0
        put_columns(acc_z, z0, j)
        put_rows(message_ref, z0, 16 * j)

    def body(i, carry):
        for k in range(LONG):
            one(i * LONG + k)
        return carry

    lax.fori_loop(0, PAIRS // LONG, body, 0)
    columns_to_message(acc_z, turned, message_ref, 0, 16)
    put_extras(codes, turned, message_ref, 8, 16)


def local_part(state, local, edges_ref, acc, turned):
    def body(i, carry):
        for k in range(CHUNK):
            j = i * CHUNK + k
            diag = state[j, 256:384, :]
            root = diag * lax.rsqrt(diag)
            rhat = state[j, 384:512, :]
            y0 = root * state[j, 576:704, :]
            local[j] = tile_part(y0, state[j, 0:128, :], state[j, 128:256, :], state[j, 512:576, :]) - rhat
            r = root * rhat
            put_columns(acc, r, j)
            put_rows(edges_ref, r, 8 * j)
        return carry

    lax.fori_loop(0, CHUNKS, body, 0)
    columns_to_message(acc, turned, edges_ref, 0, 8)


def owner_sums(state, d_ref, p_ref, sums_ref):
    def body(i, carry):
        totals = [jnp.zeros((8, 128), F32) for _ in range(6)]
        for k in range(CHUNK):
            j = i * CHUNK + k
            diag = state[j, 256:384, :]
            r = diag * lax.rsqrt(diag) * state[j, 384:512, :]
            d, p = d_ref[j], p_ref[j]
            for index, (left, right) in enumerate(((r, r), (r, d), (d, d), (r, p), (d, p), (p, p))):
                product = left * right
                for n in range(16):
                    totals[index] = totals[index] + product[8 * n : 8 * n + 8]
        for index in range(6):
            sums_ref[index] += totals[index]
        return carry

    sums_ref[...] = jnp.zeros((6, 8, 128), F32)
    lax.fori_loop(0, CHUNKS, body, 0)


def second_step(
    codes, halo_ref, state, local, weight,
    z1s, d_ref, p_ref, message_ref,
    acc_z, acc_p, acc_d, hv, turned,
):
    message_to_columns(halo_ref, turned, hv, 0, 16)
    lane = iota((128, 128), 1) % 64
    at_side = (lane == 0) | (lane == 63)
    first, last = iota((8, 128), 0) == 0, iota((8, 128), 0) == 7

    def one(j):
        west, south, turn = state[j, 0:128, :], state[j, 128:256, :], state[j, 512:576, :]
        diag = state[j, 256:384, :]
        scale = lax.rsqrt(diag)
        root = diag * scale
        what = local[j] - jnp.where(at_side, scale * get_columns(hv[...], j), 0.0)
        rows = halo_ref[pl.ds(pl.multiple_of(16 * j, 16), 8), :]
        fixed = []
        for c in range(2):
            part = what[64 * c : 64 * c + 64]
            s = scale[64 * c : 64 * c + 64]
            low = part[:8] - jnp.where(first, s[:8] * rows[4 + 2 * c : 5 + 2 * c], 0.0)
            high = part[56:] - jnp.where(last, s[56:] * rows[5 + 2 * c : 6 + 2 * c], 0.0)
            fixed += [low, part[8:56], high]
        dhat = jnp.concatenate(fixed, axis=0)
        y1 = relax(dhat, weight[j], west, south, turn)
        phat = tile_part(y1, west, south, turn) - dhat
        z1 = scale * y1
        z1s[j] = z1
        d, p = root * dhat, root * phat
        d_ref[j] = d
        p_ref[j] = p
        for k, (acc, x) in enumerate(((acc_z, z1), (acc_p, p), (acc_d, d))):
            put_columns(acc, x, j)
            put_rows(message_ref, x, 32 * j + 8 * k)

    def body(i, carry):
        for k in range(LONG):
            one(i * LONG + k)
        return carry

    lax.fori_loop(0, PAIRS // LONG, body, 0)
    columns_to_message(acc_p, turned, message_ref, 8, 32)
    columns_to_message(acc_d, turned, message_ref, 16, 32)
    columns_to_message(acc_z, turned, message_ref, 0, 32)
    put_extras(codes, turned, message_ref, 24, 32)


def to_normal(x, r):
    row = iota((8, 128), 0)
    return jnp.where(r == 1, jnp.where(row < 4, roll(x, 6, 0), roll(x, 64, 1)), x)


def halo_of(west, east, south, north):
    row = iota((8, 128), 0)
    side = jnp.where(row == 0, roll(west, 7, 0), roll(east, 1, 0))
    end = jnp.where(row % 2 == 0, roll(south, 7, 0), roll(north, 1, 0))
    return jnp.where(row < 2, side, jnp.where(row >= 4, end, 0.0))


def tile_block(arrival, received_ref, t, k):
    at = arrival[t]
    return to_normal(received_ref[at // 2, 8 * k : 8 * k + 8, :], at % 2)


def boundary(arrival, received_ref, south_ref, north_ref):
    for k in range(south_ref.shape[1] // 8):
        rows = slice(8 * k, 8 * k + 8)
        for x in range(8):
            south_ref[x, rows, :] = tile_block(arrival, received_ref, x, k)
            north_ref[x, rows, :] = tile_block(arrival, received_ref, 24 + x, k)


def tile_halos(arrival, received_ref, from_south, from_north, k, extra):
    group = lax.axis_index("grp")
    blocks = [tile_block(arrival, received_ref, t, k) for t in range(TILES)]
    sides = received_ref[0, 8 * extra : 8 * extra + 8, :]
    for o in range(1, PAIRS):
        sides = sides + received_ref[o, 8 * extra : 8 * extra + 8, :]
    rows = slice(8 * k, 8 * k + 8)
    last = lax.axis_size("grp") - 1
    below = [jnp.where(group > 0, from_south[x, rows, :], 0.0) for x in range(8)]
    above = [jnp.where(group < last, from_north[x, rows, :], 0.0) for x in range(8)]
    halos = []
    for t in range(TILES):
        ty, tx = t // 8, t % 8
        halos.append(
            halo_of(
                blocks[t - 1] if tx > 0 else roll(sides, (1 - ty) % 8, 0),
                blocks[t + 1] if tx < 7 else roll(sides, 4 - ty, 0),
                blocks[t - 8] if ty > 0 else below[tx],
                blocks[t + 8] if ty < 3 else above[tx],
            )
        )
    return blocks, halos


def hand_back(arrival, t, k, halo, out_ref):
    at = arrival[t]
    r = at % 2
    row, lane = iota((8, 128), 0), iota((8, 128), 1)
    placed = jnp.where(r == 1, jnp.where(row < 4, roll(halo, 2, 0), roll(halo, 64, 1)), halo)
    mine = ((row < 4) & (row // 2 == r)) | ((row >= 4) & (lane // 64 == r))
    rows = slice(8 * k, 8 * k + 8)
    out_ref[at // 2, rows, :] += jnp.where(mine, placed, 0.0)


def first_return(arrival, received_ref, south, north, out_ref, face_ref):
    row, lane = iota((8, 128), 0), iota((8, 128), 1)
    along_x = jnp.where(lane < 64, KX[0], KX[1])
    along_y = jnp.where(row < 6, KY[0], KY[1])
    factor = 0.5 * jnp.where(row < 4, along_x, along_y)
    out_ref[...] = jnp.zeros(out_ref.shape, F32)
    for k in range(2):
        blocks, halos = tile_halos(arrival, received_ref, south, north, k, 2 + k)
        for t in range(TILES):
            hand_back(arrival, t, k, halos[t], out_ref)
            if k == 1:
                face_ref[t] = factor * (blocks[t] + halos[t])


def second_return(arrival, received_ref, south, north, edges_ref, face_ref, out_ref):
    out_ref[:, 0:8, :] = jnp.zeros((PAIRS, 8, 128), F32)
    out_ref[:, 8:16, :] = edges_ref[...]
    blocks, halos = tile_halos(arrival, received_ref, south, north, 0, 1)
    for t in range(TILES):
        hand_back(arrival, t, 0, face_ref[t] * halos[t], out_ref)


def edge_sums(arrival, received_ref, south, north, earlier_ref, face_ref, sums_ref, out_ref):
    row, lane = iota((8, 128), 0), iota((8, 128), 1)
    valid = (row < 2) | ((row >= 4) & (lane < 64))
    total_r = jnp.zeros((8, 128), F32)
    total_d = jnp.zeros((8, 128), F32)
    total_p = jnp.zeros((8, 128), F32)
    blocks, halos = tile_halos(arrival, received_ref, south, north, 0, 3)
    for t in range(TILES):
        h = jnp.where(valid, -face_ref[t] * halos[t], 0.0)
        p = tile_block(arrival, received_ref, t, 1)
        d = tile_block(arrival, received_ref, t, 2)
        r = tile_block(arrival, earlier_ref, t, 1)
        total_r = total_r + jnp.where(valid, h * r, 0.0)
        total_d = total_d + jnp.where(valid, h * d, 0.0)
        wide_w = jnp.broadcast_to(h[0:1], (8, 128))
        wide_e = jnp.broadcast_to(h[1:2], (8, 128))
        corner_w = jnp.where(
            row == 4, wide_w,
            jnp.where(row == 5, roll(wide_w, 65, 1), jnp.where(row == 6, roll(wide_w, 64, 1), roll(wide_w, 1, 1))),
        )
        corner_e = jnp.where(
            row == 4, roll(wide_e, 63, 1),
            jnp.where(row == 5, wide_e, jnp.where(row == 6, roll(wide_e, 127, 1), roll(wide_e, 64, 1))),
        )
        corner = jnp.where(lane == 0, corner_w, jnp.where(lane == 63, corner_e, 0.0))
        corner = jnp.where(row >= 4, corner, 0.0)
        total_p = total_p + jnp.where(valid, h * (2.0 * (p + corner) + h), 0.0)
    lane = iota((1, 128), 1)
    out = jnp.zeros((1, 128), F32)
    for index in range(6):
        total = sums_ref[index]
        if index == 3:
            total = total + total_r
        if index == 4:
            total = total + total_d
        if index == 5:
            total = total + total_p
        value = jnp.sum(jnp.sum(total, axis=0, keepdims=True), axis=1, keepdims=True)
        out = jnp.where(lane == index, value, out)
    out_ref[...] = jnp.broadcast_to(out, (128, 128))


def least_squares(magnitude, upper_first, below_first, upper_cross, upper_second, below_second):
    radius_first = jnp.sqrt(upper_first * upper_first + below_first * below_first)
    cosine_first = upper_first / radius_first
    sine_first = below_first / radius_first
    lifted_top = cosine_first * upper_cross + sine_first * upper_second
    lifted_low = cosine_first * upper_second - sine_first * upper_cross
    radius_second = jnp.sqrt(lifted_low * lifted_low + below_second * below_second)
    weight_second = -(sine_first * magnitude) * (lifted_low / radius_second) / radius_second
    weight_first = (cosine_first * magnitude - lifted_top * weight_second) / radius_first
    return (weight_first, weight_second)


def final_weights(gathered):
    total = jnp.sum(gathered, axis=0, keepdims=True)
    lane = iota((1, 128), 1)
    rr, rd, dd, re, de, ee = [
        jnp.sum(jnp.where(lane == index, total, 0.0), axis=1, keepdims=True) for index in range(6)
    ]
    square = rr + EPSILON
    magnitude = jnp.sqrt(square)
    h11 = (rr + rd) / square
    gap = -(rd - EPSILON) / square
    h21_square = jnp.maximum((dd + 2.0 * gap * rd + gap * gap * rr) / square, 0.0) + EPSILON
    h21 = jnp.sqrt(h21_square)
    unit = 1.0 / (magnitude * h21)
    h12 = (gap * rr + (1.0 + gap) * rd + re) * unit / magnitude
    h22 = (
        gap * (gap * rr + rd) + (1.0 + gap) * (gap * rd + dd) + (gap * re + de)
    ) * unit * unit
    c_r = gap * unit - h12 / magnitude - h22 * gap * unit
    c_d = (1.0 + gap - h22) * unit
    c_e = unit
    h32_square = (
        c_r * c_r * rr + c_d * c_d * dd + c_e * c_e * ee
        + 2.0 * (c_r * c_d * rd + c_r * c_e * re + c_d * c_e * de)
    )
    h32 = jnp.sqrt(jnp.maximum(h32_square, 0.0) + EPSILON)
    y1, y2 = least_squares(magnitude, h11, h21, h12, h22, h32)
    return y1 / magnitude + y2 * gap * unit, y2 * unit


def last_step(
    table, gathered_ref, pairs, state, z1,
    out_hbm,
    out, sem_out,
):
    out[...] = jnp.zeros(out.shape, F32)
    weight0, weight1 = final_weights(gathered_ref[...])

    def body(i, carry):
        for k in range(CHUNK):
            j = i * CHUNK + k
            new = pairs[j, 0:128, :] + weight0 * state[j, 576:704, :] + weight1 * z1[j]
            slots = [jnp.where(table[2 * j + r] >= 0, table[2 * j + r], SLOTS) for r in range(2)]
            for c in range(2):
                for r, x in enumerate(split_up(new[64 * c : 64 * c + 64])):
                    for q in range(4):
                        out[slots[r], pl.ds(c + 2 * q, 8, stride=8), :] = x[8 * q : 8 * q + 8]
        return carry

    lax.fori_loop(0, CHUNKS, body, 0)
    copy = pltpu.make_async_copy(out.at[pl.ds(0, SLOTS)], out_hbm, sem_out)
    copy.start()
    copy.wait()


def call(kernel, outs, specs, scratch=(), out_specs=None, mebibytes=4):
    return pl.pallas_call(
        kernel,
        out_shape=outs,
        in_specs=specs,
        out_specs=out_specs if out_specs is not None else jax.tree.map(lambda _: vmem(), outs),
        scratch_shapes=list(scratch),
        compiler_params=params(mebibytes),
    )


def hbm():
    return pl.BlockSpec(memory_space=pl.ANY)


def square(rows=128):
    return pltpu.VMEM((rows, 128), F32)


def buffer(*shape, dtype=F32):
    return pltpu.VMEM(shape, dtype)


def sems(*shape):
    return pltpu.SemaphoreType.DMA(shape)


def vector_view(x):
    return x.reshape(64, 2, 32, 128).transpose(0, 2, 1, 3).reshape(64, 64, 128)


def field_view(x):
    return x.reshape(8, 8, 32, 128).transpose(0, 2, 1, 3).reshape(8, 256, 128)


def exchange(x):
    return lax.all_to_all(x, "dev", split_axis=0, concat_axis=0, tiled=True)


def boundaries(arrival, received, count):
    side = struct(8, 8 * count, 128)
    return call(boundary, (side, side), [smem(), vmem()])(arrival, received)


def from_groups(south, north):
    size = lax.axis_size("grp")
    ahead = [(i, (i + 1) % size) for i in range(size)]
    return lax.ppermute(north, "grp", ahead), lax.ppermute(south, "grp", [(j, i) for i, j in ahead])


def shards(velocity, forcing, mass, coriolis, viscosity, lines, tile_source_slot, ocean_tile):
    u, b = vector_view(velocity), vector_view(forcing)
    a, f, z, p = [field_view(x) for x in (mass, coriolis, viscosity, lines)]

    tiles, vectors = resident(8, 256, 128), resident(64, 64, 128)
    message, table, codes, arrival, pairs, p, b, a, f = call(
        first_edges,
        (
            struct(PAIRS * 32, 128), struct(TABLE, dtype=jnp.int32), struct(CODES, dtype=jnp.int32),
            struct(TILES + 8, dtype=jnp.int32), resident(PAIRS, 192, 128), tiles, vectors, tiles, tiles,
        ),
        [smem(), smem()] + [hbm()] * 6,
        [
            buffer(64, 64, 128), buffer(8, 256, 128), square(), square(), square(),
            pltpu.SMEM((PAIRS + 8,), jnp.int32), pltpu.SMEM((PAIRS,), jnp.int32), sems(6),
        ],
        (vmem(), smem(), smem(), smem()) + (vmem(),) * 5,
        8,
    )(*[kept(x) for x in (ocean_tile, tile_source_slot, u, z, p, b, a, f)])

    received = exchange(message.reshape(PAIRS, 32, 128))
    south, north = boundaries(arrival, received, 2)
    south, north, p = lax.optimization_barrier((south, north, p))
    weight, fields = call(
        prepare, (resident(PAIRS, 128, 256, dtype=BF16), resident(PAIRS, 128, 128)), [smem()] + [vmem()] * 3,
        [buffer(MIDDLE, 128, 128)],
    )(table, held(p), held(a), held(f))
    halo, face = call(
        first_return, (struct(PAIRS, 16, 128), struct(TILES, 8, 128)), [smem()] + [vmem()] * 3
    )(arrival, received, *from_groups(south, north))
    halo, weight, fields = lax.optimization_barrier((halo, weight, fields))
    halo = exchange(halo).reshape(PAIRS * 16, 128)

    state, message = call(
        first_step,
        (resident(PAIRS, STATE, 128), struct(PAIRS * 16, 128)),
        [smem()] * 2 + [vmem()] * 5,
        [square()] * 4,
        mebibytes=8,
    )(table, codes, halo, held(pairs), held(b), held(fields), held(weight))
    received = exchange(message.reshape(PAIRS, 16, 128))
    south, north = boundaries(arrival, received, 1)
    south, north, state = lax.optimization_barrier((south, north, state))
    whole = resident(PAIRS, 128, 128)
    local, edges = call(
        local_part, (whole, struct(PAIRS * 8, 128)), [vmem()], [square(), square()]
    )(held(state))
    halo = call(second_return, struct(PAIRS, 16, 128), [smem()] + [vmem()] * 5)(
        arrival, received, *from_groups(south, north), edges.reshape(PAIRS, 8, 128), face
    )
    halo, local = lax.optimization_barrier((halo, local))
    earlier = exchange(halo)
    halo = earlier.reshape(PAIRS * 16, 128)

    z1, d, p, message = call(
        second_step,
        (whole, whole, whole, struct(PAIRS * 32, 128)),
        [smem()] + [vmem()] * 4,
        [square()] * 5,
        mebibytes=8,
    )(codes, halo, held(state), held(local), held(weight))
    received = exchange(message.reshape(PAIRS, 32, 128))
    south, north = boundaries(arrival, received, 1)
    south, north, d = lax.optimization_barrier((south, north, d))
    sums = call(owner_sums, struct(6, 8, 128), [vmem()] * 3)(held(state), held(d), held(p))
    partial = call(edge_sums, struct(128, 128), [smem()] + [vmem()] * 6)(
        arrival, received, *from_groups(south, north), earlier, face, sums
    )
    gathered = lax.all_to_all(partial, ("grp", "dev"), split_axis=0, concat_axis=0, tiled=True)

    out = call(
        last_step, struct(SLOTS, 64, 128), [smem()] + [vmem()] * 4,
        [buffer(SLOTS + 1, 64, 128), pltpu.SemaphoreType.DMA],
        hbm(),
        8,
    )(table, gathered, held(pairs), held(state), held(z1))
    return out.reshape(64, 32, 2, 128).transpose(0, 2, 1, 3).reshape(64, 2, 4096)


def solution(mesh):
    return jax.shard_map(
        shards,
        mesh=mesh,
        in_specs=(
            P(("grp", "dev"), None, None),
            P(("grp", "dev"), None, None),
            P(("grp", "dev"), None),
            P(("grp", "dev"), None),
            P(("grp", "dev"), None),
            P(("grp", "dev"), None),
            P(("grp", "dev")),
            P(("grp", "dev")),
        ),
        out_specs=P(("grp", "dev"), None, None),
        check_vma=False,
    )
```
